128 devices in a mesh: dp: 16 (over y_lo, z, core), cent: 8 (over x, y_hi).
Axes of the slice: x: 4, y: 4 (y_hi: 2, y_lo: 2; y = y_hi * 2 + y_lo), z: 4, core: 2. Of those that a mesh axis runs over, the one named last changes fastest.
Arguments:
- points: bfloat16 [131072, 1024], P('dp'), may hold values from -6 to 6
- labels: int32 [131072], P('dp'), may hold values from 0 to 32767
- centroids: bfloat16 [32768, 1024], P(('dp', 'cent')), may hold values from -6 to 6
Outputs:
- new_centroids: bfloat16 [32768, 1024], P('dp')
- rotation: float32 [1024, 1024], replicated
The draws below stay inside these ranges and needn't reach their ends.
Inputs may be any that keep to these rules, and one draw needn't show every extreme that they name: The 8192 vectors of one index of dp name at most 8192 of the 32768 centroids; the sums and counts of the centroids that its labels don't name are zero and need not be sent, so a program may send only the rows that its labels name, sized by its own labels.
All inputs are finite; a program needn't handle non-finite values.
Results may differ from the reference program's by a relative error of at most 0.001.
Values may be sent and summed in bfloat16 or wider, within the bound.
A program may use at most 128 MiB of HBM per device.

```python
import jax
import jax.numpy as jnp
from jax import lax

D = 1024
K = 32768
NS_STEPS = 3
POINTS = 131072


def draw_points(key, part):
    key = jax.random.fold_in(key, 11)
    return jnp.clip(jax.random.normal(key, (POINTS, D), jnp.float32), -6.0, 6.0).astype(jnp.bfloat16)


def draw_centroids(key, part):
    key = jax.random.fold_in(key, 23)
    return jnp.clip(jax.random.normal(key, (K, D), jnp.float32), -6.0, 6.0).astype(jnp.bfloat16)


def place_ends(result, stream_key, least, high):
    extent = result.shape
    place = [jax.random.randint(jax.random.fold_in(stream_key, axis), (), 0, extent[axis]) for axis in range(len(extent))]
    result = result.at[tuple(place)].set(least)
    longest = extent.index(max(extent))
    place[longest] = (place[longest] + 1) % extent[longest]
    return result.at[tuple(place)].set(high)


def setup_inputs(seed: int = 0) -> dict:
    keys = jax.random.split(jax.random.key(seed), 4)
    return {
        "points": draw_points(jax.random.fold_in(keys[3], 71), 0),
        "labels": place_ends(jax.random.randint(keys[1], (POINTS,), 0, K), jax.random.fold_in(keys[1], 1), 0, K - 1).astype(jnp.int32),
        "centroids": draw_centroids(jax.random.fold_in(keys[3], 71), 0),
    }


def reference(points, labels, centroids):
    vectors = points.astype(jnp.float32)
    label_sums = jax.ops.segment_sum(vectors, labels, num_segments=K)
    label_counts = jax.ops.segment_sum(jnp.ones(labels.shape, jnp.float32), labels, num_segments=K)
    old_rows = centroids.astype(jnp.float32)
    cross_cov = lax.dot_general(label_sums, old_rows, (((0,), (0,)), ((), ())), precision=lax.Precision.HIGHEST)
    scale_root = jnp.sqrt(jnp.sum(cross_cov * cross_cov) / D + 1e-06)
    polar_iter = cross_cov / (3.0 * scale_root)
    for iteration in range(NS_STEPS):
        inner_prod = jnp.dot(polar_iter, polar_iter.T, precision=lax.Precision.HIGHEST)
        polar_iter = 1.5 * polar_iter - 0.5 * jnp.dot(inner_prod, polar_iter, precision=lax.Precision.HIGHEST)
    rotated_sums = jnp.dot(label_sums, polar_iter, precision=lax.Precision.HIGHEST)
    new_centroids = ((rotated_sums + old_rows) / (label_counts[:, None] + 1.0)).astype(jnp.bfloat16)
    return (new_centroids, polar_iter)
```

```python
import functools

import jax
import jax.numpy as jnp
from jax import lax
from jax.experimental import pallas as pl
from jax.experimental.pallas import tpu as pltpu
from jax.sharding import PartitionSpec as P

MESH = pl.DeviceIdType.MESH
F32 = jnp.float32
BF16 = jnp.bfloat16

NS_STEPS = 3
epsilon = 1e-06

CHUNK = 512
KEEP = 128
CAP = 112
SLOT = 128
WAYS = 4
LANES = ((0, 384), (384, 384), (768, 256))


def dot(a, b, dims=((1,), (0,))):
    return lax.dot_general(a, b, (dims, ((), ())), preferred_element_type=F32)


def split(x):
    hi = x.astype(BF16)
    return hi, (x - hi.astype(F32)).astype(BF16)


def iota(shape, axis):
    return lax.broadcasted_iota(jnp.int32, shape, axis)


def pack_kernel(data_ways, panel_ways, block_rows, lab_ref, pts_ref, kept_ref, meta_ref, bad_ref, tri, carry):
    step = pl.program_id(0)
    panel = lax.axis_index("cent")

    @pl.when(step == 0)
    def _():
        tri[...] = jnp.where(
            iota((CHUNK, CHUNK), 0) <= iota((CHUNK, CHUNK), 1), 1.0, 0.0
        ).astype(BF16)
        carry[...] = jnp.zeros_like(carry)
        bad_ref[...] = jnp.zeros_like(bad_ref)

    lab = lab_ref[0]
    block = lab // block_rows
    inside = block % panel_ways == panel
    dest = block // panel_ways
    hit = jnp.where(
        jnp.logical_and(iota((data_ways, CHUNK), 0) == dest, inside), 1.0, 0.0
    )
    count = dot(hit.astype(BF16), tri[...])
    rank = jnp.sum(hit * jnp.sum(count, axis=0, keepdims=True), axis=0, keepdims=True)
    place = jnp.sum(hit * (count + carry[:, 0:1]), axis=0, keepdims=True)
    last = count[:, CHUNK - 1 : CHUNK]
    carry[...] = carry[...] + last
    over = jnp.logical_or(
        jnp.max(carry[...], axis=0, keepdims=True) > CAP,
        jnp.sum(last, axis=0, keepdims=True) > KEEP,
    )
    bad_ref[...] = jnp.where(
        jnp.broadcast_to(over, bad_ref.shape), jnp.inf, bad_ref[...]
    )
    pick = jnp.where(
        iota((KEEP, CHUNK), 0) + 1 == rank.astype(jnp.int32), 1.0, 0.0
    ).astype(BF16)
    kept_ref[...] = dot(pick, pts_ref[...]).astype(BF16)
    row = iota((16, CHUNK), 0)
    slot = (lab % block_rows + 1).astype(F32)
    meta = jnp.where(
        row == 0,
        dest.astype(F32),
        jnp.where(row == 1, jnp.minimum(place, 255.0), jnp.where(row == 2, slot, 0.0)),
    )
    meta_ref[...] = dot(meta.astype(BF16), pick, ((1,), (1,))).astype(BF16)


def pack(labels, points, data_ways, panel_ways, block_rows):
    rows, features = points.shape
    steps = rows // CHUNK
    return pl.pallas_call(
        functools.partial(pack_kernel, data_ways, panel_ways, block_rows),
        grid=(steps,),
        in_specs=[
            pl.BlockSpec((1, 1, CHUNK), lambda i: (i, 0, 0)),
            pl.BlockSpec((CHUNK, features), lambda i: (i, 0)),
        ],
        out_specs=[
            pl.BlockSpec((KEEP, features), lambda i: (i, 0)),
            pl.BlockSpec((16, KEEP), lambda i: (0, i)),
            pl.BlockSpec((8, 128), lambda i: (0, 0)),
        ],
        out_shape=[
            jax.ShapeDtypeStruct((steps * KEEP, features), BF16),
            jax.ShapeDtypeStruct((16, steps * KEEP), BF16),
            jax.ShapeDtypeStruct((8, 128), F32),
        ],
        scratch_shapes=[pltpu.VMEM((CHUNK, CHUNK), BF16), pltpu.VMEM((data_ways, 128), F32)],
        compiler_params=pltpu.CompilerParams(vmem_limit_bytes=32 << 20),
        name="pack",
    )(labels.reshape(steps, 1, CHUNK), points)


def exchange_kernel(
    data_ways, kept_ref, meta_ref, bad_ref, cents_ref, sums_ref, count_ref, cov_ref,
    out, got, out_id, got_id, send, recv, send_id, recv_id,
):
    me = lax.axis_index("dp")
    barrier = pltpu.get_barrier_semaphore()
    for k in range(1, data_ways):
        pl.semaphore_signal(
            barrier, inc=1, device_id={"dp": (me + k) % data_ways}, device_id_type=MESH
        )
    pl.semaphore_wait(barrier, data_ways - 1)

    meta = meta_ref[...]
    whole = meta.astype(F32).astype(jnp.int32)
    dest, place = whole[0:1, :], whole[1:2, :]
    total = meta.shape[1]
    copies = []
    for k in list(range(1, data_ways)) + [0]:
        to = (me + k) % data_ways
        wanted = jnp.where(dest == to, place, 0)
        pick = jnp.where(iota((SLOT, total), 0) + 1 == wanted, 1.0, 0.0).astype(BF16)
        out[k] = dot(pick, kept_ref[...]).astype(BF16)
        out_id[k] = dot(meta, pick, ((1,), (1,))).astype(BF16)
        if k:
            for src, dst, s, r in (
                (out.at[k, pl.ds(0, CAP)], got.at[k, pl.ds(0, CAP)], send, recv),
                (out_id.at[k], got_id.at[k], send_id, recv_id),
            ):
                copy = pltpu.make_async_remote_copy(
                    src_ref=src, dst_ref=dst, send_sem=s.at[k], recv_sem=r.at[k],
                    device_id={"dp": to}, device_id_type=MESH,
                )
                copy.start()
                copies.append((k, copy))
    rows, features = sums_ref.shape
    got[:, CAP:SLOT, :] = jnp.zeros((data_ways, SLOT - CAP, features), BF16)

    ones = jnp.ones((SLOT, 128), BF16)
    for k in range(data_ways):
        for at, copy in copies:
            if at == k:
                copy.wait_recv()
        ids = (got_id if k else out_id)[k].astype(F32).astype(jnp.int32)
        pick = jnp.where(iota((rows, SLOT), 0) + 1 == ids[2:3, :], 1.0, 0.0).astype(BF16)
        vectors = (got if k else out)[k]
        if k:
            sums_ref[...] += dot(pick, vectors)
            count_ref[...] += dot(pick, ones)
        else:
            sums_ref[...] = dot(pick, vectors)
            count_ref[...] = dot(pick, ones)
    hi, lo = split(sums_ref[...])
    cents = cents_ref[...]
    first = ((0,), (0,))
    cov_ref[...] = dot(hi, cents, first) + dot(lo, cents, first)
    cov_ref[0:8, 0:128] = cov_ref[0:8, 0:128] + bad_ref[...]
    for _, copy in copies:
        copy.wait_send()


def vmem(n):
    return [pl.BlockSpec(memory_space=pltpu.VMEM)] * n


def exchange(kept, meta, bad, cents, data_ways):
    rows, features = cents.shape
    return pl.pallas_call(
        functools.partial(exchange_kernel, data_ways),
        in_specs=vmem(4),
        out_specs=vmem(3),
        out_shape=[
            jax.ShapeDtypeStruct((rows, features), F32),
            jax.ShapeDtypeStruct((rows, 128), F32),
            jax.ShapeDtypeStruct((features, features), F32),
        ],
        scratch_shapes=[
            pltpu.VMEM((data_ways, SLOT, features), BF16),
            pltpu.VMEM((data_ways, SLOT, features), BF16),
            pltpu.VMEM((data_ways, 16, SLOT), BF16),
            pltpu.VMEM((data_ways, 16, SLOT), BF16),
        ]
        + [pltpu.SemaphoreType.DMA((data_ways,))] * 4,
        compiler_params=pltpu.CompilerParams(
            collective_id=0, has_side_effects=True, vmem_limit_bytes=48 << 20
        ),
        name="exchange",
    )(kept, meta, bad, cents)


def place():
    dp, cent = lax.axis_index("dp"), lax.axis_index("cent")
    x, y, z = cent // 2, cent % 2 * 2 + dp // 8, dp // 2 % 4
    return (x, y, z), dp % 2


def device(xyz, core):
    x, y, z = xyz
    return {"dp": (y % 2 * 4 + z) * 2 + core, "cent": x * 2 + y // 2}


def moved(xyz, axis, by):
    return tuple((c + by) % WAYS if a == axis else c for a, c in enumerate(xyz))


def reduce_kernel(part_ref, all_ref, half, got1, got2, got3, acc, send, recv):
    xyz, core = place()
    features = part_ref.shape[1]
    mine = features // 2
    barrier = pltpu.get_barrier_semaphore()
    other = device(xyz, 1 - core)
    partners = [other] + [
        device(moved(xyz, axis, by), core) for axis in range(3) for by in range(1, WAYS)
    ]
    for partner in partners:
        pl.semaphore_signal(barrier, inc=1, device_id=partner, device_id_type=MESH)
    pl.semaphore_wait(barrier, len(partners))

    used = [0]
    started = []

    def copy(src, dst, to):
        n = used[0]
        used[0] += 1
        made = pltpu.make_async_remote_copy(
            src_ref=src, dst_ref=dst, send_sem=send.at[n], recv_sem=recv.at[n],
            device_id=to, device_id_type=MESH,
        )
        made.start()
        started.append(made)
        return made

    here = pl.multiple_of(core * mine, mine)
    there = pl.multiple_of((1 - core) * mine, mine)
    swap = copy(part_ref.at[pl.ds(there, mine)], half, other)
    swap.wait_recv()
    acc[...] = part_ref[pl.ds(here, mine), :] + half[...]

    base = [0, 0, 0]
    size = mine
    for stage, got in enumerate((got1, got2, got3)):
        size //= WAYS
        waits = []
        for part, (lane, width) in enumerate(LANES):
            axis = (part + stage) % 3
            row = []
            for by in range(1, WAYS):
                to = moved(xyz, axis, by)
                start = pl.multiple_of(base[part] + to[axis] * size, size)
                row.append(
                    copy(
                        acc.at[pl.ds(start, size), pl.ds(lane, width)],
                        got.at[by - 1, :, pl.ds(lane, width)],
                        device(to, core),
                    )
                )
            waits.append(row)
        for part, (lane, width) in enumerate(LANES):
            axis = (part + stage) % 3
            base[part] = pl.multiple_of(base[part] + xyz[axis] * size, size)
            for made in waits[part]:
                made.wait_recv()
            own = (pl.ds(base[part], size), pl.ds(lane, width))
            total = acc[own]
            for by in range(1, WAYS):
                total = total + got[by - 1, :, lane : lane + width]
            acc[own] = total

    for part, (lane, width) in enumerate(LANES):
        all_ref[pl.ds(here + base[part], size), pl.ds(lane, width)] = acc[
            pl.ds(base[part], size), pl.ds(lane, width)
        ]
    for stage in (2, 1, 0):
        waits = []
        for part, (lane, width) in enumerate(LANES):
            axis = (part + stage) % 3
            span = all_ref.at[
                pl.ds(pl.multiple_of(here + base[part], size), size), pl.ds(lane, width)
            ]
            for by in range(1, WAYS):
                waits.append(copy(span, span, device(moved(xyz, axis, by), core)))
            base[part] = base[part] - xyz[axis] * size
        for made in waits:
            made.wait_recv()
        size *= WAYS
    span = all_ref.at[pl.ds(here, mine)]
    copy(span, span, other).wait_recv()
    for made in started:
        made.wait_send()


def reduce_all(part):
    features = part.shape[0]
    mine = features // 2
    sizes = [mine // WAYS**n for n in (1, 2, 3)]
    copies = 2 + 2 * 3 * 3 * (WAYS - 1)
    return pl.pallas_call(
        reduce_kernel,
        in_specs=vmem(1),
        out_specs=pl.BlockSpec(memory_space=pltpu.VMEM),
        out_shape=jax.ShapeDtypeStruct(part.shape, F32),
        scratch_shapes=[pltpu.VMEM((mine, features), F32)]
        + [pltpu.VMEM((WAYS - 1, size, features), F32) for size in sizes]
        + [pltpu.VMEM((mine, features), F32)]
        + [pltpu.SemaphoreType.DMA((copies,))] * 2,
        compiler_params=pltpu.CompilerParams(
            collective_id=1, has_side_effects=True, vmem_limit_bytes=48 << 20
        ),
        name="reduce",
    )(part)


def polar_kernel(cov_ref, rot_ref, hi, lo):
    features = cov_ref.shape[0]
    tile = 256
    cov = cov_ref[...]
    square = jnp.sum(jnp.sum(cov * cov, axis=0, keepdims=True), axis=1, keepdims=True)
    rot_ref[...] = cov / (3.0 * jnp.sqrt(square / features + epsilon))
    both = ((1,), (1,))
    for iteration in range(NS_STEPS):

        @pl.loop(0, features // tile)
        def _(t):
            rows = pl.ds(pl.multiple_of(t * tile, tile), tile)
            hi[rows, :], lo[rows, :] = split(rot_ref[rows, :])

        @pl.loop(0, features // tile)
        def _(t):
            rows = pl.ds(pl.multiple_of(t * tile, tile), tile)
            inner = dot(hi[rows, :], hi[...], both) + (
                dot(hi[rows, :], lo[...], both) + dot(lo[rows, :], hi[...], both)
            )
            top, low = split(inner)
            turn = dot(top, hi[...]) + (dot(top, lo[...]) + dot(low, hi[...]))
            rot_ref[rows, :] = 1.5 * rot_ref[rows, :] - 0.5 * turn


def polar(cov):
    return pl.pallas_call(
        polar_kernel,
        in_specs=vmem(1),
        out_specs=pl.BlockSpec(memory_space=pltpu.VMEM),
        out_shape=jax.ShapeDtypeStruct(cov.shape, F32),
        scratch_shapes=[pltpu.VMEM(cov.shape, BF16)] * 2,
        compiler_params=pltpu.CompilerParams(vmem_limit_bytes=48 << 20),
        name="polar",
    )(cov)


def gather_kernel(panel_ways, sums_ref, count_ref, cents_ref, rot_ref, new_ref, fresh, keep, send, recv):
    me = lax.axis_index("cent")
    barrier = pltpu.get_barrier_semaphore()
    for k in range(1, panel_ways):
        pl.semaphore_signal(
            barrier, inc=1, device_id={"cent": (me + k) % panel_ways}, device_id_type=MESH
        )
    pl.semaphore_wait(barrier, panel_ways - 1)
    rows = fresh.shape[0]
    hi, lo = split(sums_ref[...])
    top, low = split(rot_ref[...])
    turned = dot(hi, top) + (dot(hi, low) + dot(lo, top))
    fresh[...] = (
        (turned + cents_ref[...].astype(F32)) / (count_ref[:, 0:1] + 1.0)
    ).astype(BF16)
    own = new_ref.at[pl.ds(pl.multiple_of(me * rows, rows), rows)]
    copies = []
    for k in range(1, panel_ways):
        copy = pltpu.make_async_remote_copy(
            src_ref=fresh, dst_ref=own, send_sem=send.at[k], recv_sem=recv.at[k],
            device_id={"cent": (me + k) % panel_ways}, device_id_type=MESH,
        )
        copy.start()
        copies.append(copy)
    local = pltpu.make_async_copy(fresh, own, keep)
    local.start()
    for copy in copies:
        copy.wait()
    local.wait()


def gather(sums, count, cents, rot, panel_ways):
    rows, features = cents.shape
    return pl.pallas_call(
        functools.partial(gather_kernel, panel_ways),
        in_specs=vmem(4),
        out_specs=pl.BlockSpec(memory_space=pl.ANY),
        out_shape=jax.ShapeDtypeStruct((panel_ways * rows, features), BF16),
        scratch_shapes=[pltpu.VMEM((rows, features), BF16), pltpu.SemaphoreType.DMA]
        + [pltpu.SemaphoreType.DMA((panel_ways,))] * 2,
        compiler_params=pltpu.CompilerParams(
            collective_id=2, has_side_effects=True, vmem_limit_bytes=48 << 20
        ),
        name="gather",
    )(sums, count, cents, rot)


def dense(points, labels, centroids):
    data_ways = lax.axis_size("dp")
    panel_ways = lax.axis_size("cent")
    block_rows = centroids.shape[0]
    features = points.shape[1]
    column = lax.axis_index("cent")
    owner_block = labels // block_rows
    inside = owner_block % panel_ways == column
    slot_index = jnp.where(
        inside, owner_block // panel_ways * block_rows + labels % block_rows, data_ways * block_rows
    )
    vectors = points.astype(F32)
    local_sums = jax.ops.segment_sum(vectors, slot_index, num_segments=data_ways * block_rows)
    local_counts = jax.ops.segment_sum(
        jnp.ones(labels.shape, F32), slot_index, num_segments=data_ways * block_rows
    )
    label_sums, label_counts = (
        lax.psum_scatter(local_sums, "dp", scatter_dimension=0, tiled=True),
        lax.psum_scatter(local_counts, "dp", scatter_dimension=0, tiled=True),
    )
    old_rows = centroids.astype(F32)
    cross_cov = lax.psum(
        lax.dot_general(
            label_sums, old_rows, (((0,), (0,)), ((), ())), precision=lax.Precision.HIGHEST
        ),
        ("dp", "cent"),
    )
    scale_root = jnp.sqrt(jnp.sum(cross_cov * cross_cov) / features + epsilon)
    rotation = cross_cov / (3.0 * scale_root)
    for iteration in range(NS_STEPS):
        inner_prod = jnp.dot(rotation, rotation.T, precision=lax.Precision.HIGHEST)
        rotation = 1.5 * rotation - 0.5 * jnp.dot(
            inner_prod, rotation, precision=lax.Precision.HIGHEST
        )
    rotated_sums = jnp.dot(label_sums, rotation, precision=lax.Precision.HIGHEST)
    fresh_rows = ((rotated_sums + old_rows) / (label_counts[:, None] + 1.0)).astype(BF16)
    new_centroids = lax.all_gather(fresh_rows, "cent", axis=0, tiled=True)
    return (new_centroids, rotation)


def local(points, labels, centroids):
    data_ways = lax.axis_size("dp")
    panel_ways = lax.axis_size("cent")
    kept, meta, bad = pack(labels, points, data_ways, panel_ways, centroids.shape[0])
    sums, count, part = exchange(kept, meta, bad, centroids, data_ways)
    cov = reduce_all(part)

    def sparse():
        rotation = polar(cov)
        return gather(sums, count, centroids, rotation, panel_ways), rotation

    return lax.cond(
        jnp.isfinite(cov[0, 0]), sparse, lambda: dense(points, labels, centroids)
    )


def solution(mesh):
    return jax.shard_map(
        local,
        mesh=mesh,
        in_specs=(P("dp", None), P("dp"), P(("dp", "cent"), None)),
        out_specs=(P("dp", None), P()),
        check_vma=False,
    )
```

```python
import functools

import jax
import jax.numpy as jnp
from jax import lax
from jax.experimental import pallas as pl
from jax.experimental.pallas import tpu as pltpu
from jax.sharding import PartitionSpec as P

MESH = pl.DeviceIdType.MESH
F32 = jnp.float32
BF16 = jnp.bfloat16

NS_STEPS = 3
epsilon = 1e-06

CHUNK = 512
KEEP = 128
CAP = 112
SLOT = 128
WAYS = 4
LANES = ((0, 384), (384, 384), (768, 256))


def dot(a, b, dims=((1,), (0,))):
    return lax.dot_general(a, b, (dims, ((), ())), preferred_element_type=F32)


def split(x):
    hi = x.astype(BF16)
    return hi, (x - hi.astype(F32)).astype(BF16)


def iota(shape, axis):
    return lax.broadcasted_iota(jnp.int32, shape, axis)


def exchange_kernel(
    block_rows, lab_ref, pts_ref, cents_ref, sums_ref, count_ref, cov_ref,
    pts, tri, hits, rank, meta, kept, metas, out, got, up, down, out_id, got_id, load, send, recv,
):
    dp, panel = lax.axis_index("dp"), lax.axis_index("cent")
    data_ways, panel_ways = lax.axis_size("dp"), lax.axis_size("cent")
    steps = lab_ref.shape[0]
    yl, z, core = dp // 8, dp // 2 % 4, dp % 2

    def at(dy, dz, dc):
        return {"dp": ((yl + dy) % 2 * 4 + (z + dz) % 4) * 2 + (core + dc) % 2}

    loads = []
    for step in range(steps):
        loads.append(
            pltpu.make_async_copy(
                pts_ref.at[pl.ds(step * CHUNK, CHUNK)], pts.at[step], load.at[step]
            )
        )
        loads[-1].start()
    barrier = pltpu.get_barrier_semaphore()
    for dy in range(2):
        for dz in range(4):
            for dc in range(2):
                if dy or dz or dc:
                    pl.semaphore_signal(
                        barrier, inc=1, device_id=at(dy, dz, dc), device_id_type=MESH
                    )

    tri[...] = jnp.where(
        iota((CHUNK, CHUNK), 0) <= iota((CHUNK, CHUNK), 1), 1.0, 0.0
    ).astype(BF16)
    for step in range(steps):
        block = lab_ref[step] // block_rows
        dest = block // panel_ways
        hits[step * data_ways : (step + 1) * data_ways, :] = jnp.where(
            jnp.logical_and(
                iota((data_ways, CHUNK), 0) == dest, block % panel_ways == panel
            ),
            1.0,
            0.0,
        )
    counts = dot(hits[...].astype(BF16), tri[...])
    carry = jnp.zeros((data_ways, 1), F32)
    most = jnp.zeros((1, 1), F32)
    row = iota((16, CHUNK), 0)
    for step in range(steps):
        hit = hits[step * data_ways : (step + 1) * data_ways, :]
        count = counts[step * data_ways : (step + 1) * data_ways, :]
        order = jnp.sum(
            hit * jnp.sum(count, axis=0, keepdims=True), axis=0, keepdims=True
        )
        rank[step] = order.astype(jnp.int32)
        spot = jnp.sum(hit * (count + carry), axis=0, keepdims=True)
        last = count[:, CHUNK - 1 : CHUNK]
        carry = carry + last
        most = jnp.maximum(most, jnp.sum(last, axis=0, keepdims=True))
        lab = lab_ref[step]
        dest = (lab // block_rows // panel_ways).astype(F32)
        slot = (lab % block_rows + 1).astype(F32)
        meta[step] = jnp.where(
            row == 0,
            dest,
            jnp.where(row == 1, jnp.minimum(spot, 255.0), jnp.where(row == 2, slot, 0.0)),
        ).astype(BF16)
    over = jnp.logical_or(most > KEEP, jnp.max(carry, axis=0, keepdims=True) > CAP)
    bad = jnp.where(over, jnp.inf, 0.0)

    for step in range(steps):
        pick = jnp.where(iota((KEEP, CHUNK), 0) + 1 == rank[step], 1.0, 0.0).astype(BF16)
        metas[:, step * KEEP : (step + 1) * KEEP] = dot(
            meta[step], pick, ((1,), (1,))
        ).astype(BF16)
        loads[step].wait()
        kept[step * KEEP : (step + 1) * KEEP, :] = dot(pick, pts[step]).astype(BF16)

    pl.semaphore_wait(barrier, data_ways - 1)
    used = [0]
    started = []

    def copy(src, dst, to):
        n = used[0]
        used[0] += 1
        made = pltpu.make_async_remote_copy(
            src_ref=src, dst_ref=dst, send_sem=send.at[n], recv_sem=recv.at[n],
            device_id=to, device_id_type=MESH,
        )
        made.start()
        started.append(made)
        return made

    def share(n):
        return CAP // 2 // 16 * 16 + (16 if n in (0, 3) else 0)

    places = metas[...]
    whole = places.astype(F32).astype(jnp.int32)
    dests, spots = whole[0:1, :], whole[1:2, :]
    total = places.shape[1]
    arrive = {}
    relays = []
    order = (
        [(1, 2, 0), (1, 2, 1), (0, 2, 0), (0, 2, 1)]
        + [(1, dz, dc) for dz in (1, 3) for dc in range(2)]
        + [(1, 0, 0), (1, 0, 1)]
        + [(0, dz, dc) for dz in (1, 3) for dc in range(2)]
        + [(0, 0, 1), (0, 0, 0)]
    )
    for dy, dz, dc in order:
        k = (dy * 4 + dz) * 2 + dc
        to = at(dy, dz, dc)
        wanted = jnp.where(dests == to["dp"], spots, 0)
        pick = jnp.where(iota((SLOT, total), 0) + 1 == wanted, 1.0, 0.0).astype(BF16)
        out[k] = dot(pick, kept[...]).astype(BF16)
        out_id[k] = dot(places, pick, ((1,), (1,))).astype(BF16)
        if k == 0:
            continue
        arrive[k] = [copy(out_id.at[k], got_id.at[k], to)]
        if dz == 2:
            n = dy * 2 + dc
            cut = share(n)
            for hop, buf, lo, rows in ((1, up, 0, cut), (3, down, cut, CAP - cut)):
                leg = copy(
                    out.at[k, pl.ds(lo, rows)], buf.at[n, pl.ds(0, rows)], at(0, hop, 0)
                )
                relays.append((leg, k, buf.at[n, pl.ds(0, rows)], lo, rows, at(dy, hop, dc)))
        else:
            arrive[k].append(copy(out.at[k, pl.ds(0, CAP)], got.at[k, pl.ds(0, CAP)], to))
    for leg, k, held, lo, rows, to in relays:
        leg.wait_recv()
        arrive[k].append(copy(held, got.at[k, pl.ds(lo, rows)], to))

    rows, features = sums_ref.shape
    got[:, CAP:SLOT, :] = jnp.zeros((data_ways, SLOT - CAP, features), BF16)
    ones = jnp.ones((SLOT, 128), BF16)
    for dy, dz, dc in order[::-1]:
        k = (dy * 4 + dz) * 2 + dc
        for made in arrive.get(k, ()):
            made.wait_recv()
        ids = (got_id if k else out_id)[k].astype(F32).astype(jnp.int32)
        pick = jnp.where(iota((rows, SLOT), 0) + 1 == ids[2:3, :], 1.0, 0.0).astype(BF16)
        vectors = (got if k else out)[k]
        if k:
            sums_ref[...] += dot(pick, vectors)
            count_ref[...] += dot(pick, ones)
        else:
            sums_ref[...] = dot(pick, vectors)
            count_ref[...] = dot(pick, ones)
    hi, lo = split(sums_ref[...])
    cents = cents_ref[...]
    first = ((0,), (0,))
    cov_ref[...] = dot(hi, cents, first) + dot(lo, cents, first)
    cov_ref[0:8, 0:128] = cov_ref[0:8, 0:128] + bad
    for made in started:
        made.wait_send()


def vmem(n):
    return [pl.BlockSpec(memory_space=pltpu.VMEM)] * n


def exchange(labels, points, cents):
    data_ways = lax.axis_size("dp")
    rows, features = cents.shape
    steps = points.shape[0] // CHUNK
    copies = 2 * data_ways + 12
    return pl.pallas_call(
        functools.partial(exchange_kernel, rows),
        in_specs=vmem(1) + [pl.BlockSpec(memory_space=pl.ANY)] + vmem(1),
        out_specs=vmem(3),
        out_shape=[
            jax.ShapeDtypeStruct((rows, features), F32),
            jax.ShapeDtypeStruct((rows, 128), F32),
            jax.ShapeDtypeStruct((features, features), F32),
        ],
        scratch_shapes=[
            pltpu.VMEM((steps, CHUNK, features), BF16),
            pltpu.VMEM((CHUNK, CHUNK), BF16),
            pltpu.VMEM((steps * data_ways, CHUNK), F32),
            pltpu.VMEM((steps, 1, CHUNK), jnp.int32),
            pltpu.VMEM((steps, 16, CHUNK), BF16),
            pltpu.VMEM((steps * KEEP, features), BF16),
            pltpu.VMEM((16, steps * KEEP), BF16),
            pltpu.VMEM((data_ways, SLOT, features), BF16),
            pltpu.VMEM((data_ways, SLOT, features), BF16),
            pltpu.VMEM((4, 64, features), BF16),
            pltpu.VMEM((4, 64, features), BF16),
            pltpu.VMEM((data_ways, 16, SLOT), BF16),
            pltpu.VMEM((data_ways, 16, SLOT), BF16),
            pltpu.SemaphoreType.DMA((steps,)),
            pltpu.SemaphoreType.DMA((copies,)),
            pltpu.SemaphoreType.DMA((copies,)),
        ],
        compiler_params=pltpu.CompilerParams(
            collective_id=0, has_side_effects=True, vmem_limit_bytes=52 << 20
        ),
        name="exchange",
    )(labels.reshape(steps, 1, CHUNK), points, cents)


def place():
    dp, cent = lax.axis_index("dp"), lax.axis_index("cent")
    x, y, z = cent // 2, cent % 2 * 2 + dp // 8, dp // 2 % 4
    return (x, y, z), dp % 2


def device(xyz, core):
    x, y, z = xyz
    return {"dp": (y % 2 * 4 + z) * 2 + core, "cent": x * 2 + y // 2}


def moved(xyz, axis, by):
    return tuple((c + by) % WAYS if a == axis else c for a, c in enumerate(xyz))


def reduce_kernel(part_ref, all_ref, half, got1, got2, got3, acc, send, recv):
    xyz, core = place()
    features = part_ref.shape[1]
    mine = features // 2
    barrier = pltpu.get_barrier_semaphore()
    other = device(xyz, 1 - core)
    partners = [other] + [
        device(moved(xyz, axis, by), core) for axis in range(3) for by in range(1, WAYS)
    ]
    for partner in partners:
        pl.semaphore_signal(barrier, inc=1, device_id=partner, device_id_type=MESH)
    pl.semaphore_wait(barrier, len(partners))

    used = [0]
    started = []

    def copy(src, dst, to):
        n = used[0]
        used[0] += 1
        made = pltpu.make_async_remote_copy(
            src_ref=src, dst_ref=dst, send_sem=send.at[n], recv_sem=recv.at[n],
            device_id=to, device_id_type=MESH,
        )
        made.start()
        started.append(made)
        return made

    here = pl.multiple_of(core * mine, mine)
    there = pl.multiple_of((1 - core) * mine, mine)
    swap = copy(part_ref.at[pl.ds(there, mine)], half, other)
    swap.wait_recv()
    acc[...] = part_ref[pl.ds(here, mine), :] + half[...]

    base = [0, 0, 0]
    size = mine
    for stage, got in enumerate((got1, got2, got3)):
        size //= WAYS
        waits = []
        for part, (lane, width) in enumerate(LANES):
            axis = (part + stage) % 3
            row = []
            for by in range(1, WAYS):
                to = moved(xyz, axis, by)
                start = pl.multiple_of(base[part] + to[axis] * size, size)
                row.append(
                    copy(
                        acc.at[pl.ds(start, size), pl.ds(lane, width)],
                        got.at[by - 1, :, pl.ds(lane, width)],
                        device(to, core),
                    )
                )
            waits.append(row)
        for part, (lane, width) in enumerate(LANES):
            axis = (part + stage) % 3
            base[part] = pl.multiple_of(base[part] + xyz[axis] * size, size)
            for made in waits[part]:
                made.wait_recv()
            own = (pl.ds(base[part], size), pl.ds(lane, width))
            total = acc[own]
            for by in range(1, WAYS):
                total = total + got[by - 1, :, lane : lane + width]
            acc[own] = total

    for part, (lane, width) in enumerate(LANES):
        all_ref[pl.ds(here + base[part], size), pl.ds(lane, width)] = acc[
            pl.ds(base[part], size), pl.ds(lane, width)
        ]
    for stage in (2, 1, 0):
        waits = []
        for part, (lane, width) in enumerate(LANES):
            axis = (part + stage) % 3
            span = all_ref.at[
                pl.ds(pl.multiple_of(here + base[part], size), size), pl.ds(lane, width)
            ]
            for by in range(1, WAYS):
                waits.append(copy(span, span, device(moved(xyz, axis, by), core)))
            base[part] = base[part] - xyz[axis] * size
        for made in waits:
            made.wait_recv()
        size *= WAYS
    span = all_ref.at[pl.ds(here, mine)]
    copy(span, span, other).wait_recv()
    for made in started:
        made.wait_send()


def reduce_all(part):
    features = part.shape[0]
    mine = features // 2
    sizes = [mine // WAYS**n for n in (1, 2, 3)]
    copies = 2 + 2 * 3 * 3 * (WAYS - 1)
    return pl.pallas_call(
        reduce_kernel,
        in_specs=vmem(1),
        out_specs=pl.BlockSpec(memory_space=pltpu.VMEM),
        out_shape=jax.ShapeDtypeStruct(part.shape, F32),
        scratch_shapes=[pltpu.VMEM((mine, features), F32)]
        + [pltpu.VMEM((WAYS - 1, size, features), F32) for size in sizes]
        + [pltpu.VMEM((mine, features), F32)]
        + [pltpu.SemaphoreType.DMA((copies,))] * 2,
        compiler_params=pltpu.CompilerParams(
            collective_id=1, has_side_effects=True, vmem_limit_bytes=48 << 20
        ),
        name="reduce",
    )(part)


def polar_kernel(cov_ref, rot_ref, hi, lo):
    features = cov_ref.shape[0]
    tile = 256
    cov = cov_ref[...]
    square = jnp.sum(jnp.sum(cov * cov, axis=0, keepdims=True), axis=1, keepdims=True)
    rot_ref[...] = cov / (3.0 * jnp.sqrt(square / features + epsilon))
    both = ((1,), (1,))
    for iteration in range(NS_STEPS):

        @pl.loop(0, features // tile)
        def _(t):
            rows = pl.ds(pl.multiple_of(t * tile, tile), tile)
            hi[rows, :], lo[rows, :] = split(rot_ref[rows, :])

        @pl.loop(0, features // tile)
        def _(t):
            rows = pl.ds(pl.multiple_of(t * tile, tile), tile)
            inner = dot(hi[rows, :], hi[...], both) + (
                dot(hi[rows, :], lo[...], both) + dot(lo[rows, :], hi[...], both)
            )
            top, low = split(inner)
            turn = dot(top, hi[...]) + (dot(top, lo[...]) + dot(low, hi[...]))
            rot_ref[rows, :] = 1.5 * rot_ref[rows, :] - 0.5 * turn


def polar(cov):
    return pl.pallas_call(
        polar_kernel,
        in_specs=vmem(1),
        out_specs=pl.BlockSpec(memory_space=pltpu.VMEM),
        out_shape=jax.ShapeDtypeStruct(cov.shape, F32),
        scratch_shapes=[pltpu.VMEM(cov.shape, BF16)] * 2,
        compiler_params=pltpu.CompilerParams(vmem_limit_bytes=48 << 20),
        name="polar",
    )(cov)


def gather_kernel(sums_ref, count_ref, cents_ref, rot_ref, new_ref, fresh, relay, keep, send, recv):
    xyz, core = place()
    x, y, z = xyz
    right, left = moved(xyz, 0, 1), moved(xyz, 0, WAYS - 1)
    above, below = moved(xyz, 1, 1), moved(xyz, 1, WAYS - 1)
    across = moved(xyz, 1, 2)
    barrier = pltpu.get_barrier_semaphore()
    for partner in (right, left, above, below, across):
        pl.semaphore_signal(
            barrier, inc=1, device_id=device(partner, core), device_id_type=MESH
        )
    rows = fresh.shape[0]
    half = rows // 2
    hi, lo = split(sums_ref[...])
    top, low = split(rot_ref[...])
    turned = dot(hi, top) + (dot(hi, low) + dot(lo, top))
    fresh[...] = (
        (turned + cents_ref[...].astype(F32)) / (count_ref[:, 0:1] + 1.0)
    ).astype(BF16)
    pl.semaphore_wait(barrier, 5)

    used = [0]
    started = []

    def copy(src, dst, to):
        n = used[0]
        used[0] += 1
        made = pltpu.make_async_remote_copy(
            src_ref=src, dst_ref=dst, send_sem=send.at[n], recv_sem=recv.at[n],
            device_id=device(to, core), device_id_type=MESH,
        )
        made.start()
        started.append(made)
        return made

    def spot(owner, part):
        ox, oy, _ = owner
        start = (ox * 2 + oy // 2) * rows + part * half
        return new_ref.at[pl.ds(pl.multiple_of(start, half), half)]

    def piece(part):
        return fresh.at[pl.ds(part * half, half)]

    from_below = copy(piece(1), relay, above)
    from_left = [copy(piece(0), spot(xyz, 0), right)]
    from_right = [None, copy(piece(1), spot(xyz, 1), left)]
    from_across = copy(piece(0), spot(xyz, 0), across)
    from_left.append(copy(piece(1), spot(xyz, 1), right))
    from_right[0] = copy(piece(0), spot(xyz, 0), left)
    local = pltpu.make_async_copy(
        fresh, new_ref.at[pl.ds(pl.multiple_of((x * 2 + y // 2) * rows, rows), rows)], keep
    )
    local.start()
    ends = []
    from_below.wait_recv()
    relayed = copy(relay, spot(below, 1), above)
    from_left[0].wait_recv()
    ends.append(copy(spot(left, 0), spot(left, 0), right))
    from_right[1].wait_recv()
    ends.append(copy(spot(right, 1), spot(right, 1), left))
    from_across.wait_recv()
    lefts = [copy(spot(across, 0), spot(across, 0), right)]
    rights = [copy(spot(across, 0), spot(across, 0), left)]
    relayed.wait_recv()
    rights.append(copy(spot(across, 1), spot(across, 1), left))
    lefts.append(copy(spot(across, 1), spot(across, 1), right))
    lefts[0].wait_recv()
    far = moved(left, 1, 2)
    ends.append(copy(spot(far, 0), spot(far, 0), right))
    rights[1].wait_recv()
    far = moved(right, 1, 2)
    ends.append(copy(spot(far, 1), spot(far, 1), left))
    for made in [from_left[1], from_right[0], lefts[1], rights[0]] + ends:
        made.wait_recv()
    for made in started:
        made.wait_send()
    local.wait()


def gather(sums, count, cents, rot, panel_ways):
    rows, features = cents.shape
    return pl.pallas_call(
        gather_kernel,
        in_specs=vmem(4),
        out_specs=pl.BlockSpec(memory_space=pl.ANY),
        out_shape=jax.ShapeDtypeStruct((panel_ways * rows, features), BF16),
        scratch_shapes=[
            pltpu.VMEM((rows, features), BF16),
            pltpu.VMEM((rows // 2, features), BF16),
            pltpu.SemaphoreType.DMA,
            pltpu.SemaphoreType.DMA((15,)),
            pltpu.SemaphoreType.DMA((15,)),
        ],
        compiler_params=pltpu.CompilerParams(
            collective_id=2, has_side_effects=True, vmem_limit_bytes=48 << 20
        ),
        name="gather",
    )(sums, count, cents, rot)


def dense(points, labels, centroids):
    data_ways = lax.axis_size("dp")
    panel_ways = lax.axis_size("cent")
    block_rows = centroids.shape[0]
    features = points.shape[1]
    column = lax.axis_index("cent")
    owner_block = labels // block_rows
    inside = owner_block % panel_ways == column
    slot_index = jnp.where(
        inside, owner_block // panel_ways * block_rows + labels % block_rows, data_ways * block_rows
    )
    vectors = points.astype(F32)
    local_sums = jax.ops.segment_sum(vectors, slot_index, num_segments=data_ways * block_rows)
    local_counts = jax.ops.segment_sum(
        jnp.ones(labels.shape, F32), slot_index, num_segments=data_ways * block_rows
    )
    label_sums, label_counts = (
        lax.psum_scatter(local_sums, "dp", scatter_dimension=0, tiled=True),
        lax.psum_scatter(local_counts, "dp", scatter_dimension=0, tiled=True),
    )
    old_rows = centroids.astype(F32)
    cross_cov = lax.psum(
        lax.dot_general(
            label_sums, old_rows, (((0,), (0,)), ((), ())), precision=lax.Precision.HIGHEST
        ),
        ("dp", "cent"),
    )
    scale_root = jnp.sqrt(jnp.sum(cross_cov * cross_cov) / features + epsilon)
    rotation = cross_cov / (3.0 * scale_root)
    for iteration in range(NS_STEPS):
        inner_prod = jnp.dot(rotation, rotation.T, precision=lax.Precision.HIGHEST)
        rotation = 1.5 * rotation - 0.5 * jnp.dot(
            inner_prod, rotation, precision=lax.Precision.HIGHEST
        )
    rotated_sums = jnp.dot(label_sums, rotation, precision=lax.Precision.HIGHEST)
    fresh_rows = ((rotated_sums + old_rows) / (label_counts[:, None] + 1.0)).astype(BF16)
    new_centroids = lax.all_gather(fresh_rows, "cent", axis=0, tiled=True)
    return (new_centroids, rotation)


def local(points, labels, centroids):
    panel_ways = lax.axis_size("cent")
    sums, count, part = exchange(labels, points, centroids)
    cov = reduce_all(part)
    rotation = polar(cov)
    new_centroids = gather(sums, count, centroids, rotation, panel_ways)
    _, new_centroids, rotation = lax.while_loop(
        lambda state: state[0],
        lambda state: (jnp.array(False), *dense(points, labels, centroids)),
        (jnp.logical_not(jnp.isfinite(cov[0, 0])), new_centroids, rotation),
    )
    return new_centroids, rotation


def solution(mesh):
    return jax.shard_map(
        local,
        mesh=mesh,
        in_specs=(P("dp", None), P("dp"), P(("dp", "cent"), None)),
        out_specs=(P("dp", None), P()),
        check_vma=False,
    )
```

```python
import functools

import jax
import jax.numpy as jnp
from jax import lax
from jax.experimental import pallas as pl
from jax.experimental.pallas import tpu as pltpu
from jax.sharding import PartitionSpec as P

MESH = pl.DeviceIdType.MESH
F32 = jnp.float32
BF16 = jnp.bfloat16

NS_STEPS = 3
epsilon = 1e-06

CHUNK = 512
KEEP = 128
CAP = 112
SLOT = 128
WAYS = 4
LANES = ((0, 384), (384, 384), (768, 256))


def dot(a, b, dims=((1,), (0,))):
    return lax.dot_general(a, b, (dims, ((), ())), preferred_element_type=F32)


def split(x):
    hi = x.astype(BF16)
    return hi, (x - hi.astype(F32)).astype(BF16)


def iota(shape, axis):
    return lax.broadcasted_iota(jnp.int32, shape, axis)


def exchange_kernel(
    block_rows, lab_ref, pts_ref, cents_ref, sums_ref, count_ref, cov_ref,
    pts, tri, hits, rank, meta, kept, metas, out, got, up, down, out_id, got_id, load, send, recv,
):
    dp, panel = lax.axis_index("dp"), lax.axis_index("cent")
    data_ways, panel_ways = lax.axis_size("dp"), lax.axis_size("cent")
    steps = lab_ref.shape[0]
    yl, z, core = dp // 8, dp // 2 % 4, dp % 2

    def at(dy, dz, dc):
        return {"dp": ((yl + dy) % 2 * 4 + (z + dz) % 4) * 2 + (core + dc) % 2}

    loads = []
    for step in range(steps):
        loads.append(
            pltpu.make_async_copy(
                pts_ref.at[pl.ds(step * CHUNK, CHUNK)], pts.at[step], load.at[step]
            )
        )
        loads[-1].start()
    barrier = pltpu.get_barrier_semaphore()
    for dy in range(2):
        for dz in range(4):
            for dc in range(2):
                if dy or dz or dc:
                    pl.semaphore_signal(
                        barrier, inc=1, device_id=at(dy, dz, dc), device_id_type=MESH
                    )

    tri[...] = jnp.where(
        iota((CHUNK, CHUNK), 0) <= iota((CHUNK, CHUNK), 1), 1.0, 0.0
    ).astype(BF16)
    for step in range(steps):
        block = lab_ref[step] // block_rows
        dest = block // panel_ways
        hits[step * data_ways : (step + 1) * data_ways, :] = jnp.where(
            jnp.logical_and(
                iota((data_ways, CHUNK), 0) == dest, block % panel_ways == panel
            ),
            1.0,
            0.0,
        )
    counts = dot(hits[...].astype(BF16), tri[...])
    carry = jnp.zeros((data_ways, 1), F32)
    most = jnp.zeros((1, 1), F32)
    row = iota((16, CHUNK), 0)
    for step in range(steps):
        hit = hits[step * data_ways : (step + 1) * data_ways, :]
        count = counts[step * data_ways : (step + 1) * data_ways, :]
        order = jnp.sum(
            hit * jnp.sum(count, axis=0, keepdims=True), axis=0, keepdims=True
        )
        rank[step] = order.astype(jnp.int32)
        spot = jnp.sum(hit * (count + carry), axis=0, keepdims=True)
        last = count[:, CHUNK - 1 : CHUNK]
        carry = carry + last
        most = jnp.maximum(most, jnp.sum(last, axis=0, keepdims=True))
        lab = lab_ref[step]
        dest = (lab // block_rows // panel_ways).astype(F32)
        slot = (lab % block_rows + 1).astype(F32)
        meta[step] = jnp.where(
            row == 0,
            dest,
            jnp.where(row == 1, jnp.minimum(spot, 255.0), jnp.where(row == 2, slot, 0.0)),
        ).astype(BF16)
    over = jnp.logical_or(most > KEEP, jnp.max(carry, axis=0, keepdims=True) > CAP)
    bad = jnp.where(over, jnp.inf, 0.0)

    for step in range(steps):
        pick = jnp.where(iota((KEEP, CHUNK), 0) + 1 == rank[step], 1.0, 0.0).astype(BF16)
        metas[:, step * KEEP : (step + 1) * KEEP] = dot(
            meta[step], pick, ((1,), (1,))
        ).astype(BF16)
        loads[step].wait()
        kept[step * KEEP : (step + 1) * KEEP, :] = dot(pick, pts[step]).astype(BF16)

    pl.semaphore_wait(barrier, data_ways - 1)
    used = [0]
    started = []

    def copy(src, dst, to):
        n = used[0]
        used[0] += 1
        made = pltpu.make_async_remote_copy(
            src_ref=src, dst_ref=dst, send_sem=send.at[n], recv_sem=recv.at[n],
            device_id=to, device_id_type=MESH,
        )
        made.start()
        started.append(made)
        return made

    def share(n):
        return CAP // 2 // 16 * 16 + (16 if n in (0, 3) else 0)

    places = metas[...]
    whole = places.astype(F32).astype(jnp.int32)
    dests, spots = whole[0:1, :], whole[1:2, :]
    total = places.shape[1]
    arrive = {}
    relays = []
    order = (
        [(1, 2, 0), (1, 2, 1), (0, 2, 0), (0, 2, 1)]
        + [(1, dz, dc) for dz in (1, 3) for dc in range(2)]
        + [(1, 0, 0), (1, 0, 1)]
        + [(0, dz, dc) for dz in (1, 3) for dc in range(2)]
        + [(0, 0, 1), (0, 0, 0)]
    )
    for dy, dz, dc in order:
        k = (dy * 4 + dz) * 2 + dc
        to = at(dy, dz, dc)
        wanted = jnp.where(dests == to["dp"], spots, 0)
        pick = jnp.where(iota((SLOT, total), 0) + 1 == wanted, 1.0, 0.0).astype(BF16)
        out[k] = dot(pick, kept[...]).astype(BF16)
        out_id[k] = dot(places, pick, ((1,), (1,))).astype(BF16)
        if k == 0:
            continue
        arrive[k] = [copy(out_id.at[k], got_id.at[k], to)]
        if dz == 2:
            n = dy * 2 + dc
            cut = share(n)
            for hop, buf, lo, rows in ((1, up, 0, cut), (3, down, cut, CAP - cut)):
                leg = copy(
                    out.at[k, pl.ds(lo, rows)], buf.at[n, pl.ds(0, rows)], at(0, hop, 0)
                )
                relays.append((leg, k, buf.at[n, pl.ds(0, rows)], lo, rows, at(dy, hop, dc)))
        else:
            arrive[k].append(copy(out.at[k, pl.ds(0, CAP)], got.at[k, pl.ds(0, CAP)], to))
    for leg, k, held, lo, rows, to in relays:
        leg.wait_recv()
        arrive[k].append(copy(held, got.at[k, pl.ds(lo, rows)], to))

    rows, features = sums_ref.shape
    got[:, CAP:SLOT, :] = jnp.zeros((data_ways, SLOT - CAP, features), BF16)
    ones = jnp.ones((SLOT, 128), BF16)
    for dy, dz, dc in order[::-1]:
        k = (dy * 4 + dz) * 2 + dc
        for made in arrive.get(k, ()):
            made.wait_recv()
        ids = (got_id if k else out_id)[k].astype(F32).astype(jnp.int32)
        pick = jnp.where(iota((rows, SLOT), 0) + 1 == ids[2:3, :], 1.0, 0.0).astype(BF16)
        vectors = (got if k else out)[k]
        if k:
            sums_ref[...] += dot(pick, vectors)
            count_ref[...] += dot(pick, ones)
        else:
            sums_ref[...] = dot(pick, vectors)
            count_ref[...] = dot(pick, ones)
    hi, lo = split(sums_ref[...])
    cents = cents_ref[...]
    first = ((0,), (0,))
    cov_ref[...] = dot(hi, cents, first) + dot(lo, cents, first)
    cov_ref[0:8, 0:128] = cov_ref[0:8, 0:128] + bad
    for made in started:
        made.wait_send()


def vmem(n):
    return [pl.BlockSpec(memory_space=pltpu.VMEM)] * n


def exchange(labels, points, cents):
    data_ways = lax.axis_size("dp")
    rows, features = cents.shape
    steps = points.shape[0] // CHUNK
    copies = 2 * data_ways + 12
    return pl.pallas_call(
        functools.partial(exchange_kernel, rows),
        in_specs=vmem(1) + [pl.BlockSpec(memory_space=pl.ANY)] + vmem(1),
        out_specs=vmem(3),
        out_shape=[
            jax.ShapeDtypeStruct((rows, features), F32),
            jax.ShapeDtypeStruct((rows, 128), F32),
            jax.ShapeDtypeStruct((features, features), F32),
        ],
        scratch_shapes=[
            pltpu.VMEM((steps, CHUNK, features), BF16),
            pltpu.VMEM((CHUNK, CHUNK), BF16),
            pltpu.VMEM((steps * data_ways, CHUNK), F32),
            pltpu.VMEM((steps, 1, CHUNK), jnp.int32),
            pltpu.VMEM((steps, 16, CHUNK), BF16),
            pltpu.VMEM((steps * KEEP, features), BF16),
            pltpu.VMEM((16, steps * KEEP), BF16),
            pltpu.VMEM((data_ways, SLOT, features), BF16),
            pltpu.VMEM((data_ways, SLOT, features), BF16),
            pltpu.VMEM((4, 64, features), BF16),
            pltpu.VMEM((4, 64, features), BF16),
            pltpu.VMEM((data_ways, 16, SLOT), BF16),
            pltpu.VMEM((data_ways, 16, SLOT), BF16),
            pltpu.SemaphoreType.DMA((steps,)),
            pltpu.SemaphoreType.DMA((copies,)),
            pltpu.SemaphoreType.DMA((copies,)),
        ],
        compiler_params=pltpu.CompilerParams(
            collective_id=0, has_side_effects=True, vmem_limit_bytes=52 << 20
        ),
        name="exchange",
    )(labels.reshape(steps, 1, CHUNK), points, cents)


def place():
    dp, cent = lax.axis_index("dp"), lax.axis_index("cent")
    x, y, z = cent // 2, cent % 2 * 2 + dp // 8, dp // 2 % 4
    return (x, y, z), dp % 2


def device(xyz, core):
    x, y, z = xyz
    return {"dp": (y % 2 * 4 + z) * 2 + core, "cent": x * 2 + y // 2}


def moved(xyz, axis, by):
    return tuple((c + by) % WAYS if a == axis else c for a, c in enumerate(xyz))


def settle_kernel(
    part_ref, rot_ref, half, got1, got2, got3, acc, own, hx, lx, top, low, square,
    send, recv, tile_send, tile_recv,
):
    xyz, core = place()
    features = part_ref.shape[1]
    mine = features // 2
    tile = 256
    tiles = features // tile
    barrier = pltpu.get_barrier_semaphore()
    other = device(xyz, 1 - core)
    partners = [other] + [
        device(moved(xyz, axis, by), core) for axis in range(3) for by in range(1, WAYS)
    ]
    for partner in partners:
        pl.semaphore_signal(barrier, inc=1, device_id=partner, device_id_type=MESH)
    pl.semaphore_wait(barrier, len(partners))

    used = [0]
    started = []

    def remote(src, dst, s, r, to):
        made = pltpu.make_async_remote_copy(
            src_ref=src, dst_ref=dst, send_sem=s, recv_sem=r, device_id=to, device_id_type=MESH
        )
        started.append(made)
        return made

    def copy(src, dst, to):
        n = used[0]
        used[0] += 1
        made = remote(src, dst, send.at[n], recv.at[n], to)
        made.start()
        return made

    here = pl.multiple_of(core * mine, mine)
    there = pl.multiple_of((1 - core) * mine, mine)
    parts = range(len(LANES))
    lanes = [pl.ds(lane, width) for lane, width in LANES]
    sizes = [mine // WAYS ** (stage + 1) for stage in range(3)]
    gots = (got1, got2, got3)
    base = [0, 0, 0]
    waits = [
        [copy(part_ref.at[pl.ds(there, mine), lanes[part]], half.at[:, lanes[part]], other)]
        for part in parts
    ]

    def scatter(stage, part):
        size, axis = sizes[stage], (part + stage) % 3
        made = []
        for by in range(1, WAYS):
            to = moved(xyz, axis, by)
            start = pl.multiple_of(base[part] + to[axis] * size, size)
            made.append(
                copy(
                    acc.at[pl.ds(start, size), lanes[part]],
                    gots[stage].at[by - 1, :, lanes[part]],
                    device(to, core),
                )
            )
        return made

    def spread(stage, part):
        size, axis = sizes[stage], (part + stage) % 3
        span = own.at[pl.ds(pl.multiple_of(base[part], size), size), lanes[part]]
        made = [copy(span, span, device(moved(xyz, axis, by), core)) for by in range(1, WAYS)]
        base[part] = base[part] - xyz[axis] * size
        return made

    def arrived(part):
        for made in waits[part]:
            made.wait_recv()

    for part in parts:
        arrived(part)
        acc[:, lanes[part]] = part_ref[pl.ds(here, mine), lanes[part]] + half[:, lanes[part]]
        waits[part] = scatter(0, part)
    for stage in range(3):
        size = sizes[stage]
        for part in parts:
            arrived(part)
            base[part] = pl.multiple_of(base[part] + xyz[(part + stage) % 3] * size, size)
            at = (pl.ds(base[part], size), lanes[part])
            total = acc[at]
            for by in range(1, WAYS):
                total = total + gots[stage][by - 1, :, lanes[part]]
            if stage < 2:
                acc[at] = total
                waits[part] = scatter(stage + 1, part)
            else:
                own[at] = total
                waits[part] = spread(2, part)
    for stage in (1, 0):
        for part in parts:
            arrived(part)
            waits[part] = spread(stage, part)
    squares = jnp.zeros((1, 1), F32)
    for part in parts:
        arrived(part)
        at = (slice(0, mine), lanes[part])
        value = own[at]
        hx[0, 0:mine, lanes[part]], lx[0, 0:mine, lanes[part]] = split(value)
        waits[part] = [
            copy(ref.at[0, pl.ds(0, mine), lanes[part]], ref.at[0, pl.ds(mine, mine), lanes[part]], other)
            for ref in (hx, lx)
        ]
        squares = squares + jnp.sum(
            jnp.sum(value * value, axis=0, keepdims=True), axis=1, keepdims=True
        )
    square[0] = jnp.broadcast_to(squares, square.shape[1:])
    waits.append([copy(square.at[0], square.at[1], other)])

    def sent(step, b, c, ref):
        if step == NS_STEPS - 1:
            cols = pl.ds(pl.multiple_of(c * tile, tile), tile)
            src, dst = own.at[:, cols], rot_ref.at[pl.ds(here, mine), cols]
        else:
            cols = pl.ds(pl.multiple_of(c * tile, tile), tile)
            src = ref.at[(step + 1) % 2, pl.ds(0, mine), cols]
            dst = ref.at[(step + 1) % 2, pl.ds(mine, mine), cols]
        return pltpu.make_async_remote_copy(
            src_ref=src, dst_ref=dst, send_sem=tile_send.at[step, b, c],
            recv_sem=tile_recv.at[step, b, c], device_id=other, device_id_type=MESH,
        )

    both = ((1,), (1,))
    keep, turned = 1.5, 0.5
    for step in range(NS_STEPS):
        now, later = step % 2, (step + 1) % 2

        def inner(j):
            rows = pl.ds(pl.multiple_of(j * tile, tile), tile)
            hi, lo = hx[now, 0:mine, :], lx[now, 0:mine, :]
            there_hi = hx[now, rows, :]
            value = dot(hi, there_hi, both) + (
                dot(hi, lx[now, rows, :], both) + dot(lo, there_hi, both)
            )
            top[:, rows], low[:, rows] = split(value)

        pl.loop(0, tiles // 2)(inner)
        if step == 0:
            for row in waits:
                for made in row:
                    made.wait_recv()
            for made in started:
                made.wait_send()
            total = square[0, 0:1, 0:1] + square[1, 0:1, 0:1]
            inverse = 1.0 / (3.0 * jnp.sqrt(total / features + epsilon))
            keep, turned = 1.5 * inverse, 0.5 * inverse * inverse * inverse
        else:
            keep, turned = 1.5, 0.5
            for c in range(tiles):
                for b, ref in enumerate((hx, lx)):
                    sent(step - 1, b, c, ref).wait()
        pl.loop(tiles // 2, tiles)(inner)

        @pl.loop(0, tiles)
        def _(c):
            cols = pl.ds(pl.multiple_of(c * tile, tile), tile)
            hi = hx[now, :, cols]
            turn = dot(top[...], hi) + (dot(top[...], lx[now, :, cols]) + dot(low[...], hi))
            value = keep * own[:, cols] - turned * turn
            own[:, cols] = value
            if step == NS_STEPS - 1:
                rot_ref[pl.ds(here, mine), cols] = value
                sent(step, 0, c, None).start()
            else:
                hx[later, 0:mine, cols], lx[later, 0:mine, cols] = split(value)
                for b, ref in enumerate((hx, lx)):
                    sent(step, b, c, ref).start()

    for c in range(tiles):
        sent(NS_STEPS - 1, 0, c, None).wait()


def settle(part):
    features = part.shape[0]
    mine = features // 2
    sizes = [mine // WAYS**n for n in (1, 2, 3)]
    copies = 3 + 2 * 3 * 3 * (WAYS - 1) + 2 * 3 + 1
    return pl.pallas_call(
        settle_kernel,
        in_specs=vmem(1),
        out_specs=pl.BlockSpec(memory_space=pltpu.VMEM),
        out_shape=jax.ShapeDtypeStruct(part.shape, F32),
        scratch_shapes=[pltpu.VMEM((mine, features), F32)]
        + [pltpu.VMEM((WAYS - 1, size, features), F32) for size in sizes]
        + [pltpu.VMEM((mine, features), F32)] * 2
        + [pltpu.VMEM((2, features, features), BF16)] * 2
        + [pltpu.VMEM((mine, features), BF16)] * 2
        + [pltpu.VMEM((2, 8, 128), F32)]
        + [pltpu.SemaphoreType.DMA((copies,))] * 2
        + [pltpu.SemaphoreType.DMA((NS_STEPS, 2, features // 256))] * 2,
        compiler_params=pltpu.CompilerParams(
            collective_id=1, has_side_effects=True, vmem_limit_bytes=40 << 20
        ),
        name="settle",
    )(part)


def gather_kernel(sums_ref, count_ref, cents_ref, rot_ref, new_ref, fresh, relay, keep, send, recv):
    xyz, core = place()
    x, y, z = xyz
    right, left = moved(xyz, 0, 1), moved(xyz, 0, WAYS - 1)
    above, below = moved(xyz, 1, 1), moved(xyz, 1, WAYS - 1)
    across = moved(xyz, 1, 2)
    barrier = pltpu.get_barrier_semaphore()
    for partner in (right, left, above, below, across):
        pl.semaphore_signal(
            barrier, inc=1, device_id=device(partner, core), device_id_type=MESH
        )
    rows = fresh.shape[0]
    half = rows // 2
    hi, lo = split(sums_ref[...])
    top, low = split(rot_ref[...])
    turned = dot(hi, top) + (dot(hi, low) + dot(lo, top))
    fresh[...] = (
        (turned + cents_ref[...].astype(F32)) / (count_ref[:, 0:1] + 1.0)
    ).astype(BF16)
    pl.semaphore_wait(barrier, 5)

    used = [0]
    started = []

    def copy(src, dst, to):
        n = used[0]
        used[0] += 1
        made = pltpu.make_async_remote_copy(
            src_ref=src, dst_ref=dst, send_sem=send.at[n], recv_sem=recv.at[n],
            device_id=device(to, core), device_id_type=MESH,
        )
        made.start()
        started.append(made)
        return made

    def spot(owner, part):
        ox, oy, _ = owner
        start = (ox * 2 + oy // 2) * rows + part * half
        return new_ref.at[pl.ds(pl.multiple_of(start, half), half)]

    def piece(part):
        return fresh.at[pl.ds(part * half, half)]

    from_below = copy(piece(1), relay, above)
    from_left = [copy(piece(0), spot(xyz, 0), right)]
    from_right = [None, copy(piece(1), spot(xyz, 1), left)]
    from_across = copy(piece(0), spot(xyz, 0), across)
    from_left.append(copy(piece(1), spot(xyz, 1), right))
    from_right[0] = copy(piece(0), spot(xyz, 0), left)
    local = pltpu.make_async_copy(
        fresh, new_ref.at[pl.ds(pl.multiple_of((x * 2 + y // 2) * rows, rows), rows)], keep
    )
    local.start()
    ends = []
    from_below.wait_recv()
    relayed = copy(relay, spot(below, 1), above)
    from_left[0].wait_recv()
    ends.append(copy(spot(left, 0), spot(left, 0), right))
    from_right[1].wait_recv()
    ends.append(copy(spot(right, 1), spot(right, 1), left))
    from_across.wait_recv()
    lefts = [copy(spot(across, 0), spot(across, 0), right)]
    rights = [copy(spot(across, 0), spot(across, 0), left)]
    relayed.wait_recv()
    rights.append(copy(spot(across, 1), spot(across, 1), left))
    lefts.append(copy(spot(across, 1), spot(across, 1), right))
    lefts[0].wait_recv()
    far = moved(left, 1, 2)
    ends.append(copy(spot(far, 0), spot(far, 0), right))
    rights[1].wait_recv()
    far = moved(right, 1, 2)
    ends.append(copy(spot(far, 1), spot(far, 1), left))
    for made in [from_left[1], from_right[0], lefts[1], rights[0]] + ends:
        made.wait_recv()
    for made in started:
        made.wait_send()
    local.wait()


def gather(sums, count, cents, rot, panel_ways):
    rows, features = cents.shape
    return pl.pallas_call(
        gather_kernel,
        in_specs=vmem(4),
        out_specs=pl.BlockSpec(memory_space=pl.ANY),
        out_shape=jax.ShapeDtypeStruct((panel_ways * rows, features), BF16),
        scratch_shapes=[
            pltpu.VMEM((rows, features), BF16),
            pltpu.VMEM((rows // 2, features), BF16),
            pltpu.SemaphoreType.DMA,
            pltpu.SemaphoreType.DMA((15,)),
            pltpu.SemaphoreType.DMA((15,)),
        ],
        compiler_params=pltpu.CompilerParams(
            collective_id=2, has_side_effects=True, vmem_limit_bytes=48 << 20
        ),
        name="gather",
    )(sums, count, cents, rot)


def dense(points, labels, centroids):
    data_ways = lax.axis_size("dp")
    panel_ways = lax.axis_size("cent")
    block_rows = centroids.shape[0]
    features = points.shape[1]
    column = lax.axis_index("cent")
    owner_block = labels // block_rows
    inside = owner_block % panel_ways == column
    slot_index = jnp.where(
        inside, owner_block // panel_ways * block_rows + labels % block_rows, data_ways * block_rows
    )
    vectors = points.astype(F32)
    local_sums = jax.ops.segment_sum(vectors, slot_index, num_segments=data_ways * block_rows)
    local_counts = jax.ops.segment_sum(
        jnp.ones(labels.shape, F32), slot_index, num_segments=data_ways * block_rows
    )
    label_sums, label_counts = (
        lax.psum_scatter(local_sums, "dp", scatter_dimension=0, tiled=True),
        lax.psum_scatter(local_counts, "dp", scatter_dimension=0, tiled=True),
    )
    old_rows = centroids.astype(F32)
    cross_cov = lax.psum(
        lax.dot_general(
            label_sums, old_rows, (((0,), (0,)), ((), ())), precision=lax.Precision.HIGHEST
        ),
        ("dp", "cent"),
    )
    scale_root = jnp.sqrt(jnp.sum(cross_cov * cross_cov) / features + epsilon)
    rotation = cross_cov / (3.0 * scale_root)
    for iteration in range(NS_STEPS):
        inner_prod = jnp.dot(rotation, rotation.T, precision=lax.Precision.HIGHEST)
        rotation = 1.5 * rotation - 0.5 * jnp.dot(
            inner_prod, rotation, precision=lax.Precision.HIGHEST
        )
    rotated_sums = jnp.dot(label_sums, rotation, precision=lax.Precision.HIGHEST)
    fresh_rows = ((rotated_sums + old_rows) / (label_counts[:, None] + 1.0)).astype(BF16)
    new_centroids = lax.all_gather(fresh_rows, "cent", axis=0, tiled=True)
    return (new_centroids, rotation)


def local(points, labels, centroids):
    panel_ways = lax.axis_size("cent")
    sums, count, part = exchange(labels, points, centroids)
    rotation = settle(part)
    new_centroids = gather(sums, count, centroids, rotation, panel_ways)
    _, new_centroids, rotation = lax.while_loop(
        lambda state: state[0],
        lambda state: (jnp.array(False), *dense(points, labels, centroids)),
        (jnp.logical_not(jnp.isfinite(rotation[0, 0])), new_centroids, rotation),
    )
    return new_centroids, rotation


def solution(mesh):
    return jax.shard_map(
        local,
        mesh=mesh,
        in_specs=(P("dp", None), P("dp"), P(("dp", "cent"), None)),
        out_specs=(P("dp", None), P()),
        check_vma=False,
    )
```

```python
import functools

import jax
import jax.numpy as jnp
from jax import lax
from jax.experimental import pallas as pl
from jax.experimental.pallas import tpu as pltpu
from jax.sharding import PartitionSpec as P

MESH = pl.DeviceIdType.MESH
F32 = jnp.float32
BF16 = jnp.bfloat16

NS_STEPS = 3
epsilon = 1e-06

CHUNK = 512
KEEP = 128
CAP = 112
SLOT = 128
WAYS = 4
LANES = ((0, 384), (384, 384), (768, 256))


def dot(a, b, dims=((1,), (0,))):
    return lax.dot_general(a, b, (dims, ((), ())), preferred_element_type=F32)


def split(x):
    hi = x.astype(BF16)
    return hi, (x - hi.astype(F32)).astype(BF16)


def iota(shape, axis):
    return lax.broadcasted_iota(jnp.int32, shape, axis)


def place():
    dp, cent = lax.axis_index("dp"), lax.axis_index("cent")
    x, y, z = cent // 2, cent % 2 * 2 + dp // 8, dp // 2 % 4
    return (x, y, z), dp % 2


def device(xyz, core):
    x, y, z = xyz
    return {"dp": (y % 2 * 4 + z) * 2 + core, "cent": x * 2 + y // 2}


def moved(xyz, axis, by):
    return tuple((c + by) % WAYS if a == axis else c for a, c in enumerate(xyz))


class Ring:
    def __init__(self, copy, xyz, core, piece, all_ref):
        self.copy, self.xyz, self.core, self.piece, self.all_ref = copy, xyz, core, piece, all_ref
        self.right, self.left = moved(xyz, 0, 1), moved(xyz, 0, WAYS - 1)
        self.across = moved(xyz, 1, 2)
        self.copies = []

    def spot(self, owner, part):
        half = self.all_ref.shape[0] // (4 * WAYS)
        start = ((owner[0] * 2 + owner[1] // 2) * 2 + part) * half
        return self.all_ref.at[pl.ds(pl.multiple_of(start, half), half)]

    def send(self, owner, part, to, fresh=False):
        spot = self.spot(owner, part)
        made = self.copy(self.piece(part) if fresh else spot, spot, device(to, self.core))
        self.copies.append(made)
        return made

    def begin(self):
        me = self.xyz
        self.over = [self.send(me, 0, self.across, True)]
        self.rights = [self.send(me, 0, self.right, True)]
        self.lefts = [None, self.send(me, 1, self.left, True)]
        self.over.append(self.send(me, 1, self.across, True))
        self.rights.append(self.send(me, 1, self.right, True))
        self.lefts[0] = self.send(me, 0, self.left, True)

    def forward(self):
        self.rights[0].wait_recv()
        self.ends = [self.send(self.left, 0, self.right)]
        self.lefts[1].wait_recv()
        self.ends.append(self.send(self.right, 1, self.left))
        self.over[0].wait_recv()
        self.rights2 = [self.send(self.across, 0, self.right)]
        self.lefts2 = [self.send(self.across, 0, self.left)]
        self.over[1].wait_recv()
        self.lefts2.append(self.send(self.across, 1, self.left))
        self.rights2.append(self.send(self.across, 1, self.right))

    def last(self):
        self.rights2[0].wait_recv()
        self.ends.append(self.send(moved(self.left, 1, 2), 0, self.right))
        self.lefts2[1].wait_recv()
        self.ends.append(self.send(moved(self.right, 1, 2), 1, self.left))

    def finish(self):
        for made in [self.rights[1], self.lefts[0], self.rights2[1], self.lefts2[0]] + self.ends:
            made.wait_recv()


RING = 14


def exchange_kernel(
    block_rows, lab_ref, pts_ref, cents_ref, sums_ref, count_ref, cov_ref, old_ref,
    pts, tri, hits, rank, meta, kept, metas, out, got, out_id, got_id, load, local, send, recv,
):
    xyz, _ = place()
    dp, panel = lax.axis_index("dp"), lax.axis_index("cent")
    data_ways, panel_ways = lax.axis_size("dp"), lax.axis_size("cent")
    steps = lab_ref.shape[0]
    yl, z, core = dp // 8, dp // 2 % 4, dp % 2

    def at(dy, dz, dc):
        return {"dp": ((yl + dy) % 2 * 4 + (z + dz) % 4) * 2 + (core + dc) % 2}

    loads = []
    for step in range(steps):
        loads.append(
            pltpu.make_async_copy(
                pts_ref.at[pl.ds(step * CHUNK, CHUNK)], pts.at[step], load.at[step]
            )
        )
        loads[-1].start()
    barrier = pltpu.get_barrier_semaphore()
    for dy in range(2):
        for dz in range(4):
            for dc in range(2):
                if dy or dz or dc:
                    pl.semaphore_signal(
                        barrier, inc=1, device_id=at(dy, dz, dc), device_id_type=MESH
                    )
    for partner in (moved(xyz, 0, 1), moved(xyz, 0, WAYS - 1), moved(xyz, 1, 2)):
        pl.semaphore_signal(
            barrier, inc=1, device_id=device(partner, core), device_id_type=MESH
        )

    tri[...] = jnp.where(
        iota((CHUNK, CHUNK), 0) <= iota((CHUNK, CHUNK), 1), 1.0, 0.0
    ).astype(BF16)
    for step in range(steps):
        block = lab_ref[step] // block_rows
        dest = block // panel_ways
        hits[step * data_ways : (step + 1) * data_ways, :] = jnp.where(
            jnp.logical_and(
                iota((data_ways, CHUNK), 0) == dest, block % panel_ways == panel
            ),
            1.0,
            0.0,
        )
    counts = dot(hits[...].astype(BF16), tri[...])
    carry = jnp.zeros((data_ways, 1), F32)
    most = jnp.zeros((1, 1), F32)
    row = iota((16, CHUNK), 0)
    for step in range(steps):
        hit = hits[step * data_ways : (step + 1) * data_ways, :]
        count = counts[step * data_ways : (step + 1) * data_ways, :]
        order = jnp.sum(
            hit * jnp.sum(count, axis=0, keepdims=True), axis=0, keepdims=True
        )
        rank[step] = order.astype(jnp.int32)
        spot = jnp.sum(hit * (count + carry), axis=0, keepdims=True)
        last = count[:, CHUNK - 1 : CHUNK]
        carry = carry + last
        most = jnp.maximum(most, jnp.sum(last, axis=0, keepdims=True))
        lab = lab_ref[step]
        dest = (lab // block_rows // panel_ways).astype(F32)
        slot = (lab % block_rows + 1).astype(F32)
        meta[step] = jnp.where(
            row == 0,
            dest,
            jnp.where(row == 1, jnp.minimum(spot, 255.0), jnp.where(row == 2, slot, 0.0)),
        ).astype(BF16)
    over = jnp.logical_or(most > KEEP, jnp.max(carry, axis=0, keepdims=True) > CAP)
    bad = jnp.where(over, jnp.inf, 0.0)

    pl.semaphore_wait(barrier, data_ways + 2)
    used = [0]
    started = []

    def copy(src, dst, to):
        n = used[0]
        used[0] += 1
        made = pltpu.make_async_remote_copy(
            src_ref=src, dst_ref=dst, send_sem=send.at[n], recv_sem=recv.at[n],
            device_id=to, device_id_type=MESH,
        )
        made.start()
        started.append(made)
        return made

    half = block_rows // 2
    ring = Ring(copy, xyz, core, lambda part: cents_ref.at[pl.ds(part * half, half)], old_ref)
    ring.begin()
    own = pl.ds(pl.multiple_of(panel * block_rows, block_rows), block_rows)
    stay = pltpu.make_async_copy(cents_ref, old_ref.at[own], local)
    stay.start()

    for step in range(steps):
        pick = jnp.where(iota((KEEP, CHUNK), 0) + 1 == rank[step], 1.0, 0.0).astype(BF16)
        metas[:, step * KEEP : (step + 1) * KEEP] = dot(
            meta[step], pick, ((1,), (1,))
        ).astype(BF16)
        loads[step].wait()
        kept[step * KEEP : (step + 1) * KEEP, :] = dot(pick, pts[step]).astype(BF16)

    places = metas[...]
    whole = places.astype(F32).astype(jnp.int32)
    dests, spots = whole[0:1, :], whole[1:2, :]
    total = places.shape[1]
    arrive = {}
    order = [(1, 2), (0, 2), (1, 1), (0, 3), (1, 3), (0, 1), (1, 0), (0, 0)]
    for dy, dz in order:
        wanted = jnp.concatenate(
            [
                jnp.broadcast_to(
                    jnp.where(dests == at(dy, dz, dc)["dp"], spots, 0), (SLOT, total)
                )
                for dc in range(2)
            ],
            axis=0,
        )
        pick = jnp.where(iota((2 * SLOT, total), 0) % SLOT + 1 == wanted, 1.0, 0.0).astype(BF16)
        rows = dot(pick, kept[...]).astype(BF16)
        ids = dot(places, pick, ((1,), (1,))).astype(BF16)
        for dc in range(2):
            k = (dy * 4 + dz) * 2 + dc
            out[k] = rows[dc * SLOT : (dc + 1) * SLOT, :]
            out_id[k] = ids[:, dc * SLOT : (dc + 1) * SLOT]
            if k:
                to = at(dy, dz, dc)
                arrive[k] = [
                    copy(out_id.at[k], got_id.at[k], to),
                    copy(out.at[k, pl.ds(0, CAP)], got.at[k, pl.ds(0, CAP)], to),
                ]
    ring.forward()

    rows, features = sums_ref.shape
    got[:, CAP:SLOT, :] = jnp.zeros((data_ways, SLOT - CAP, features), BF16)
    ones = jnp.ones((8, SLOT), BF16)
    across = ((1,), (1,))
    for dy, dz in order[::-1]:
        for dc in range(2):
            k = (dy * 4 + dz) * 2 + dc
            for made in arrive.get(k, ()):
                made.wait_recv()
            ids = (got_id if k else out_id)[k].astype(F32).astype(jnp.int32)
            pick = jnp.where(iota((rows, SLOT), 0) + 1 == ids[2:3, :], 1.0, 0.0).astype(BF16)
            vectors = (got if k else out)[k]
            if k:
                sums_ref[...] += dot(pick, vectors)
                count_ref[...] += dot(ones, pick, across)
            else:
                sums_ref[...] = dot(pick, vectors)
                count_ref[...] = dot(ones, pick, across)
        if dy == 0 and dz == 3:
            ring.last()
    hi, lo = split(sums_ref[...])
    cents = cents_ref[...]
    first = ((0,), (0,))
    cov_ref[...] = dot(hi, cents, first) + dot(lo, cents, first)
    cov_ref[0:8, 0:128] = cov_ref[0:8, 0:128] + bad
    ring.finish()
    stay.wait()
    for made in started:
        made.wait_send()


def vmem(n):
    return [pl.BlockSpec(memory_space=pltpu.VMEM)] * n


def exchange(labels, points, cents):
    data_ways = lax.axis_size("dp")
    rows, features = cents.shape
    steps = points.shape[0] // CHUNK
    copies = 2 * (data_ways - 1) + RING
    return pl.pallas_call(
        functools.partial(exchange_kernel, rows),
        in_specs=vmem(1) + [pl.BlockSpec(memory_space=pl.ANY)] + vmem(1),
        out_specs=vmem(3) + [pl.BlockSpec(memory_space=pltpu.HBM)],
        out_shape=[
            jax.ShapeDtypeStruct((rows, features), F32),
            jax.ShapeDtypeStruct((8, rows), F32),
            jax.ShapeDtypeStruct((features, features), F32),
            jax.ShapeDtypeStruct((2 * WAYS * rows, features), BF16),
        ],
        scratch_shapes=[
            pltpu.VMEM((steps, CHUNK, features), BF16),
            pltpu.VMEM((CHUNK, CHUNK), BF16),
            pltpu.VMEM((steps * data_ways, CHUNK), F32),
            pltpu.VMEM((steps, 1, CHUNK), jnp.int32),
            pltpu.VMEM((steps, 16, CHUNK), BF16),
            pltpu.VMEM((steps * KEEP, features), BF16),
            pltpu.VMEM((16, steps * KEEP), BF16),
            pltpu.VMEM((data_ways, SLOT, features), BF16),
            pltpu.VMEM((data_ways, SLOT, features), BF16),
            pltpu.VMEM((data_ways, 16, SLOT), BF16),
            pltpu.VMEM((data_ways, 16, SLOT), BF16),
            pltpu.SemaphoreType.DMA((steps,)),
            pltpu.SemaphoreType.DMA,
            pltpu.SemaphoreType.DMA((copies,)),
            pltpu.SemaphoreType.DMA((copies,)),
        ],
        compiler_params=pltpu.CompilerParams(
            collective_id=0, has_side_effects=True, vmem_limit_bytes=40 << 20
        ),
        name="exchange",
    )(labels.reshape(steps, 1, CHUNK), points, cents)


def settle_kernel(
    part_ref, sums_ref, count_ref, rot_ref, all_sums_ref, all_count_ref, half, got1, got2, got3, acc, own, hx, lx, top, low, square,
    send, recv, tile_send, tile_recv, local,
):
    xyz, core = place()
    panel = lax.axis_index("cent")
    panels = [
        device(moved(moved(xyz, 0, dx), 1, dy), core)
        for dx in range(WAYS)
        for dy in (0, 2)
        if dx or dy
    ]
    features = part_ref.shape[1]
    mine = features // 2
    tile = 256
    tiles = features // tile
    barrier = pltpu.get_barrier_semaphore()
    other = device(xyz, 1 - core)
    partners = [other] + [
        device(moved(xyz, axis, by), core) for axis in range(3) for by in range(1, WAYS)
    ]
    partners += [
        device(moved(moved(xyz, 0, dx), 1, 2), core) for dx in range(1, WAYS)
    ]
    for partner in partners:
        pl.semaphore_signal(barrier, inc=1, device_id=partner, device_id_type=MESH)
    pl.semaphore_wait(barrier, len(partners))

    used = [0]
    started = []

    def remote(src, dst, s, r, to):
        made = pltpu.make_async_remote_copy(
            src_ref=src, dst_ref=dst, send_sem=s, recv_sem=r, device_id=to, device_id_type=MESH
        )
        started.append(made)
        return made

    def copy(src, dst, to):
        n = used[0]
        used[0] += 1
        made = remote(src, dst, send.at[n], recv.at[n], to)
        made.start()
        return made

    here = pl.multiple_of(core * mine, mine)
    there = pl.multiple_of((1 - core) * mine, mine)
    parts = range(len(LANES))
    lanes = [pl.ds(lane, width) for lane, width in LANES]
    sizes = [mine // WAYS ** (stage + 1) for stage in range(3)]
    gots = (got1, got2, got3)
    base = [0, 0, 0]
    waits = [
        [copy(part_ref.at[pl.ds(there, mine), lanes[part]], half.at[:, lanes[part]], other)]
        for part in parts
    ]

    def scatter(stage, part):
        size, axis = sizes[stage], (part + stage) % 3
        made = []
        for by in range(1, WAYS):
            to = moved(xyz, axis, by)
            start = pl.multiple_of(base[part] + to[axis] * size, size)
            made.append(
                copy(
                    acc.at[pl.ds(start, size), lanes[part]],
                    gots[stage].at[by - 1, :, lanes[part]],
                    device(to, core),
                )
            )
        return made

    def spread(stage, part):
        size, axis = sizes[stage], (part + stage) % 3
        span = own.at[pl.ds(pl.multiple_of(base[part], size), size), lanes[part]]
        made = [copy(span, span, device(moved(xyz, axis, by), core)) for by in range(1, WAYS)]
        base[part] = base[part] - xyz[axis] * size
        return made

    def arrived(part):
        for made in waits[part]:
            made.wait_recv()

    for part in parts:
        arrived(part)
        acc[:, lanes[part]] = part_ref[pl.ds(here, mine), lanes[part]] + half[:, lanes[part]]
        waits[part] = scatter(0, part)

    rows = sums_ref.shape[0]
    ring = Ring(
        copy, xyz, core, lambda n: sums_ref.at[pl.ds(n * (rows // 2), rows // 2)], all_sums_ref
    )
    ring.begin()
    counts = [copy(count_ref, all_count_ref.at[panel], to) for to in panels]
    stays = [
        pltpu.make_async_copy(
            sums_ref,
            all_sums_ref.at[pl.ds(pl.multiple_of(panel * rows, rows), rows)],
            local.at[0],
        ),
        pltpu.make_async_copy(count_ref, all_count_ref.at[panel], local.at[1]),
    ]
    for made in stays:
        made.start()

    for stage in range(3):
        size = sizes[stage]
        for part in parts:
            arrived(part)
            base[part] = pl.multiple_of(base[part] + xyz[(part + stage) % 3] * size, size)
            at = (pl.ds(base[part], size), lanes[part])
            total = acc[at]
            for by in range(1, WAYS):
                total = total + gots[stage][by - 1, :, lanes[part]]
            if stage < 2:
                acc[at] = total
                waits[part] = scatter(stage + 1, part)
            else:
                own[at] = total
                waits[part] = spread(2, part)
    for stage in (1, 0):
        for part in parts:
            arrived(part)
            waits[part] = spread(stage, part)
    ring.forward()
    squares = jnp.zeros((1, 1), F32)
    for part in parts:
        arrived(part)
        at = (slice(0, mine), lanes[part])
        value = own[at]
        hx[0, 0:mine, lanes[part]], lx[0, 0:mine, lanes[part]] = split(value)
        waits[part] = [
            copy(ref.at[0, pl.ds(0, mine), lanes[part]], ref.at[0, pl.ds(mine, mine), lanes[part]], other)
            for ref in (hx, lx)
        ]
        squares = squares + jnp.sum(
            jnp.sum(value * value, axis=0, keepdims=True), axis=1, keepdims=True
        )
    square[0] = jnp.broadcast_to(squares, square.shape[1:])
    waits.append([copy(square.at[0], square.at[1], other)])
    held = ring.copies + counts
    plain = [made for made in started if all(made is not one for one in held)]

    def sent(step, b, c, ref):
        if step == NS_STEPS - 1:
            cols = pl.ds(pl.multiple_of(c * tile, tile), tile)
            src, dst = own.at[:, cols], rot_ref.at[pl.ds(here, mine), cols]
        else:
            cols = pl.ds(pl.multiple_of(c * tile, tile), tile)
            src = ref.at[(step + 1) % 2, pl.ds(0, mine), cols]
            dst = ref.at[(step + 1) % 2, pl.ds(mine, mine), cols]
        return pltpu.make_async_remote_copy(
            src_ref=src, dst_ref=dst, send_sem=tile_send.at[step, b, c],
            recv_sem=tile_recv.at[step, b, c], device_id=other, device_id_type=MESH,
        )

    both = ((1,), (1,))
    keep, turned = 1.5, 0.5
    for step in range(NS_STEPS):
        now, later = step % 2, (step + 1) % 2

        def inner(j):
            rows = pl.ds(pl.multiple_of(j * tile, tile), tile)
            hi, lo = hx[now, 0:mine, :], lx[now, 0:mine, :]
            there_hi = hx[now, rows, :]
            value = dot(hi, there_hi, both) + (
                dot(hi, lx[now, rows, :], both) + dot(lo, there_hi, both)
            )
            top[:, rows], low[:, rows] = split(value)

        pl.loop(0, tiles // 2)(inner)
        if step == 0:
            for row in waits:
                for made in row:
                    made.wait_recv()
            for made in plain:
                made.wait_send()
            total = square[0, 0:1, 0:1] + square[1, 0:1, 0:1]
            inverse = 1.0 / (3.0 * jnp.sqrt(total / features + epsilon))
            keep, turned = 1.5 * inverse, 0.5 * inverse * inverse * inverse
        else:
            keep, turned = 1.5, 0.5
            for c in range(tiles):
                for b, ref in enumerate((hx, lx)):
                    sent(step - 1, b, c, ref).wait()
        pl.loop(tiles // 2, tiles)(inner)
        if step == 1:
            ring.last()

        @pl.loop(0, tiles)
        def _(c):
            cols = pl.ds(pl.multiple_of(c * tile, tile), tile)
            hi = hx[now, :, cols]
            turn = dot(top[...], hi) + (dot(top[...], lx[now, :, cols]) + dot(low[...], hi))
            value = keep * own[:, cols] - turned * turn
            own[:, cols] = value
            if step == NS_STEPS - 1:
                rot_ref[pl.ds(here, mine), cols] = value
                sent(step, 0, c, None).start()
            else:
                hx[later, 0:mine, cols], lx[later, 0:mine, cols] = split(value)
                for b, ref in enumerate((hx, lx)):
                    sent(step, b, c, ref).start()

    for c in range(tiles):
        sent(NS_STEPS - 1, 0, c, None).wait()
    ring.finish()
    for made in counts:
        made.wait_recv()
    for made in ring.copies + counts:
        made.wait_send()
    for made in stays:
        made.wait()


def settle(part, sums, count):
    features = part.shape[0]
    panel_ways = 2 * WAYS
    mine = features // 2
    sizes = [mine // WAYS**n for n in (1, 2, 3)]
    copies = 3 + 2 * 3 * 3 * (WAYS - 1) + 2 * 3 + 1 + RING + panel_ways - 1
    return pl.pallas_call(
        settle_kernel,
        in_specs=vmem(3),
        out_specs=vmem(1) + [pl.BlockSpec(memory_space=pltpu.HBM)] * 2,
        out_shape=[
            jax.ShapeDtypeStruct(part.shape, F32),
            jax.ShapeDtypeStruct((panel_ways * sums.shape[0], features), F32),
            jax.ShapeDtypeStruct((panel_ways, *count.shape), F32),
        ],
        scratch_shapes=[pltpu.VMEM((mine, features), F32)]
        + [pltpu.VMEM((WAYS - 1, size, features), F32) for size in sizes]
        + [pltpu.VMEM((mine, features), F32)] * 2
        + [pltpu.VMEM((2, features, features), BF16)] * 2
        + [pltpu.VMEM((mine, features), BF16)] * 2
        + [pltpu.VMEM((2, 8, 128), F32)]
        + [pltpu.SemaphoreType.DMA((copies,))] * 2
        + [pltpu.SemaphoreType.DMA((NS_STEPS, 2, features // 256))] * 2
        + [pltpu.SemaphoreType.DMA((2,))],
        compiler_params=pltpu.CompilerParams(
            collective_id=1, has_side_effects=True, vmem_limit_bytes=26 << 20
        ),
        name="settle",
    )(part, sums, count)


def turn_kernel(sums_ref, count_ref, old_ref, rot_ref, new_ref, same_ref, top, low):
    step = pl.program_id(0)

    @pl.when(step == 0)
    def _():
        top[...], low[...] = split(rot_ref[...])

    rows = same_ref.shape[0]
    same_ref[...] = rot_ref[pl.ds(pl.multiple_of(step * rows, rows), rows), :]
    hi, lo = split(sums_ref[...])
    turned = dot(hi, top[...]) + (dot(hi, low[...]) + dot(lo, top[...]))
    panels, _, rows = count_ref.shape
    unit = jnp.where(iota((8, 128), 0) == 0, 1.0, 0.0)
    for n in range(panels):
        here = slice(n * rows, (n + 1) * rows)
        count = lax.dot_general(
            count_ref[n], unit, (((0,), (0,)), ((), ())),
            precision=lax.Precision.HIGHEST, preferred_element_type=F32,
        )
        new_ref[here, :] = (
            (turned[here, :] + old_ref[here, :].astype(F32)) / (count[:, 0:1] + 1.0)
        ).astype(BF16)


def turn(sums, count, old, rot):
    total, features = sums.shape
    steps = 4
    rows = total // steps
    return pl.pallas_call(
        turn_kernel,
        grid=(steps,),
        in_specs=[
            pl.BlockSpec((rows, features), lambda i: (i, 0)),
            pl.BlockSpec((count.shape[0] // steps, *count.shape[1:]), lambda i: (i, 0, 0)),
            pl.BlockSpec((rows, features), lambda i: (i, 0)),
            pl.BlockSpec(memory_space=pltpu.VMEM),
        ],
        out_specs=[
            pl.BlockSpec((rows, features), lambda i: (i, 0)),
            pl.BlockSpec((features // steps, features), lambda i: (i, 0)),
        ],
        out_shape=[
            jax.ShapeDtypeStruct((total, features), BF16),
            jax.ShapeDtypeStruct(rot.shape, F32),
        ],
        scratch_shapes=[pltpu.VMEM(rot.shape, BF16)] * 2,
        compiler_params=pltpu.CompilerParams(vmem_limit_bytes=28 << 20),
        name="turn",
    )(sums, count, old, rot)


def dense(points, labels, centroids):
    data_ways = lax.axis_size("dp")
    panel_ways = lax.axis_size("cent")
    block_rows = centroids.shape[0]
    features = points.shape[1]
    column = lax.axis_index("cent")
    owner_block = labels // block_rows
    inside = owner_block % panel_ways == column
    slot_index = jnp.where(
        inside, owner_block // panel_ways * block_rows + labels % block_rows, data_ways * block_rows
    )
    vectors = points.astype(F32)
    local_sums = jax.ops.segment_sum(vectors, slot_index, num_segments=data_ways * block_rows)
    local_counts = jax.ops.segment_sum(
        jnp.ones(labels.shape, F32), slot_index, num_segments=data_ways * block_rows
    )
    label_sums, label_counts = (
        lax.psum_scatter(local_sums, "dp", scatter_dimension=0, tiled=True),
        lax.psum_scatter(local_counts, "dp", scatter_dimension=0, tiled=True),
    )
    old_rows = centroids.astype(F32)
    cross_cov = lax.psum(
        lax.dot_general(
            label_sums, old_rows, (((0,), (0,)), ((), ())), precision=lax.Precision.HIGHEST
        ),
        ("dp", "cent"),
    )
    scale_root = jnp.sqrt(jnp.sum(cross_cov * cross_cov) / features + epsilon)
    rotation = cross_cov / (3.0 * scale_root)
    for iteration in range(NS_STEPS):
        inner_prod = jnp.dot(rotation, rotation.T, precision=lax.Precision.HIGHEST)
        rotation = 1.5 * rotation - 0.5 * jnp.dot(
            inner_prod, rotation, precision=lax.Precision.HIGHEST
        )
    rotated_sums = jnp.dot(label_sums, rotation, precision=lax.Precision.HIGHEST)
    moved_rows = lax.all_gather(rotated_sums + old_rows, "cent", axis=0, tiled=True)
    all_counts = lax.all_gather(label_counts, "cent", axis=0, tiled=True)
    return ((moved_rows / (all_counts[:, None] + 1.0)).astype(BF16), rotation)


def local(points, labels, centroids):
    sums, count, part, old = exchange(labels, points, centroids)
    rotation, sums, count = settle(part, sums, count)
    bad = jnp.logical_not(jnp.isfinite(rotation[0, 0]))
    new_centroids, rotation = turn(sums, count, old, rotation)
    _, new_centroids, rotation = lax.while_loop(
        lambda state: state[0],
        lambda state: (jnp.array(False), *dense(points, labels, centroids)),
        (bad, new_centroids, rotation),
    )
    return new_centroids, rotation


def solution(mesh):
    return jax.shard_map(
        local,
        mesh=mesh,
        in_specs=(P("dp", None), P("dp"), P(("dp", "cent"), None)),
        out_specs=(P("dp", None), P()),
        check_vma=False,
    )
```

```python
import functools

import jax
import jax.numpy as jnp
from jax import lax
from jax.experimental import pallas as pl
from jax.experimental.pallas import tpu as pltpu
from jax.sharding import PartitionSpec as P

MESH = pl.DeviceIdType.MESH
F32 = jnp.float32
BF16 = jnp.bfloat16

NS_STEPS = 3
epsilon = 1e-06

CHUNK = 512
KEEP = 128
CAP = 112
SLOT = 128
WAYS = 4
LANES = ((0, 384), (384, 384), (768, 256))


def dot(a, b, dims=((1,), (0,))):
    return lax.dot_general(a, b, (dims, ((), ())), preferred_element_type=F32)


def split(x):
    hi = x.astype(BF16)
    return hi, (x - hi.astype(F32)).astype(BF16)


def iota(shape, axis):
    return lax.broadcasted_iota(jnp.int32, shape, axis)


def place():
    dp, cent = lax.axis_index("dp"), lax.axis_index("cent")
    x, y, z = cent // 2, cent % 2 * 2 + dp // 8, dp // 2 % 4
    return (x, y, z), dp % 2


def device(xyz, core):
    x, y, z = xyz
    return {"dp": (y % 2 * 4 + z) * 2 + core, "cent": x * 2 + y // 2}


def moved(xyz, axis, by):
    return tuple((c + by) % WAYS if a == axis else c for a, c in enumerate(xyz))


class Ring:
    def __init__(self, copy, xyz, core, fresh, all_ref, lanes):
        self.copy, self.xyz, self.core = copy, xyz, core
        self.fresh, self.all_ref, self.lanes = fresh, all_ref, lanes
        self.right, self.left = moved(xyz, 0, 1), moved(xyz, 0, WAYS - 1)
        self.across = moved(xyz, 1, 2)

    def spot(self, owner, part):
        half = self.all_ref.shape[0] // (4 * WAYS)
        start = ((owner[0] * 2 + owner[1] // 2) * 2 + part) * half
        return self.all_ref.at[pl.ds(pl.multiple_of(start, half), half), self.lanes]

    def send(self, owner, part, to, fresh=False):
        spot = self.spot(owner, part)
        half = spot.shape[0]
        own = self.fresh.at[pl.ds(part * half, half), self.lanes]
        return self.copy(own if fresh else spot, spot, device(to, self.core))

    def begin(self):
        me = self.xyz
        self.over = [self.send(me, 0, self.across, True)]
        self.rights = [self.send(me, 0, self.right, True)]
        self.lefts = [None, self.send(me, 1, self.left, True)]
        self.over.append(self.send(me, 1, self.across, True))
        self.rights.append(self.send(me, 1, self.right, True))
        self.lefts[0] = self.send(me, 0, self.left, True)

    def forward(self):
        self.rights[0].wait_recv()
        self.ends = [self.send(self.left, 0, self.right)]
        self.lefts[1].wait_recv()
        self.ends.append(self.send(self.right, 1, self.left))
        self.over[0].wait_recv()
        self.rights2 = [self.send(self.across, 0, self.right)]
        self.lefts2 = [self.send(self.across, 0, self.left)]
        self.over[1].wait_recv()
        self.lefts2.append(self.send(self.across, 1, self.left))
        self.rights2.append(self.send(self.across, 1, self.right))

    def last(self):
        self.rights2[0].wait_recv()
        self.ends.append(self.send(moved(self.left, 1, 2), 0, self.right))
        self.lefts2[1].wait_recv()
        self.ends.append(self.send(moved(self.right, 1, 2), 1, self.left))

    def finish(self):
        for made in [self.rights[1], self.lefts[0], self.rights2[1], self.lefts2[0]] + self.ends:
            made.wait_recv()


RING = 14
RINGS = 2


def exchange_kernel(
    block_rows, lab_ref, pts_ref, cents_ref, sums_ref, count_ref, cov_ref,
    pts, tri, hits, rank, meta, kept, metas, out, got, out_id, got_id, load, send, recv,
):
    dp, panel = lax.axis_index("dp"), lax.axis_index("cent")
    data_ways, panel_ways = lax.axis_size("dp"), lax.axis_size("cent")
    steps = lab_ref.shape[0]
    yl, z, core = dp // 8, dp // 2 % 4, dp % 2

    def at(dy, dz, dc):
        return {"dp": ((yl + dy) % 2 * 4 + (z + dz) % 4) * 2 + (core + dc) % 2}

    loads = []
    for step in range(steps):
        loads.append(
            pltpu.make_async_copy(
                pts_ref.at[pl.ds(step * CHUNK, CHUNK)], pts.at[step], load.at[step]
            )
        )
        loads[-1].start()
    barrier = pltpu.get_barrier_semaphore()
    for dy in range(2):
        for dz in range(4):
            for dc in range(2):
                if dy or dz or dc:
                    pl.semaphore_signal(
                        barrier, inc=1, device_id=at(dy, dz, dc), device_id_type=MESH
                    )

    tri[...] = jnp.where(
        iota((CHUNK, CHUNK), 0) <= iota((CHUNK, CHUNK), 1), 1.0, 0.0
    ).astype(BF16)
    for step in range(steps):
        block = lab_ref[step] // block_rows
        dest = block // panel_ways
        hits[step * data_ways : (step + 1) * data_ways, :] = jnp.where(
            jnp.logical_and(
                iota((data_ways, CHUNK), 0) == dest, block % panel_ways == panel
            ),
            1.0,
            0.0,
        )
    counts = dot(hits[...].astype(BF16), tri[...])
    carry = jnp.zeros((data_ways, 1), F32)
    most = jnp.zeros((1, 1), F32)
    row = iota((16, CHUNK), 0)
    for step in range(steps):
        hit = hits[step * data_ways : (step + 1) * data_ways, :]
        count = counts[step * data_ways : (step + 1) * data_ways, :]
        order = jnp.sum(
            hit * jnp.sum(count, axis=0, keepdims=True), axis=0, keepdims=True
        )
        rank[step] = order.astype(jnp.int32)
        spot = jnp.sum(hit * (count + carry), axis=0, keepdims=True)
        last = count[:, CHUNK - 1 : CHUNK]
        carry = carry + last
        most = jnp.maximum(most, jnp.sum(last, axis=0, keepdims=True))
        lab = lab_ref[step]
        dest = (lab // block_rows // panel_ways).astype(F32)
        slot = (lab % block_rows + 1).astype(F32)
        meta[step] = jnp.where(
            row == 0,
            dest,
            jnp.where(row == 1, jnp.minimum(spot, 255.0), jnp.where(row == 2, slot, 0.0)),
        ).astype(BF16)
    over = jnp.logical_or(most > KEEP, jnp.max(carry, axis=0, keepdims=True) > CAP)
    bad = jnp.where(over, jnp.inf, 0.0)

    used = [0]
    started = []

    def copy(src, dst, to):
        n = used[0]
        used[0] += 1
        made = pltpu.make_async_remote_copy(
            src_ref=src, dst_ref=dst, send_sem=send.at[n], recv_sem=recv.at[n],
            device_id=to, device_id_type=MESH,
        )
        made.start()
        started.append(made)
        return made

    for step in range(steps):
        pick = jnp.where(iota((KEEP, CHUNK), 0) + 1 == rank[step], 1.0, 0.0).astype(BF16)
        metas[:, step * KEEP : (step + 1) * KEEP] = dot(
            meta[step], pick, ((1,), (1,))
        ).astype(BF16)
        loads[step].wait()
        kept[step * KEEP : (step + 1) * KEEP, :] = dot(pick, pts[step]).astype(BF16)

    pl.semaphore_wait(barrier, data_ways - 1)
    places = metas[...]
    whole = places.astype(F32).astype(jnp.int32)
    dests, spots = whole[0:1, :], whole[1:2, :]
    total = places.shape[1]
    arrive = {}
    order = [(1, 2), (0, 2), (1, 1), (0, 3), (1, 3), (0, 1), (1, 0), (0, 0)]
    for dy, dz in order:
        wanted = jnp.concatenate(
            [
                jnp.broadcast_to(
                    jnp.where(dests == at(dy, dz, dc)["dp"], spots, 0), (SLOT, total)
                )
                for dc in range(2)
            ],
            axis=0,
        )
        pick = jnp.where(iota((2 * SLOT, total), 0) % SLOT + 1 == wanted, 1.0, 0.0).astype(BF16)
        rows = dot(pick, kept[...]).astype(BF16)
        ids = dot(places, pick, ((1,), (1,))).astype(BF16)
        for dc in range(2):
            k = (dy * 4 + dz) * 2 + dc
            out[k] = rows[dc * SLOT : (dc + 1) * SLOT, :]
            out_id[k] = ids[:, dc * SLOT : (dc + 1) * SLOT]
            if k:
                to = at(dy, dz, dc)
                arrive[k] = [
                    copy(out_id.at[k], got_id.at[k], to),
                    copy(out.at[k, pl.ds(0, CAP)], got.at[k, pl.ds(0, CAP)], to),
                ]

    rows, features = sums_ref.shape
    got[:, CAP:SLOT, :] = jnp.zeros((data_ways, SLOT - CAP, features), BF16)
    ones = jnp.ones((8, SLOT), BF16)
    across = ((1,), (1,))
    for dy, dz in order[::-1]:
        for dc in range(2):
            k = (dy * 4 + dz) * 2 + dc
            for made in arrive.get(k, ()):
                made.wait_recv()
            ids = (got_id if k else out_id)[k].astype(F32).astype(jnp.int32)
            pick = jnp.where(iota((rows, SLOT), 0) + 1 == ids[2:3, :], 1.0, 0.0).astype(BF16)
            vectors = (got if k else out)[k]
            if k:
                sums_ref[...] += dot(pick, vectors)
                count_ref[...] += dot(ones, pick, across)
            else:
                sums_ref[...] = dot(pick, vectors)
                count_ref[...] = dot(ones, pick, across)
    hi, lo = split(sums_ref[...])
    cents = cents_ref[...]
    first = ((0,), (0,))
    cov_ref[...] = dot(hi, cents, first) + dot(lo, cents, first)
    cov_ref[0:8, 0:128] = cov_ref[0:8, 0:128] + bad
    for made in started:
        made.wait_send()


def vmem(n):
    return [pl.BlockSpec(memory_space=pltpu.VMEM)] * n


def exchange(labels, points, cents):
    data_ways = lax.axis_size("dp")
    rows, features = cents.shape
    steps = points.shape[0] // CHUNK
    copies = 2 * (data_ways - 1)
    return pl.pallas_call(
        functools.partial(exchange_kernel, rows),
        in_specs=vmem(1) + [pl.BlockSpec(memory_space=pl.ANY)] + vmem(1),
        out_specs=vmem(3),
        out_shape=[
            jax.ShapeDtypeStruct((rows, features), F32),
            jax.ShapeDtypeStruct((8, rows), F32),
            jax.ShapeDtypeStruct((features, features), F32),
        ],
        scratch_shapes=[
            pltpu.VMEM((steps, CHUNK, features), BF16),
            pltpu.VMEM((CHUNK, CHUNK), BF16),
            pltpu.VMEM((steps * data_ways, CHUNK), F32),
            pltpu.VMEM((steps, 1, CHUNK), jnp.int32),
            pltpu.VMEM((steps, 16, CHUNK), BF16),
            pltpu.VMEM((steps * KEEP, features), BF16),
            pltpu.VMEM((16, steps * KEEP), BF16),
            pltpu.VMEM((data_ways, SLOT, features), BF16),
            pltpu.VMEM((data_ways, SLOT, features), BF16),
            pltpu.VMEM((data_ways, 16, SLOT), BF16),
            pltpu.VMEM((data_ways, 16, SLOT), BF16),
            pltpu.SemaphoreType.DMA((steps,)),
            pltpu.SemaphoreType.DMA((copies,)),
            pltpu.SemaphoreType.DMA((copies,)),
        ],
        compiler_params=pltpu.CompilerParams(
            collective_id=0, has_side_effects=True, vmem_limit_bytes=40 << 20
        ),
        name="exchange",
    )(labels.reshape(steps, 1, CHUNK), points, cents)


def settle_kernel(
    part_ref, sums_ref, count_ref, cents_ref, rot_ref, new_ref, half, got1, got2, got3, acc, own, hx, lx, top, low, square,
    sum_hi, sum_lo, counts, fresh, send, recv, tile_send, tile_recv,
):
    xyz, core = place()
    panel = lax.axis_index("cent")
    features = part_ref.shape[1]
    mine = features // 2
    tile = 256
    tiles = features // tile
    barrier = pltpu.get_barrier_semaphore()
    other = device(xyz, 1 - core)
    partners = [other] + [
        device(moved(xyz, axis, by), core) for axis in range(3) for by in range(1, WAYS)
    ]
    for partner in partners:
        pl.semaphore_signal(barrier, inc=1, device_id=partner, device_id_type=MESH)
    pl.semaphore_wait(barrier, len(partners))

    used = [0]
    started = []

    def remote(src, dst, s, r, to):
        made = pltpu.make_async_remote_copy(
            src_ref=src, dst_ref=dst, send_sem=s, recv_sem=r, device_id=to, device_id_type=MESH
        )
        started.append(made)
        return made

    def copy(src, dst, to):
        n = used[0]
        used[0] += 1
        made = remote(src, dst, send.at[n], recv.at[n], to)
        made.start()
        return made

    here = pl.multiple_of(core * mine, mine)
    there = pl.multiple_of((1 - core) * mine, mine)
    parts = range(len(LANES))
    lanes = [pl.ds(lane, width) for lane, width in LANES]
    sizes = [mine // WAYS ** (stage + 1) for stage in range(3)]
    gots = (got1, got2, got3)
    base = [0, 0, 0]
    waits = [
        [copy(part_ref.at[pl.ds(there, mine), lanes[part]], half.at[:, lanes[part]], other)]
        for part in parts
    ]

    def scatter(stage, part):
        size, axis = sizes[stage], (part + stage) % 3
        made = []
        for by in range(1, WAYS):
            to = moved(xyz, axis, by)
            start = pl.multiple_of(base[part] + to[axis] * size, size)
            made.append(
                copy(
                    acc.at[pl.ds(start, size), lanes[part]],
                    gots[stage].at[by - 1, :, lanes[part]],
                    device(to, core),
                )
            )
        return made

    def spread(stage, part):
        size, axis = sizes[stage], (part + stage) % 3
        span = own.at[pl.ds(pl.multiple_of(base[part], size), size), lanes[part]]
        made = [copy(span, span, device(moved(xyz, axis, by), core)) for by in range(1, WAYS)]
        base[part] = base[part] - xyz[axis] * size
        return made

    def arrived(part):
        for made in waits[part]:
            made.wait_recv()

    for part in parts:
        arrived(part)
        acc[:, lanes[part]] = part_ref[pl.ds(here, mine), lanes[part]] + half[:, lanes[part]]
        waits[part] = scatter(0, part)

    sum_hi[...], sum_lo[...] = split(sums_ref[...])
    unit = jnp.where(iota((8, 128), 0) == 0, 1.0, 0.0)
    counts[...] = lax.dot_general(
        count_ref[...], unit, (((0,), (0,)), ((), ())),
        precision=lax.Precision.HIGHEST, preferred_element_type=F32,
    )

    for stage in range(3):
        size = sizes[stage]
        for part in parts:
            arrived(part)
            base[part] = pl.multiple_of(base[part] + xyz[(part + stage) % 3] * size, size)
            at = (pl.ds(base[part], size), lanes[part])
            total = acc[at]
            for by in range(1, WAYS):
                total = total + gots[stage][by - 1, :, lanes[part]]
            if stage < 2:
                acc[at] = total
                waits[part] = scatter(stage + 1, part)
            else:
                own[at] = total
                waits[part] = spread(2, part)
    for stage in (1, 0):
        for part in parts:
            arrived(part)
            waits[part] = spread(stage, part)
    squares = jnp.zeros((1, 1), F32)
    for part in parts:
        arrived(part)
        at = (slice(0, mine), lanes[part])
        value = own[at]
        hx[0, 0:mine, lanes[part]], lx[0, 0:mine, lanes[part]] = split(value)
        waits[part] = [
            copy(ref.at[0, pl.ds(0, mine), lanes[part]], ref.at[0, pl.ds(mine, mine), lanes[part]], other)
            for ref in (hx, lx)
        ]
        squares = squares + jnp.sum(
            jnp.sum(value * value, axis=0, keepdims=True), axis=1, keepdims=True
        )
    square[0] = jnp.broadcast_to(squares, square.shape[1:])
    waits.append([copy(square.at[0], square.at[1], other)])

    def sent(step, b, c, ref):
        if step == NS_STEPS - 1:
            cols = pl.ds(pl.multiple_of(c * tile, tile), tile)
            src, dst = own.at[:, cols], rot_ref.at[pl.ds(here, mine), cols]
        else:
            cols = pl.ds(pl.multiple_of(c * tile, tile), tile)
            src = ref.at[(step + 1) % 2, pl.ds(0, mine), cols]
            dst = ref.at[(step + 1) % 2, pl.ds(mine, mine), cols]
        return pltpu.make_async_remote_copy(
            src_ref=src, dst_ref=dst, send_sem=tile_send.at[step, b, c],
            recv_sem=tile_recv.at[step, b, c], device_id=other, device_id_type=MESH,
        )

    both = ((1,), (1,))
    keep, turned = 1.5, 0.5
    for step in range(NS_STEPS):
        now, later = step % 2, (step + 1) % 2

        def inner(j):
            rows = pl.ds(pl.multiple_of(j * tile, tile), tile)
            hi, lo = hx[now, 0:mine, :], lx[now, 0:mine, :]
            there_hi = hx[now, rows, :]
            value = dot(hi, there_hi, both) + (
                dot(hi, lx[now, rows, :], both) + dot(lo, there_hi, both)
            )
            top[:, rows], low[:, rows] = split(value)

        pl.loop(0, tiles // 2)(inner)
        if step == 0:
            for row in waits:
                for made in row:
                    made.wait_recv()
            for made in started:
                made.wait_send()
            total = square[0, 0:1, 0:1] + square[1, 0:1, 0:1]
            inverse = 1.0 / (3.0 * jnp.sqrt(total / features + epsilon))
            keep, turned = 1.5 * inverse, 0.5 * inverse * inverse * inverse
        else:
            keep, turned = 1.5, 0.5
            for c in range(tiles):
                for b, ref in enumerate((hx, lx)):
                    sent(step - 1, b, c, ref).wait()
        pl.loop(tiles // 2, tiles)(inner)

        def update(c):
            cols = pl.ds(pl.multiple_of(c * tile, tile), tile)
            hi = hx[now, :, cols]
            turn = dot(top[...], hi) + (dot(top[...], lx[now, :, cols]) + dot(low[...], hi))
            value = keep * own[:, cols] - turned * turn
            own[:, cols] = value
            if step == NS_STEPS - 1:
                rot_ref[pl.ds(here, mine), cols] = value
                sent(step, 0, c, None).start()
            else:
                hx[later, 0:mine, cols], lx[later, 0:mine, cols] = split(value)
                for b, ref in enumerate((hx, lx)):
                    sent(step, b, c, ref).start()

        if step < NS_STEPS - 1:
            pl.loop(0, tiles)(update)

    begun = len(started)
    rings = []
    span = features // RINGS
    per = tiles // RINGS
    for c in range(tiles + 1):
        if c < tiles:
            update(c)
        if c and c % per == 0:
            for done in range(c - per, c):
                sent(NS_STEPS - 1, 0, done, None).wait()
            cols = slice((c - per) * tile, c * tile)
            rot_hi, rot_lo = split(rot_ref[:, cols])
            moved_rows = dot(sum_hi[...], rot_hi) + (
                dot(sum_hi[...], rot_lo) + dot(sum_lo[...], rot_hi)
            )
            value = (
                (moved_rows + cents_ref[:, cols].astype(F32)) / (counts[:, 0:1] + 1.0)
            ).astype(BF16)
            fresh[:, cols] = value
            ring = Ring(copy, xyz, core, fresh, new_ref, pl.ds((c - per) * tile, span))
            ring.begin()
            rings.append(ring)
    rows = fresh.shape[0]
    new_ref[pl.ds(pl.multiple_of(lax.axis_index("cent") * rows, rows), rows), :] = fresh[...]
    for ring in rings:
        ring.forward()
    for ring in rings:
        ring.last()
    for ring in rings:
        ring.finish()
    for made in started[begun:]:
        made.wait_send()


def settle(part, sums, count, cents):
    features = part.shape[0]
    panel_ways = 2 * WAYS
    mine = features // 2
    sizes = [mine // WAYS**n for n in (1, 2, 3)]
    copies = 3 + 2 * 3 * 3 * (WAYS - 1) + 2 * 3 + 1 + RING * RINGS
    return pl.pallas_call(
        settle_kernel,
        in_specs=vmem(4),
        out_specs=vmem(2),
        out_shape=[
            jax.ShapeDtypeStruct(part.shape, F32),
            jax.ShapeDtypeStruct((panel_ways * sums.shape[0], features), BF16),
        ],
        scratch_shapes=[pltpu.VMEM((mine, features), F32)]
        + [pltpu.VMEM((WAYS - 1, size, features), F32) for size in sizes]
        + [pltpu.VMEM((mine, features), F32)] * 2
        + [pltpu.VMEM((2, features, features), BF16)] * 2
        + [pltpu.VMEM((mine, features), BF16)] * 2
        + [pltpu.VMEM((2, 8, 128), F32)]
        + [pltpu.VMEM(cents.shape, BF16)] * 2
        + [pltpu.VMEM((cents.shape[0], 128), F32), pltpu.VMEM(cents.shape, BF16)]
        + [pltpu.SemaphoreType.DMA((copies,))] * 2
        + [pltpu.SemaphoreType.DMA((NS_STEPS, 2, features // 256))] * 2,
        compiler_params=pltpu.CompilerParams(
            collective_id=1, has_side_effects=True, vmem_limit_bytes=28 << 20
        ),
        name="settle",
    )(part, sums, count, cents)


def emit_kernel(new_ref, rot_ref, new_out, rot_out, done):
    copies = [
        pltpu.make_async_copy(src, dst, done.at[n])
        for n, (src, dst) in enumerate(((new_ref, new_out), (rot_ref, rot_out)))
    ]
    for made in copies:
        made.start()
    for made in copies:
        made.wait()


def emit(new, rot):
    return pl.pallas_call(
        emit_kernel,
        in_specs=vmem(2),
        out_specs=[pl.BlockSpec(memory_space=pltpu.HBM)] * 2,
        out_shape=[
            jax.ShapeDtypeStruct(new.shape, new.dtype),
            jax.ShapeDtypeStruct(rot.shape, rot.dtype),
        ],
        scratch_shapes=[pltpu.SemaphoreType.DMA((2,))],
        compiler_params=pltpu.CompilerParams(vmem_limit_bytes=16 << 20),
        name="emit",
    )(new, rot)


def dense(points, labels, centroids):
    data_ways = lax.axis_size("dp")
    panel_ways = lax.axis_size("cent")
    block_rows = centroids.shape[0]
    features = points.shape[1]
    column = lax.axis_index("cent")
    owner_block = labels // block_rows
    inside = owner_block % panel_ways == column
    slot_index = jnp.where(
        inside, owner_block // panel_ways * block_rows + labels % block_rows, data_ways * block_rows
    )
    vectors = points.astype(F32)
    local_sums = jax.ops.segment_sum(vectors, slot_index, num_segments=data_ways * block_rows)
    local_counts = jax.ops.segment_sum(
        jnp.ones(labels.shape, F32), slot_index, num_segments=data_ways * block_rows
    )
    label_sums, label_counts = (
        lax.psum_scatter(local_sums, "dp", scatter_dimension=0, tiled=True),
        lax.psum_scatter(local_counts, "dp", scatter_dimension=0, tiled=True),
    )
    old_rows = centroids.astype(F32)
    cross_cov = lax.psum(
        lax.dot_general(
            label_sums, old_rows, (((0,), (0,)), ((), ())), precision=lax.Precision.HIGHEST
        ),
        ("dp", "cent"),
    )
    scale_root = jnp.sqrt(jnp.sum(cross_cov * cross_cov) / features + epsilon)
    rotation = cross_cov / (3.0 * scale_root)
    for iteration in range(NS_STEPS):
        inner_prod = jnp.dot(rotation, rotation.T, precision=lax.Precision.HIGHEST)
        rotation = 1.5 * rotation - 0.5 * jnp.dot(
            inner_prod, rotation, precision=lax.Precision.HIGHEST
        )
    rotated_sums = jnp.dot(label_sums, rotation, precision=lax.Precision.HIGHEST)
    moved_rows = lax.all_gather(rotated_sums + old_rows, "cent", axis=0, tiled=True)
    all_counts = lax.all_gather(label_counts, "cent", axis=0, tiled=True)
    return ((moved_rows / (all_counts[:, None] + 1.0)).astype(BF16), rotation)


def local(points, labels, centroids):
    sums, count, part = exchange(labels, points, centroids)
    rotation, new_centroids = settle(part, sums, count, centroids)
    bad = jnp.logical_not(jnp.isfinite(rotation[0, 0]))
    new_centroids, rotation = emit(new_centroids, rotation)
    _, new_centroids, rotation = lax.while_loop(
        lambda state: state[0],
        lambda state: (jnp.array(False), *dense(points, labels, centroids)),
        (bad, new_centroids, rotation),
    )
    return new_centroids, rotation


def solution(mesh):
    return jax.shard_map(
        local,
        mesh=mesh,
        in_specs=(P("dp", None), P("dp"), P(("dp", "cent"), None)),
        out_specs=(P("dp", None), P()),
        check_vma=False,
    )
```

```python
import functools

import jax
import jax.numpy as jnp
from jax import lax
from jax.experimental import pallas as pl
from jax.experimental.pallas import tpu as pltpu
from jax.sharding import PartitionSpec as P

MESH = pl.DeviceIdType.MESH
F32 = jnp.float32
BF16 = jnp.bfloat16

NS_STEPS = 3
epsilon = 1e-06

CHUNK = 512
KEEP = 128
CAP = 112
SLOT = 128
WAYS = 4
LANES = ((0, 384), (384, 384), (768, 256))


def dot(a, b, dims=((1,), (0,))):
    return lax.dot_general(a, b, (dims, ((), ())), preferred_element_type=F32)


def split(x):
    hi = x.astype(BF16)
    return hi, (x - hi.astype(F32)).astype(BF16)


def iota(shape, axis):
    return lax.broadcasted_iota(jnp.int32, shape, axis)


def place():
    dp, cent = lax.axis_index("dp"), lax.axis_index("cent")
    x, y, z = cent // 2, cent % 2 * 2 + dp // 8, dp // 2 % 4
    return (x, y, z), dp % 2


def device(xyz, core):
    x, y, z = xyz
    return {"dp": (y % 2 * 4 + z) * 2 + core, "cent": x * 2 + y // 2}


def moved(xyz, axis, by):
    return tuple((c + by) % WAYS if a == axis else c for a, c in enumerate(xyz))


class Ring:
    def __init__(self, copy, xyz, core, fresh, all_ref, lanes):
        self.copy, self.xyz, self.core = copy, xyz, core
        self.fresh, self.all_ref, self.lanes = fresh, all_ref, lanes
        self.right, self.left = moved(xyz, 0, 1), moved(xyz, 0, WAYS - 1)
        self.across = moved(xyz, 1, 2)

    def spot(self, owner, part):
        half = self.all_ref.shape[0] // (4 * WAYS)
        start = ((owner[0] * 2 + owner[1] // 2) * 2 + part) * half
        return self.all_ref.at[pl.ds(pl.multiple_of(start, half), half), self.lanes]

    def send(self, owner, part, to, fresh=False):
        spot = self.spot(owner, part)
        half = spot.shape[0]
        own = self.fresh.at[pl.ds(part * half, half), self.lanes]
        return self.copy(own if fresh else spot, spot, device(to, self.core))

    def begin(self):
        me = self.xyz
        self.over = [self.send(me, 0, self.across, True)]
        self.rights = [self.send(me, 0, self.right, True)]
        self.lefts = [None, self.send(me, 1, self.left, True)]
        self.over.append(self.send(me, 1, self.across, True))
        self.rights.append(self.send(me, 1, self.right, True))
        self.lefts[0] = self.send(me, 0, self.left, True)

    def forward(self):
        self.rights[0].wait_recv()
        self.overs = []
        self.ends = [self.send(self.left, 0, self.right)]
        self.lefts[1].wait_recv()
        self.ends.append(self.send(self.right, 1, self.left))
        self.over[0].wait_recv()
        self.rights2 = [self.send(self.across, 0, self.right)]
        self.lefts2 = [self.send(self.across, 0, self.left)]
        self.over[1].wait_recv()
        self.lefts2.append(self.send(self.across, 1, self.left))
        self.rights2.append(self.send(self.across, 1, self.right))

    def last(self):
        opposite = moved(self.xyz, 0, 2)
        for part in range(2):
            self.ends[part].wait_recv()
            self.overs.append(self.send(opposite, part, self.across))

    def finish(self):
        late = [self.rights[1], self.lefts[0]] + self.rights2 + self.lefts2 + self.overs
        for made in late:
            made.wait_recv()


RING = 14
RINGS = 2


def exchange_kernel(
    block_rows, lab_ref, pts_ref, cents_ref, sums_ref, count_ref, cov_ref,
    pts, tri, hits, rank, meta, kept, metas, out, got, out_id, got_id, load, send, recv,
):
    dp, panel = lax.axis_index("dp"), lax.axis_index("cent")
    data_ways, panel_ways = lax.axis_size("dp"), lax.axis_size("cent")
    steps = lab_ref.shape[0]
    yl, z, core = dp // 8, dp // 2 % 4, dp % 2

    def at(dy, dz, dc):
        return {"dp": ((yl + dy) % 2 * 4 + (z + dz) % 4) * 2 + (core + dc) % 2}

    loads = []
    for step in range(steps):
        loads.append(
            pltpu.make_async_copy(
                pts_ref.at[pl.ds(step * CHUNK, CHUNK)], pts.at[step], load.at[step]
            )
        )
        loads[-1].start()
    barrier = pltpu.get_barrier_semaphore()
    for dy in range(2):
        for dz in range(4):
            for dc in range(2):
                if dy or dz or dc:
                    pl.semaphore_signal(
                        barrier, inc=1, device_id=at(dy, dz, dc), device_id_type=MESH
                    )

    tri[...] = jnp.where(
        iota((CHUNK, CHUNK), 0) <= iota((CHUNK, CHUNK), 1), 1.0, 0.0
    ).astype(BF16)
    for step in range(steps):
        block = lab_ref[step] // block_rows
        dest = block // panel_ways
        hits[step * data_ways : (step + 1) * data_ways, :] = jnp.where(
            jnp.logical_and(
                iota((data_ways, CHUNK), 0) == dest, block % panel_ways == panel
            ),
            1.0,
            0.0,
        )
    counts = dot(hits[...].astype(BF16), tri[...])
    carry = jnp.zeros((data_ways, 1), F32)
    most = jnp.zeros((1, 1), F32)
    row = iota((16, CHUNK), 0)
    for step in range(steps):
        hit = hits[step * data_ways : (step + 1) * data_ways, :]
        count = counts[step * data_ways : (step + 1) * data_ways, :]
        order = jnp.sum(
            hit * jnp.sum(count, axis=0, keepdims=True), axis=0, keepdims=True
        )
        rank[step] = order.astype(jnp.int32)
        spot = jnp.sum(hit * (count + carry), axis=0, keepdims=True)
        last = count[:, CHUNK - 1 : CHUNK]
        carry = carry + last
        most = jnp.maximum(most, jnp.sum(last, axis=0, keepdims=True))
        lab = lab_ref[step]
        dest = (lab // block_rows // panel_ways).astype(F32)
        slot = (lab % block_rows + 1).astype(F32)
        meta[step] = jnp.where(
            row == 0,
            dest,
            jnp.where(row == 1, jnp.minimum(spot, 255.0), jnp.where(row == 2, slot, 0.0)),
        ).astype(BF16)
    over = jnp.logical_or(most > KEEP, jnp.max(carry, axis=0, keepdims=True) > CAP)
    bad = jnp.where(over, jnp.inf, 0.0)

    used = [0]
    started = []

    def copy(src, dst, to):
        n = used[0]
        used[0] += 1
        made = pltpu.make_async_remote_copy(
            src_ref=src, dst_ref=dst, send_sem=send.at[n], recv_sem=recv.at[n],
            device_id=to, device_id_type=MESH,
        )
        made.start()
        started.append(made)
        return made

    for step in range(steps):
        pick = jnp.where(iota((KEEP, CHUNK), 0) + 1 == rank[step], 1.0, 0.0).astype(BF16)
        metas[:, step * KEEP : (step + 1) * KEEP] = dot(
            meta[step], pick, ((1,), (1,))
        ).astype(BF16)
        loads[step].wait()
        kept[step * KEEP : (step + 1) * KEEP, :] = dot(pick, pts[step]).astype(BF16)

    pl.semaphore_wait(barrier, data_ways - 1)
    places = metas[...]
    whole = places.astype(F32).astype(jnp.int32)
    dests, spots = whole[0:1, :], whole[1:2, :]
    total = places.shape[1]
    arrive = {}
    order = [(1, 2), (0, 2), (1, 1), (0, 3), (1, 3), (0, 1), (1, 0), (0, 0)]
    for dy, dz in order:
        wanted = jnp.concatenate(
            [
                jnp.broadcast_to(
                    jnp.where(dests == at(dy, dz, dc)["dp"], spots, 0), (SLOT, total)
                )
                for dc in range(2)
            ],
            axis=0,
        )
        pick = jnp.where(iota((2 * SLOT, total), 0) % SLOT + 1 == wanted, 1.0, 0.0).astype(BF16)
        rows = dot(pick, kept[...]).astype(BF16)
        ids = dot(places, pick, ((1,), (1,))).astype(BF16)
        for dc in range(2):
            k = (dy * 4 + dz) * 2 + dc
            out[k] = rows[dc * SLOT : (dc + 1) * SLOT, :]
            out_id[k] = ids[:, dc * SLOT : (dc + 1) * SLOT]
            if k:
                to = at(dy, dz, dc)
                arrive[k] = [
                    copy(out_id.at[k], got_id.at[k], to),
                    copy(out.at[k, pl.ds(0, CAP)], got.at[k, pl.ds(0, CAP)], to),
                ]

    rows, features = sums_ref.shape
    got[:, CAP:SLOT, :] = jnp.zeros((data_ways, SLOT - CAP, features), BF16)
    ones = jnp.ones((8, SLOT), BF16)
    across = ((1,), (1,))
    for dy, dz in order[::-1]:
        for dc in range(2):
            k = (dy * 4 + dz) * 2 + dc
            for made in arrive.get(k, ()):
                made.wait_recv()
            ids = (got_id if k else out_id)[k].astype(F32).astype(jnp.int32)
            pick = jnp.where(iota((rows, SLOT), 0) + 1 == ids[2:3, :], 1.0, 0.0).astype(BF16)
            vectors = (got if k else out)[k]
            if k:
                sums_ref[...] += dot(pick, vectors)
                count_ref[...] += dot(ones, pick, across)
            else:
                sums_ref[...] = dot(pick, vectors)
                count_ref[...] = dot(ones, pick, across)
    hi, lo = split(sums_ref[...])
    cents = cents_ref[...]
    first = ((0,), (0,))
    cov_ref[...] = dot(hi, cents, first) + dot(lo, cents, first)
    cov_ref[0:8, 0:128] = cov_ref[0:8, 0:128] + bad
    for made in started:
        made.wait_send()


def vmem(n):
    return [pl.BlockSpec(memory_space=pltpu.VMEM)] * n


def exchange(labels, points, cents):
    data_ways = lax.axis_size("dp")
    rows, features = cents.shape
    steps = points.shape[0] // CHUNK
    copies = 2 * (data_ways - 1)
    return pl.pallas_call(
        functools.partial(exchange_kernel, rows),
        in_specs=vmem(1) + [pl.BlockSpec(memory_space=pl.ANY)] + vmem(1),
        out_specs=vmem(3),
        out_shape=[
            jax.ShapeDtypeStruct((rows, features), F32),
            jax.ShapeDtypeStruct((8, rows), F32),
            jax.ShapeDtypeStruct((features, features), F32),
        ],
        scratch_shapes=[
            pltpu.VMEM((steps, CHUNK, features), BF16),
            pltpu.VMEM((CHUNK, CHUNK), BF16),
            pltpu.VMEM((steps * data_ways, CHUNK), F32),
            pltpu.VMEM((steps, 1, CHUNK), jnp.int32),
            pltpu.VMEM((steps, 16, CHUNK), BF16),
            pltpu.VMEM((steps * KEEP, features), BF16),
            pltpu.VMEM((16, steps * KEEP), BF16),
            pltpu.VMEM((data_ways, SLOT, features), BF16),
            pltpu.VMEM((data_ways, SLOT, features), BF16),
            pltpu.VMEM((data_ways, 16, SLOT), BF16),
            pltpu.VMEM((data_ways, 16, SLOT), BF16),
            pltpu.SemaphoreType.DMA((steps,)),
            pltpu.SemaphoreType.DMA((copies,)),
            pltpu.SemaphoreType.DMA((copies,)),
        ],
        compiler_params=pltpu.CompilerParams(
            collective_id=0, has_side_effects=True, vmem_limit_bytes=40 << 20
        ),
        name="exchange",
    )(labels.reshape(steps, 1, CHUNK), points, cents)


def settle_kernel(
    part_ref, sums_ref, count_ref, cents_ref, rot_ref, new_ref, half, got1, got2, got3, acc, own, hx, lx, top, low, square,
    sum_hi, sum_lo, counts, fresh, send, recv, tile_send, tile_recv,
):
    xyz, core = place()
    panel = lax.axis_index("cent")
    features = part_ref.shape[1]
    mine = features // 2
    tile = 256
    tiles = features // tile
    barrier = pltpu.get_barrier_semaphore()
    other = device(xyz, 1 - core)
    partners = [other] + [
        device(moved(xyz, axis, by), core) for axis in range(3) for by in range(1, WAYS)
    ]
    for partner in partners:
        pl.semaphore_signal(barrier, inc=1, device_id=partner, device_id_type=MESH)
    pl.semaphore_wait(barrier, len(partners))

    used = [0]
    started = []

    def remote(src, dst, s, r, to):
        made = pltpu.make_async_remote_copy(
            src_ref=src, dst_ref=dst, send_sem=s, recv_sem=r, device_id=to, device_id_type=MESH
        )
        started.append(made)
        return made

    def copy(src, dst, to):
        n = used[0]
        used[0] += 1
        made = remote(src, dst, send.at[n], recv.at[n], to)
        made.start()
        return made

    here = pl.multiple_of(core * mine, mine)
    there = pl.multiple_of((1 - core) * mine, mine)
    parts = range(len(LANES))
    lanes = [pl.ds(lane, width) for lane, width in LANES]
    sizes = [mine // WAYS ** (stage + 1) for stage in range(3)]
    gots = (got1, got2, got3)
    base = [0, 0, 0]
    waits = [
        [copy(part_ref.at[pl.ds(there, mine), lanes[part]], half.at[:, lanes[part]], other)]
        for part in parts
    ]

    def scatter(stage, part):
        size, axis = sizes[stage], (part + stage) % 3
        made = []
        for by in range(1, WAYS):
            to = moved(xyz, axis, by)
            start = pl.multiple_of(base[part] + to[axis] * size, size)
            made.append(
                copy(
                    acc.at[pl.ds(start, size), lanes[part]],
                    gots[stage].at[by - 1, :, lanes[part]],
                    device(to, core),
                )
            )
        return made

    def spread(stage, part):
        size, axis = sizes[stage], (part + stage) % 3
        span = own.at[pl.ds(pl.multiple_of(base[part], size), size), lanes[part]]
        made = [copy(span, span, device(moved(xyz, axis, by), core)) for by in range(1, WAYS)]
        base[part] = base[part] - xyz[axis] * size
        return made

    def arrived(part):
        for made in waits[part]:
            made.wait_recv()

    for part in parts:
        arrived(part)
        acc[:, lanes[part]] = part_ref[pl.ds(here, mine), lanes[part]] + half[:, lanes[part]]
        waits[part] = scatter(0, part)

    sum_hi[...], sum_lo[...] = split(sums_ref[...])
    unit = jnp.where(iota((8, 128), 0) == 0, 1.0, 0.0)
    counts[...] = lax.dot_general(
        count_ref[...], unit, (((0,), (0,)), ((), ())),
        precision=lax.Precision.HIGHEST, preferred_element_type=F32,
    )

    for stage in range(3):
        size = sizes[stage]
        for part in parts:
            arrived(part)
            base[part] = pl.multiple_of(base[part] + xyz[(part + stage) % 3] * size, size)
            at = (pl.ds(base[part], size), lanes[part])
            total = acc[at]
            for by in range(1, WAYS):
                total = total + gots[stage][by - 1, :, lanes[part]]
            if stage < 2:
                acc[at] = total
                waits[part] = scatter(stage + 1, part)
            else:
                own[at] = total
                waits[part] = spread(2, part)
    for stage in (1, 0):
        for part in parts:
            arrived(part)
            waits[part] = spread(stage, part)
    squares = jnp.zeros((1, 1), F32)
    for part in parts:
        arrived(part)
        at = (slice(0, mine), lanes[part])
        value = own[at]
        hx[0, 0:mine, lanes[part]], lx[0, 0:mine, lanes[part]] = split(value)
        waits[part] = [
            copy(ref.at[0, pl.ds(0, mine), lanes[part]], ref.at[0, pl.ds(mine, mine), lanes[part]], other)
            for ref in (hx, lx)
        ]
        squares = squares + jnp.sum(
            jnp.sum(value * value, axis=0, keepdims=True), axis=1, keepdims=True
        )
    square[0] = jnp.broadcast_to(squares, square.shape[1:])
    waits.append([copy(square.at[0], square.at[1], other)])

    def sent(step, b, c, ref):
        if step == NS_STEPS - 1:
            cols = pl.ds(pl.multiple_of(c * tile, tile), tile)
            src, dst = own.at[:, cols], rot_ref.at[pl.ds(here, mine), cols]
        else:
            cols = pl.ds(pl.multiple_of(c * tile, tile), tile)
            src = ref.at[(step + 1) % 2, pl.ds(0, mine), cols]
            dst = ref.at[(step + 1) % 2, pl.ds(mine, mine), cols]
        return pltpu.make_async_remote_copy(
            src_ref=src, dst_ref=dst, send_sem=tile_send.at[step, b, c],
            recv_sem=tile_recv.at[step, b, c], device_id=other, device_id_type=MESH,
        )

    both = ((1,), (1,))
    keep, turned = 1.5, 0.5
    for step in range(NS_STEPS):
        now, later = step % 2, (step + 1) % 2

        def inner(j):
            rows = pl.ds(pl.multiple_of(j * tile, tile), tile)
            hi, lo = hx[now, 0:mine, :], lx[now, 0:mine, :]
            there_hi = hx[now, rows, :]
            value = dot(hi, there_hi, both) + (
                dot(hi, lx[now, rows, :], both) + dot(lo, there_hi, both)
            )
            top[:, rows], low[:, rows] = split(value)

        pl.loop(0, tiles // 2)(inner)
        if step == 0:
            for row in waits:
                for made in row:
                    made.wait_recv()
            for made in started:
                made.wait_send()
            total = square[0, 0:1, 0:1] + square[1, 0:1, 0:1]
            inverse = 1.0 / (3.0 * jnp.sqrt(total / features + epsilon))
            keep, turned = 1.5 * inverse, 0.5 * inverse * inverse * inverse
        else:
            keep, turned = 1.5, 0.5
            for c in range(tiles):
                for b, ref in enumerate((hx, lx)):
                    sent(step - 1, b, c, ref).wait()
        pl.loop(tiles // 2, tiles)(inner)

        def update(c):
            cols = pl.ds(pl.multiple_of(c * tile, tile), tile)
            hi = hx[now, :, cols]
            turn = dot(top[...], hi) + (dot(top[...], lx[now, :, cols]) + dot(low[...], hi))
            value = keep * own[:, cols] - turned * turn
            own[:, cols] = value
            if step == NS_STEPS - 1:
                rot_ref[pl.ds(here, mine), cols] = value
                sent(step, 0, c, None).start()
            else:
                hx[later, 0:mine, cols], lx[later, 0:mine, cols] = split(value)
                for b, ref in enumerate((hx, lx)):
                    sent(step, b, c, ref).start()

        if step < NS_STEPS - 1:
            pl.loop(0, tiles)(update)

    begun = len(started)
    rings = []
    span = features // RINGS
    per = tiles // RINGS
    for c in range(tiles + 1):
        if c < tiles:
            update(c)
        if c and c % per == 0:
            for done in range(c - per, c):
                sent(NS_STEPS - 1, 0, done, None).wait()
            cols = slice((c - per) * tile, c * tile)
            rot_hi, rot_lo = split(rot_ref[:, cols])
            moved_rows = dot(sum_hi[...], rot_hi) + (
                dot(sum_hi[...], rot_lo) + dot(sum_lo[...], rot_hi)
            )
            value = (
                (moved_rows + cents_ref[:, cols].astype(F32)) / (counts[:, 0:1] + 1.0)
            ).astype(BF16)
            fresh[:, cols] = value
            ring = Ring(copy, xyz, core, fresh, new_ref, pl.ds((c - per) * tile, span))
            ring.begin()
            rings.append(ring)
    rows = fresh.shape[0]
    new_ref[pl.ds(pl.multiple_of(lax.axis_index("cent") * rows, rows), rows), :] = fresh[...]
    for ring in rings:
        ring.forward()
    for ring in rings:
        ring.last()
    for ring in rings:
        ring.finish()
    for made in started[begun:]:
        made.wait_send()


def settle(part, sums, count, cents):
    features = part.shape[0]
    panel_ways = 2 * WAYS
    mine = features // 2
    sizes = [mine // WAYS**n for n in (1, 2, 3)]
    copies = 3 + 2 * 3 * 3 * (WAYS - 1) + 2 * 3 + 1 + RING * RINGS
    return pl.pallas_call(
        settle_kernel,
        in_specs=vmem(4),
        out_specs=vmem(2),
        out_shape=[
            jax.ShapeDtypeStruct(part.shape, F32),
            jax.ShapeDtypeStruct((panel_ways * sums.shape[0], features), BF16),
        ],
        scratch_shapes=[pltpu.VMEM((mine, features), F32)]
        + [pltpu.VMEM((WAYS - 1, size, features), F32) for size in sizes]
        + [pltpu.VMEM((mine, features), F32)] * 2
        + [pltpu.VMEM((2, features, features), BF16)] * 2
        + [pltpu.VMEM((mine, features), BF16)] * 2
        + [pltpu.VMEM((2, 8, 128), F32)]
        + [pltpu.VMEM(cents.shape, BF16)] * 2
        + [pltpu.VMEM((cents.shape[0], 128), F32), pltpu.VMEM(cents.shape, BF16)]
        + [pltpu.SemaphoreType.DMA((copies,))] * 2
        + [pltpu.SemaphoreType.DMA((NS_STEPS, 2, features // 256))] * 2,
        compiler_params=pltpu.CompilerParams(
            collective_id=1, has_side_effects=True, vmem_limit_bytes=28 << 20
        ),
        name="settle",
    )(part, sums, count, cents)


def emit_kernel(new_ref, rot_ref, new_out, rot_out, done):
    copies = [
        pltpu.make_async_copy(src, dst, done.at[n])
        for n, (src, dst) in enumerate(((new_ref, new_out), (rot_ref, rot_out)))
    ]
    for made in copies:
        made.start()
    for made in copies:
        made.wait()


def emit(new, rot):
    return pl.pallas_call(
        emit_kernel,
        in_specs=vmem(2),
        out_specs=[pl.BlockSpec(memory_space=pltpu.HBM)] * 2,
        out_shape=[
            jax.ShapeDtypeStruct(new.shape, new.dtype),
            jax.ShapeDtypeStruct(rot.shape, rot.dtype),
        ],
        scratch_shapes=[pltpu.SemaphoreType.DMA((2,))],
        compiler_params=pltpu.CompilerParams(vmem_limit_bytes=16 << 20),
        name="emit",
    )(new, rot)


def summed(x, axes, ways):
    parts = lax.all_to_all(x, axes, 0, 0, tiled=True)
    return jnp.sum(parts.reshape(ways, x.shape[0] // ways, *x.shape[1:]), axis=0)


def joined(x, axes, ways):
    copies = jnp.broadcast_to(x[None], (ways, *x.shape)).reshape(ways * x.shape[0], *x.shape[1:])
    return lax.all_to_all(copies, axes, 0, 0, tiled=True)


def dense(points, labels, centroids):
    data_ways = lax.axis_size("dp")
    panel_ways = lax.axis_size("cent")
    block_rows = centroids.shape[0]
    features = points.shape[1]
    column = lax.axis_index("cent")
    owner_block = labels // block_rows
    inside = owner_block % panel_ways == column
    slot_index = jnp.where(
        inside, owner_block // panel_ways * block_rows + labels % block_rows, data_ways * block_rows
    )
    vectors = points.astype(F32)
    local_sums = jax.ops.segment_sum(vectors, slot_index, num_segments=data_ways * block_rows)
    local_counts = jax.ops.segment_sum(
        jnp.ones((*labels.shape, 128), F32), slot_index, num_segments=data_ways * block_rows
    )[:, 0]
    label_sums = summed(local_sums, "dp", data_ways)
    label_counts = summed(local_counts, "dp", data_ways)
    old_rows = centroids.astype(F32)
    part = lax.dot_general(
        label_sums, old_rows, (((0,), (0,)), ((), ())), precision=lax.Precision.HIGHEST
    )
    every = ("dp", "cent")
    cross_cov = joined(
        summed(part, every, data_ways * panel_ways), every, data_ways * panel_ways
    )
    scale_root = jnp.sqrt(jnp.sum(cross_cov * cross_cov) / features + epsilon)
    rotation = cross_cov / (3.0 * scale_root)
    for iteration in range(NS_STEPS):
        inner_prod = jnp.dot(rotation, rotation.T, precision=lax.Precision.HIGHEST)
        rotation = 1.5 * rotation - 0.5 * jnp.dot(
            inner_prod, rotation, precision=lax.Precision.HIGHEST
        )
    rotated_sums = jnp.dot(label_sums, rotation, precision=lax.Precision.HIGHEST)
    moved_rows = joined(rotated_sums + old_rows, "cent", panel_ways)
    all_counts = joined(label_counts, "cent", panel_ways)
    return ((moved_rows / (all_counts[:, None] + 1.0)).astype(BF16), rotation)


def local(points, labels, centroids):
    sums, count, part = exchange(labels, points, centroids)
    rotation, new_centroids = settle(part, sums, count, centroids)
    bad = jnp.logical_not(jnp.isfinite(rotation[0, 0]))
    new_centroids, rotation = emit(new_centroids, rotation)
    _, new_centroids, rotation = lax.while_loop(
        lambda state: state[0],
        lambda state: (jnp.array(False), *dense(points, labels, centroids)),
        (bad, new_centroids, rotation),
    )
    return new_centroids, rotation


def solution(mesh):
    return jax.shard_map(
        local,
        mesh=mesh,
        in_specs=(P("dp", None), P("dp"), P(("dp", "cent"), None)),
        out_specs=(P("dp", None), P()),
        check_vma=False,
    )
```

```python
import functools

import jax
import jax.numpy as jnp
from jax import lax
from jax.experimental import pallas as pl
from jax.experimental.pallas import tpu as pltpu
from jax.sharding import PartitionSpec as P

MESH = pl.DeviceIdType.MESH
F32 = jnp.float32
BF16 = jnp.bfloat16

NS_STEPS = 3
epsilon = 1e-06

CHUNK = 512
KEEP = 128
CAP = 112
SLOT = 128
WAYS = 4
LANES = ((0, 384), (384, 384), (768, 256))


def dot(a, b, dims=((1,), (0,))):
    return lax.dot_general(a, b, (dims, ((), ())), preferred_element_type=F32)


def split(x):
    hi = x.astype(BF16)
    return hi, (x - hi.astype(F32)).astype(BF16)


def iota(shape, axis):
    return lax.broadcasted_iota(jnp.int32, shape, axis)


def place():
    dp, cent = lax.axis_index("dp"), lax.axis_index("cent")
    x, y, z = cent // 2, cent % 2 * 2 + dp // 8, dp // 2 % 4
    return (x, y, z), dp % 2


def device(xyz, core):
    x, y, z = xyz
    return {"dp": (y % 2 * 4 + z) * 2 + core, "cent": x * 2 + y // 2}


def moved(xyz, axis, by):
    return tuple((c + by) % WAYS if a == axis else c for a, c in enumerate(xyz))


class Ring:
    def __init__(self, copy, xyz, core, fresh, all_ref, lanes):
        self.copy, self.xyz, self.core = copy, xyz, core
        self.fresh, self.all_ref, self.lanes = fresh, all_ref, lanes
        self.right, self.left = moved(xyz, 0, 1), moved(xyz, 0, WAYS - 1)
        self.across = moved(xyz, 1, 2)

    def spot(self, owner, part):
        half = self.all_ref.shape[0] // (4 * WAYS)
        start = ((owner[0] * 2 + owner[1] // 2) * 2 + part) * half
        return self.all_ref.at[pl.ds(pl.multiple_of(start, half), half), self.lanes]

    def send(self, owner, part, to, fresh=False):
        spot = self.spot(owner, part)
        half = spot.shape[0]
        own = self.fresh.at[pl.ds(part * half, half), self.lanes]
        return self.copy(own if fresh else spot, spot, device(to, self.core))

    def begin(self):
        me = self.xyz
        self.over = [self.send(me, 0, self.across, True)]
        self.rights = [self.send(me, 0, self.right, True)]
        self.lefts = [None, self.send(me, 1, self.left, True)]
        self.over.append(self.send(me, 1, self.across, True))
        self.rights.append(self.send(me, 1, self.right, True))
        self.lefts[0] = self.send(me, 0, self.left, True)

    def forward(self):
        self.rights[0].wait_recv()
        self.overs = []
        self.ends = [self.send(self.left, 0, self.right)]
        self.lefts[1].wait_recv()
        self.ends.append(self.send(self.right, 1, self.left))
        self.over[0].wait_recv()
        self.rights2 = [self.send(self.across, 0, self.right)]
        self.lefts2 = [self.send(self.across, 0, self.left)]
        self.over[1].wait_recv()
        self.lefts2.append(self.send(self.across, 1, self.left))
        self.rights2.append(self.send(self.across, 1, self.right))

    def last(self):
        opposite = moved(self.xyz, 0, 2)
        for part in range(2):
            self.ends[part].wait_recv()
            self.overs.append(self.send(opposite, part, self.across))

    def finish(self):
        late = [self.rights[1], self.lefts[0]] + self.rights2 + self.lefts2 + self.overs
        for made in late:
            made.wait_recv()


RING = 14
RINGS = 2


def exchange_kernel(
    block_rows, lab_ref, pts_ref, cents_ref, sums_ref, count_ref, cov_ref,
    pts, tri, hits, rank, meta, kept, metas, out, got, out_id, got_id, sum_hi, sum_lo, pair_hi, pair_lo, pair_cents, load, send, recv,
):
    dp, panel = lax.axis_index("dp"), lax.axis_index("cent")
    data_ways, panel_ways = lax.axis_size("dp"), lax.axis_size("cent")
    steps = lab_ref.shape[0]
    yl, z, core = dp // 8, dp // 2 % 4, dp % 2

    def at(dy, dz, dc):
        return {"dp": ((yl + dy) % 2 * 4 + (z + dz) % 4) * 2 + (core + dc) % 2}

    loads = []
    for step in range(steps):
        loads.append(
            pltpu.make_async_copy(
                pts_ref.at[pl.ds(step * CHUNK, CHUNK)], pts.at[step], load.at[step]
            )
        )
        loads[-1].start()
    barrier = pltpu.get_barrier_semaphore()
    for dy in range(2):
        for dz in range(4):
            for dc in range(2):
                if dy or dz or dc:
                    pl.semaphore_signal(
                        barrier, inc=1, device_id=at(dy, dz, dc), device_id_type=MESH
                    )

    tri[...] = jnp.where(
        iota((CHUNK, CHUNK), 0) <= iota((CHUNK, CHUNK), 1), 1.0, 0.0
    ).astype(BF16)
    for step in range(steps):
        block = lab_ref[step] // block_rows
        dest = block // panel_ways
        hits[step * data_ways : (step + 1) * data_ways, :] = jnp.where(
            jnp.logical_and(
                iota((data_ways, CHUNK), 0) == dest, block % panel_ways == panel
            ),
            1.0,
            0.0,
        )
    counts = dot(hits[...].astype(BF16), tri[...])
    carry = jnp.zeros((data_ways, 1), F32)
    most = jnp.zeros((1, 1), F32)
    row = iota((16, CHUNK), 0)
    for step in range(steps):
        hit = hits[step * data_ways : (step + 1) * data_ways, :]
        count = counts[step * data_ways : (step + 1) * data_ways, :]
        order = jnp.sum(
            hit * jnp.sum(count, axis=0, keepdims=True), axis=0, keepdims=True
        )
        rank[step] = order.astype(jnp.int32)
        spot = jnp.sum(hit * (count + carry), axis=0, keepdims=True)
        last = count[:, CHUNK - 1 : CHUNK]
        carry = carry + last
        most = jnp.maximum(most, jnp.sum(last, axis=0, keepdims=True))
        lab = lab_ref[step]
        dest = (lab // block_rows // panel_ways).astype(F32)
        slot = (lab % block_rows + 1).astype(F32)
        meta[step] = jnp.where(
            row == 0,
            dest,
            jnp.where(row == 1, jnp.minimum(spot, 255.0), jnp.where(row == 2, slot, 0.0)),
        ).astype(BF16)
    over = jnp.logical_or(most > KEEP, jnp.max(carry, axis=0, keepdims=True) > CAP)
    bad = jnp.where(over, jnp.inf, 0.0)

    used = [0]
    started = []

    def copy(src, dst, to):
        n = used[0]
        used[0] += 1
        made = pltpu.make_async_remote_copy(
            src_ref=src, dst_ref=dst, send_sem=send.at[n], recv_sem=recv.at[n],
            device_id=to, device_id_type=MESH,
        )
        made.start()
        started.append(made)
        return made

    for step in range(steps):
        pick = jnp.where(iota((KEEP, CHUNK), 0) + 1 == rank[step], 1.0, 0.0).astype(BF16)
        metas[:, step * KEEP : (step + 1) * KEEP] = dot(
            meta[step], pick, ((1,), (1,))
        ).astype(BF16)
        loads[step].wait()
        kept[step * KEEP : (step + 1) * KEEP, :] = dot(pick, pts[step]).astype(BF16)

    pl.semaphore_wait(barrier, data_ways - 1)
    beside = at(0, 0, 1)
    shown = copy(cents_ref, pair_cents, beside)
    places = metas[...]
    whole = places.astype(F32).astype(jnp.int32)
    dests, spots = whole[0:1, :], whole[1:2, :]
    total = places.shape[1]
    arrive = {}
    order = [(1, 2), (0, 2), (1, 1), (0, 3), (1, 3), (0, 1), (1, 0), (0, 0)]
    for dy, dz in order:
        wanted = jnp.concatenate(
            [
                jnp.broadcast_to(
                    jnp.where(dests == at(dy, dz, dc)["dp"], spots, 0), (SLOT, total)
                )
                for dc in range(2)
            ],
            axis=0,
        )
        pick = jnp.where(iota((2 * SLOT, total), 0) % SLOT + 1 == wanted, 1.0, 0.0).astype(BF16)
        rows = dot(pick, kept[...]).astype(BF16)
        ids = dot(places, pick, ((1,), (1,))).astype(BF16)
        for dc in range(2):
            k = (dy * 4 + dz) * 2 + dc
            out[k] = rows[dc * SLOT : (dc + 1) * SLOT, :]
            out_id[k] = ids[:, dc * SLOT : (dc + 1) * SLOT]
            if k:
                to = at(dy, dz, dc)
                arrive[k] = [
                    copy(out_id.at[k], got_id.at[k], to),
                    copy(out.at[k, pl.ds(0, CAP)], got.at[k, pl.ds(0, CAP)], to),
                ]

    rows, features = sums_ref.shape
    got[:, CAP:SLOT, :] = jnp.zeros((data_ways, SLOT - CAP, features), BF16)
    ones = jnp.ones((8, SLOT), BF16)
    across = ((1,), (1,))
    for dy, dz in order[::-1]:
        for dc in range(2):
            k = (dy * 4 + dz) * 2 + dc
            for made in arrive.get(k, ()):
                made.wait_recv()
            ids = (got_id if k else out_id)[k].astype(F32).astype(jnp.int32)
            pick = jnp.where(iota((rows, SLOT), 0) + 1 == ids[2:3, :], 1.0, 0.0).astype(BF16)
            vectors = (got if k else out)[k]
            if k:
                sums_ref[...] += dot(pick, vectors)
                count_ref[...] += dot(ones, pick, across)
            else:
                sums_ref[...] = dot(pick, vectors)
                count_ref[...] = dot(ones, pick, across)
    mine = features // 2
    here = pl.ds(pl.multiple_of(core * mine, mine), mine)
    there = pl.ds(pl.multiple_of((1 - core) * mine, mine), mine)
    sum_hi[...], sum_lo[...] = split(sums_ref[...])
    halves = [
        copy(sum_hi.at[:, there], pair_hi, beside), copy(sum_lo.at[:, there], pair_lo, beside)
    ]
    cents = cents_ref[...]
    first = ((0,), (0,))
    cov_ref[...] = dot(sum_hi[:, here], cents, first) + dot(sum_lo[:, here], cents, first)
    for made in [shown] + halves:
        made.wait_recv()
    cents = pair_cents[...]
    cov_ref[...] += dot(pair_hi[...], cents, first) + dot(pair_lo[...], cents, first)
    cov_ref[0:8, 0:128] = cov_ref[0:8, 0:128] + bad
    for made in started:
        made.wait_send()


def vmem(n):
    return [pl.BlockSpec(memory_space=pltpu.VMEM)] * n


def exchange(labels, points, cents):
    data_ways = lax.axis_size("dp")
    rows, features = cents.shape
    steps = points.shape[0] // CHUNK
    copies = 2 * (data_ways - 1) + 3
    return pl.pallas_call(
        functools.partial(exchange_kernel, rows),
        in_specs=vmem(1) + [pl.BlockSpec(memory_space=pl.ANY)] + vmem(1),
        out_specs=vmem(3),
        out_shape=[
            jax.ShapeDtypeStruct((rows, features), F32),
            jax.ShapeDtypeStruct((8, rows), F32),
            jax.ShapeDtypeStruct((features // 2, features), F32),
        ],
        scratch_shapes=[
            pltpu.VMEM((steps, CHUNK, features), BF16),
            pltpu.VMEM((CHUNK, CHUNK), BF16),
            pltpu.VMEM((steps * data_ways, CHUNK), F32),
            pltpu.VMEM((steps, 1, CHUNK), jnp.int32),
            pltpu.VMEM((steps, 16, CHUNK), BF16),
            pltpu.VMEM((steps * KEEP, features), BF16),
            pltpu.VMEM((16, steps * KEEP), BF16),
            pltpu.VMEM((data_ways, SLOT, features), BF16),
            pltpu.VMEM((data_ways, SLOT, features), BF16),
            pltpu.VMEM((data_ways, 16, SLOT), BF16),
            pltpu.VMEM((data_ways, 16, SLOT), BF16),
            pltpu.VMEM((rows, features), BF16),
            pltpu.VMEM((rows, features), BF16),
            pltpu.VMEM((rows, features // 2), BF16),
            pltpu.VMEM((rows, features // 2), BF16),
            pltpu.VMEM((rows, features), BF16),
            pltpu.SemaphoreType.DMA((steps,)),
            pltpu.SemaphoreType.DMA((copies,)),
            pltpu.SemaphoreType.DMA((copies,)),
        ],
        compiler_params=pltpu.CompilerParams(
            collective_id=0, has_side_effects=True, vmem_limit_bytes=40 << 20
        ),
        name="exchange",
    )(labels.reshape(steps, 1, CHUNK), points, cents)


def settle_kernel(
    part_ref, sums_ref, count_ref, cents_ref, rot_ref, new_ref, got1, got2, got3, acc, own, hx, lx, top, low, square,
    sum_hi, sum_lo, counts, fresh, send, recv, tile_send, tile_recv,
):
    xyz, core = place()
    panel = lax.axis_index("cent")
    features = part_ref.shape[1]
    mine = features // 2
    tile = 256
    tiles = features // tile
    barrier = pltpu.get_barrier_semaphore()
    other = device(xyz, 1 - core)
    partners = [other] + [
        device(moved(xyz, axis, by), core) for axis in range(3) for by in range(1, WAYS)
    ]
    for partner in partners:
        pl.semaphore_signal(barrier, inc=1, device_id=partner, device_id_type=MESH)
    pl.semaphore_wait(barrier, len(partners))

    used = [0]
    started = []

    def remote(src, dst, s, r, to):
        made = pltpu.make_async_remote_copy(
            src_ref=src, dst_ref=dst, send_sem=s, recv_sem=r, device_id=to, device_id_type=MESH
        )
        started.append(made)
        return made

    def copy(src, dst, to):
        n = used[0]
        used[0] += 1
        made = remote(src, dst, send.at[n], recv.at[n], to)
        made.start()
        return made

    here = pl.multiple_of(core * mine, mine)
    parts = range(len(LANES))
    lanes = [pl.ds(lane, width) for lane, width in LANES]
    sizes = [mine // WAYS ** (stage + 1) for stage in range(3)]
    gots = (got1, got2, got3)
    base = [0, 0, 0]

    def scatter(stage, part):
        size, axis = sizes[stage], (part + stage) % 3
        made = []
        for by in range(1, WAYS):
            to = moved(xyz, axis, by)
            start = pl.multiple_of(base[part] + to[axis] * size, size)
            made.append(
                copy(
                    (acc if stage else part_ref).at[pl.ds(start, size), lanes[part]],
                    gots[stage].at[by - 1, :, lanes[part]],
                    device(to, core),
                )
            )
        return made

    def spread(stage, part):
        size, axis = sizes[stage], (part + stage) % 3
        span = own.at[pl.ds(pl.multiple_of(base[part], size), size), lanes[part]]
        made = [copy(span, span, device(moved(xyz, axis, by), core)) for by in range(1, WAYS)]
        base[part] = base[part] - xyz[axis] * size
        return made

    def arrived(part):
        for made in waits[part]:
            made.wait_recv()

    waits = [scatter(0, part) for part in parts]

    sum_hi[...], sum_lo[...] = split(sums_ref[...])
    unit = jnp.where(iota((8, 128), 0) == 0, 1.0, 0.0)
    counts[...] = lax.dot_general(
        count_ref[...], unit, (((0,), (0,)), ((), ())),
        precision=lax.Precision.HIGHEST, preferred_element_type=F32,
    )

    for stage in range(3):
        size = sizes[stage]
        for part in parts:
            arrived(part)
            base[part] = pl.multiple_of(base[part] + xyz[(part + stage) % 3] * size, size)
            at = (pl.ds(base[part], size), lanes[part])
            total = (acc if stage else part_ref)[at]
            for by in range(1, WAYS):
                total = total + gots[stage][by - 1, :, lanes[part]]
            if stage < 2:
                acc[at] = total
                waits[part] = scatter(stage + 1, part)
            else:
                own[at] = total
                waits[part] = spread(2, part)
    for stage in (1, 0):
        for part in parts:
            arrived(part)
            waits[part] = spread(stage, part)
    squares = jnp.zeros((1, 1), F32)
    for part in parts:
        arrived(part)
        at = (slice(0, mine), lanes[part])
        value = own[at]
        hx[0, 0:mine, lanes[part]], lx[0, 0:mine, lanes[part]] = split(value)
        waits[part] = [
            copy(ref.at[0, pl.ds(0, mine), lanes[part]], ref.at[0, pl.ds(mine, mine), lanes[part]], other)
            for ref in (hx, lx)
        ]
        squares = squares + jnp.sum(
            jnp.sum(value * value, axis=0, keepdims=True), axis=1, keepdims=True
        )
    square[0] = jnp.broadcast_to(squares, square.shape[1:])
    waits.append([copy(square.at[0], square.at[1], other)])

    def sent(step, b, c, ref):
        cols = pl.ds(c * tile, tile)
        if step == NS_STEPS - 1:
            src, dst = own.at[:, cols], rot_ref.at[pl.ds(here, mine), cols]
        else:
            src = ref.at[(step + 1) % 2, pl.ds(0, mine), cols]
            dst = ref.at[(step + 1) % 2, pl.ds(mine, mine), cols]
        return pltpu.make_async_remote_copy(
            src_ref=src, dst_ref=dst, send_sem=tile_send.at[step, b, c],
            recv_sem=tile_recv.at[step, b, c], device_id=other, device_id_type=MESH,
        )

    both = ((1,), (1,))
    keep, turned = 1.5, 0.5
    for step in range(NS_STEPS):
        now, later = step % 2, (step + 1) % 2

        def inner(j):
            rows = slice(j * tile, (j + 1) * tile)
            hi, lo = hx[now, 0:mine, :], lx[now, 0:mine, :]
            there_hi = hx[now, rows, :]
            value = dot(hi, there_hi, both) + (
                dot(hi, lx[now, rows, :], both) + dot(lo, there_hi, both)
            )
            top[:, rows], low[:, rows] = split(value)

        for j in range(tiles // 2):
            inner(j)
        if step == 0:
            for row in waits:
                for made in row:
                    made.wait_recv()
            for made in started:
                made.wait_send()
            total = square[0, 0:1, 0:1] + square[1, 0:1, 0:1]
            inverse = 1.0 / (3.0 * jnp.sqrt(total / features + epsilon))
            keep, turned = 1.5 * inverse, 0.5 * inverse * inverse * inverse
        else:
            keep, turned = 1.5, 0.5
            for c in range(tiles):
                for b, ref in enumerate((hx, lx)):
                    sent(step - 1, b, c, ref).wait()
        for j in range(tiles // 2, tiles):
            inner(j)

        def update(c):
            cols = slice(c * tile, (c + 1) * tile)
            hi = hx[now, :, cols]
            turn = dot(top[...], hi) + (dot(top[...], lx[now, :, cols]) + dot(low[...], hi))
            value = keep * own[:, cols] - turned * turn
            own[:, cols] = value
            if step == NS_STEPS - 1:
                rot_ref[pl.ds(here, mine), cols] = value
                sent(step, 0, c, None).start()
            else:
                hx[later, 0:mine, cols], lx[later, 0:mine, cols] = split(value)
                for b, ref in enumerate((hx, lx)):
                    sent(step, b, c, ref).start()

        if step < NS_STEPS - 1:
            for c in range(tiles):
                update(c)

    begun = len(started)
    rings = []
    span = features // RINGS
    per = tiles // RINGS
    for c in range(tiles + 1):
        if c < tiles:
            update(c)
        if c and c % per == 0:
            for done in range(c - per, c):
                sent(NS_STEPS - 1, 0, done, None).wait()
            cols = slice((c - per) * tile, c * tile)
            rot_hi, rot_lo = split(rot_ref[:, cols])
            moved_rows = dot(sum_hi[...], rot_hi) + (
                dot(sum_hi[...], rot_lo) + dot(sum_lo[...], rot_hi)
            )
            value = (
                (moved_rows + cents_ref[:, cols].astype(F32)) / (counts[:, 0:1] + 1.0)
            ).astype(BF16)
            fresh[:, cols] = value
            ring = Ring(copy, xyz, core, fresh, new_ref, pl.ds((c - per) * tile, span))
            ring.begin()
            rings.append(ring)
    rows = fresh.shape[0]
    new_ref[pl.ds(pl.multiple_of(lax.axis_index("cent") * rows, rows), rows), :] = fresh[...]
    for ring in rings:
        ring.forward()
    for ring in rings:
        ring.last()
    for ring in rings:
        ring.finish()
    for made in started[begun:]:
        made.wait_send()


def settle(part, sums, count, cents):
    features = part.shape[1]
    panel_ways = 2 * WAYS
    mine = features // 2
    sizes = [mine // WAYS**n for n in (1, 2, 3)]
    copies = 2 * 3 * 3 * (WAYS - 1) + 2 * 3 + 1 + RING * RINGS
    return pl.pallas_call(
        settle_kernel,
        in_specs=vmem(4),
        out_specs=vmem(2),
        out_shape=[
            jax.ShapeDtypeStruct((features, features), F32),
            jax.ShapeDtypeStruct((panel_ways * sums.shape[0], features), BF16),
        ],
        scratch_shapes=[pltpu.VMEM((WAYS - 1, size, features), F32) for size in sizes]
        + [pltpu.VMEM((mine, features), F32)] * 2
        + [pltpu.VMEM((2, features, features), BF16)] * 2
        + [pltpu.VMEM((mine, features), BF16)] * 2
        + [pltpu.VMEM((2, 8, 128), F32)]
        + [pltpu.VMEM(cents.shape, BF16)] * 2
        + [pltpu.VMEM((cents.shape[0], 128), F32), pltpu.VMEM(cents.shape, BF16)]
        + [pltpu.SemaphoreType.DMA((copies,))] * 2
        + [pltpu.SemaphoreType.DMA((NS_STEPS, 2, features // 256))] * 2,
        compiler_params=pltpu.CompilerParams(
            collective_id=1, has_side_effects=True, vmem_limit_bytes=28 << 20
        ),
        name="settle",
    )(part, sums, count, cents)


def emit_kernel(new_ref, rot_ref, new_out, rot_out, bad_ref, done):
    copies = [
        pltpu.make_async_copy(
            src.at[pl.ds(n * src.shape[0] // 4, src.shape[0] // 4)],
            dst.at[pl.ds(n * src.shape[0] // 4, src.shape[0] // 4)],
            done.at[which, n],
        )
        for n in range(4)
        for which, (src, dst) in enumerate(((new_ref, new_out), (rot_ref, rot_out)))
    ]
    for made in copies:
        made.start()
    bad_ref[...] = jnp.where(jnp.abs(rot_ref[0:1, 0:1]) < jnp.inf, 0, 1)
    for made in copies:
        made.wait()


def emit(new, rot):
    return pl.pallas_call(
        emit_kernel,
        in_specs=vmem(2),
        out_specs=[pl.BlockSpec(memory_space=pltpu.HBM)] * 2 + vmem(1),
        out_shape=[
            jax.ShapeDtypeStruct(new.shape, new.dtype),
            jax.ShapeDtypeStruct(rot.shape, rot.dtype),
            jax.ShapeDtypeStruct((1, 1), jnp.int32),
        ],
        scratch_shapes=[pltpu.SemaphoreType.DMA((2, 4))],
        compiler_params=pltpu.CompilerParams(vmem_limit_bytes=16 << 20),
        name="emit",
    )(new, rot)


def summed(x, axes, ways):
    parts = lax.all_to_all(x, axes, 0, 0, tiled=True)
    return jnp.sum(parts.reshape(ways, x.shape[0] // ways, *x.shape[1:]), axis=0)


def joined(x, axes, ways):
    copies = jnp.broadcast_to(x[None], (ways, *x.shape)).reshape(ways * x.shape[0], *x.shape[1:])
    return lax.all_to_all(copies, axes, 0, 0, tiled=True)


def dense(points, labels, centroids):
    data_ways = lax.axis_size("dp")
    panel_ways = lax.axis_size("cent")
    block_rows = centroids.shape[0]
    features = points.shape[1]
    column = lax.axis_index("cent")
    owner_block = labels // block_rows
    inside = owner_block % panel_ways == column
    slot_index = jnp.where(
        inside, owner_block // panel_ways * block_rows + labels % block_rows, data_ways * block_rows
    )
    vectors = points.astype(F32)
    local_sums = jax.ops.segment_sum(vectors, slot_index, num_segments=data_ways * block_rows)
    local_counts = jax.ops.segment_sum(
        jnp.ones((*labels.shape, 128), F32), slot_index, num_segments=data_ways * block_rows
    )[:, 0]
    label_sums = summed(local_sums, "dp", data_ways)
    label_counts = summed(local_counts, "dp", data_ways)
    old_rows = centroids.astype(F32)
    part = lax.dot_general(
        label_sums, old_rows, (((0,), (0,)), ((), ())), precision=lax.Precision.HIGHEST
    )
    every = ("dp", "cent")
    cross_cov = joined(
        summed(part, every, data_ways * panel_ways), every, data_ways * panel_ways
    )
    scale_root = jnp.sqrt(jnp.sum(cross_cov * cross_cov) / features + epsilon)
    rotation = cross_cov / (3.0 * scale_root)
    for iteration in range(NS_STEPS):
        inner_prod = jnp.dot(rotation, rotation.T, precision=lax.Precision.HIGHEST)
        rotation = 1.5 * rotation - 0.5 * jnp.dot(
            inner_prod, rotation, precision=lax.Precision.HIGHEST
        )
    rotated_sums = jnp.dot(label_sums, rotation, precision=lax.Precision.HIGHEST)
    moved_rows = joined(rotated_sums + old_rows, "cent", panel_ways)
    all_counts = joined(label_counts, "cent", panel_ways)
    return ((moved_rows / (all_counts[:, None] + 1.0)).astype(BF16), rotation)


def local(points, labels, centroids):
    sums, count, part = exchange(labels, points, centroids)
    rotation, new_centroids = settle(part, sums, count, centroids)
    new_centroids, rotation, bad = emit(new_centroids, rotation)
    _, new_centroids, rotation = lax.while_loop(
        lambda state: state[0] > 0,
        lambda state: (jnp.int32(0), *dense(points, labels, centroids)),
        (bad.reshape(()), new_centroids, rotation),
    )
    return new_centroids, rotation


def solution(mesh):
    return jax.shard_map(
        local,
        mesh=mesh,
        in_specs=(P("dp", None), P("dp"), P(("dp", "cent"), None)),
        out_specs=(P("dp", None), P()),
        check_vma=False,
    )
```

```python
import functools

import jax
import jax.numpy as jnp
from jax import lax
from jax.experimental import pallas as pl
from jax.experimental.pallas import tpu as pltpu
from jax.sharding import PartitionSpec as P

MESH = pl.DeviceIdType.MESH
F32 = jnp.float32
BF16 = jnp.bfloat16

NS_STEPS = 3
epsilon = 1e-06

CHUNK = 512
KEEP = 128
CAP = 112
SLOT = 128
WAYS = 4
LANES = ((0, 384), (384, 384), (768, 256))


def dot(a, b, dims=((1,), (0,))):
    return lax.dot_general(a, b, (dims, ((), ())), preferred_element_type=F32)


def split(x):
    hi = x.astype(BF16)
    return hi, (x - hi.astype(F32)).astype(BF16)


def iota(shape, axis):
    return lax.broadcasted_iota(jnp.int32, shape, axis)


def place():
    dp, cent = lax.axis_index("dp"), lax.axis_index("cent")
    x, y, z = cent // 2, cent % 2 * 2 + dp // 8, dp // 2 % 4
    return (x, y, z), dp % 2


def device(xyz, core):
    x, y, z = xyz
    return {"dp": (y % 2 * 4 + z) * 2 + core, "cent": x * 2 + y // 2}


def moved(xyz, axis, by):
    return tuple((c + by) % WAYS if a == axis else c for a, c in enumerate(xyz))


class Ring:
    def __init__(self, copy, xyz, core, fresh, all_ref, lanes):
        self.copy, self.xyz, self.core = copy, xyz, core
        self.fresh, self.all_ref, self.lanes = fresh, all_ref, lanes
        self.right, self.left = moved(xyz, 0, 1), moved(xyz, 0, WAYS - 1)
        self.across = moved(xyz, 1, 2)

    def spot(self, owner, part):
        half = self.all_ref.shape[0] // (4 * WAYS)
        start = ((owner[0] * 2 + owner[1] // 2) * 2 + part) * half
        return self.all_ref.at[pl.ds(pl.multiple_of(start, half), half), self.lanes]

    def send(self, owner, part, to, fresh=False):
        spot = self.spot(owner, part)
        half = spot.shape[0]
        own = self.fresh.at[pl.ds(part * half, half), self.lanes]
        return self.copy(own if fresh else spot, spot, device(to, self.core))

    def begin(self):
        me = self.xyz
        self.over = [self.send(me, 0, self.across, True)]
        self.rights = [self.send(me, 0, self.right, True)]
        self.lefts = [None, self.send(me, 1, self.left, True)]
        self.over.append(self.send(me, 1, self.across, True))
        self.rights.append(self.send(me, 1, self.right, True))
        self.lefts[0] = self.send(me, 0, self.left, True)

    def forward(self):
        self.rights[0].wait_recv()
        self.overs = []
        self.ends = [self.send(self.left, 0, self.right)]
        self.lefts[1].wait_recv()
        self.ends.append(self.send(self.right, 1, self.left))
        self.over[0].wait_recv()
        self.rights2 = [self.send(self.across, 0, self.right)]
        self.lefts2 = [self.send(self.across, 0, self.left)]
        self.over[1].wait_recv()
        self.lefts2.append(self.send(self.across, 1, self.left))
        self.rights2.append(self.send(self.across, 1, self.right))

    def last(self):
        opposite = moved(self.xyz, 0, 2)
        for part in range(2):
            self.ends[part].wait_recv()
            self.overs.append(self.send(opposite, part, self.across))

    def finish(self):
        late = [self.rights[1], self.lefts[0]] + self.rights2 + self.lefts2 + self.overs
        for made in late:
            made.wait_recv()


RING = 14
RINGS = 2


def exchange_kernel(
    block_rows, lab_ref, pts_ref, cents_ref, sums_ref, count_ref, cov_ref,
    pts, tri, hits, rank, meta, kept, metas, out, got, out_id, got_id, sum_hi, sum_lo, pair_hi, pair_lo, pair_cents, load, send, recv,
):
    dp, panel = lax.axis_index("dp"), lax.axis_index("cent")
    data_ways, panel_ways = lax.axis_size("dp"), lax.axis_size("cent")
    steps = lab_ref.shape[0]
    yl, z, core = dp // 8, dp // 2 % 4, dp % 2

    def at(dy, dz, dc):
        return {"dp": ((yl + dy) % 2 * 4 + (z + dz) % 4) * 2 + (core + dc) % 2}

    loads = []
    for step in range(steps):
        loads.append(
            pltpu.make_async_copy(
                pts_ref.at[pl.ds(step * CHUNK, CHUNK)], pts.at[step], load.at[step]
            )
        )
        loads[-1].start()
    barrier = pltpu.get_barrier_semaphore()
    for dy in range(2):
        for dz in range(4):
            for dc in range(2):
                if dy or dz or dc:
                    pl.semaphore_signal(
                        barrier, inc=1, device_id=at(dy, dz, dc), device_id_type=MESH
                    )

    tri[...] = jnp.where(
        iota((CHUNK, CHUNK), 0) <= iota((CHUNK, CHUNK), 1), 1.0, 0.0
    ).astype(BF16)
    for step in range(steps):
        block = lab_ref[step] // block_rows
        dest = block // panel_ways
        hits[step * data_ways : (step + 1) * data_ways, :] = jnp.where(
            jnp.logical_and(
                iota((data_ways, CHUNK), 0) == dest, block % panel_ways == panel
            ),
            1.0,
            0.0,
        )
    counts = dot(hits[...].astype(BF16), tri[...])
    carry = jnp.zeros((data_ways, 1), F32)
    most = jnp.zeros((1, 1), F32)
    row = iota((16, CHUNK), 0)
    for step in range(steps):
        hit = hits[step * data_ways : (step + 1) * data_ways, :]
        count = counts[step * data_ways : (step + 1) * data_ways, :]
        order = jnp.sum(
            hit * jnp.sum(count, axis=0, keepdims=True), axis=0, keepdims=True
        )
        rank[step] = order.astype(jnp.int32)
        spot = jnp.sum(hit * (count + carry), axis=0, keepdims=True)
        last = count[:, CHUNK - 1 : CHUNK]
        carry = carry + last
        most = jnp.maximum(most, jnp.sum(last, axis=0, keepdims=True))
        lab = lab_ref[step]
        dest = (lab // block_rows // panel_ways).astype(F32)
        slot = (lab % block_rows + 1).astype(F32)
        meta[step] = jnp.where(
            row == 0,
            dest,
            jnp.where(row == 1, jnp.minimum(spot, 255.0), jnp.where(row == 2, slot, 0.0)),
        ).astype(BF16)
    over = jnp.logical_or(most > KEEP, jnp.max(carry, axis=0, keepdims=True) > CAP)
    bad = jnp.where(over, jnp.inf, 0.0)

    used = [0]
    started = []

    def copy(src, dst, to):
        n = used[0]
        used[0] += 1
        made = pltpu.make_async_remote_copy(
            src_ref=src, dst_ref=dst, send_sem=send.at[n], recv_sem=recv.at[n],
            device_id=to, device_id_type=MESH,
        )
        made.start()
        started.append(made)
        return made

    for step in range(steps):
        pick = jnp.where(iota((KEEP, CHUNK), 0) + 1 == rank[step], 1.0, 0.0).astype(BF16)
        metas[:, step * KEEP : (step + 1) * KEEP] = dot(
            meta[step], pick, ((1,), (1,))
        ).astype(BF16)
        loads[step].wait()
        kept[step * KEEP : (step + 1) * KEEP, :] = dot(pick, pts[step]).astype(BF16)

    pl.semaphore_wait(barrier, data_ways - 1)
    beside = at(0, 0, 1)
    shown = copy(cents_ref, pair_cents, beside)
    places = metas[...]
    whole = places.astype(F32).astype(jnp.int32)
    dests, spots = whole[0:1, :], whole[1:2, :]
    total = places.shape[1]
    arrive = {}
    order = [(1, 2), (0, 2), (1, 1), (0, 3), (1, 3), (0, 1), (1, 0), (0, 0)]
    for dy, dz in order:
        wanted = jnp.concatenate(
            [
                jnp.broadcast_to(
                    jnp.where(dests == at(dy, dz, dc)["dp"], spots, 0), (SLOT, total)
                )
                for dc in range(2)
            ],
            axis=0,
        )
        pick = jnp.where(iota((2 * SLOT, total), 0) % SLOT + 1 == wanted, 1.0, 0.0).astype(BF16)
        rows = dot(pick, kept[...]).astype(BF16)
        ids = dot(places, pick, ((1,), (1,))).astype(BF16)
        for dc in range(2):
            k = (dy * 4 + dz) * 2 + dc
            out[k] = rows[dc * SLOT : (dc + 1) * SLOT, :]
            out_id[k] = ids[:, dc * SLOT : (dc + 1) * SLOT]
            if k:
                to = at(dy, dz, dc)
                arrive[k] = [
                    copy(out_id.at[k], got_id.at[k], to),
                    copy(out.at[k, pl.ds(0, CAP)], got.at[k, pl.ds(0, CAP)], to),
                ]

    rows, features = sums_ref.shape
    got[:, CAP:SLOT, :] = jnp.zeros((data_ways, SLOT - CAP, features), BF16)
    ones = jnp.ones((8, SLOT), BF16)
    across = ((1,), (1,))
    for dy, dz in order[::-1]:
        for dc in range(2):
            k = (dy * 4 + dz) * 2 + dc
            for made in arrive.get(k, ()):
                made.wait_recv()
            ids = (got_id if k else out_id)[k].astype(F32).astype(jnp.int32)
            pick = jnp.where(iota((rows, SLOT), 0) + 1 == ids[2:3, :], 1.0, 0.0).astype(BF16)
            vectors = (got if k else out)[k]
            if k:
                sums_ref[...] += dot(pick, vectors)
                count_ref[...] += dot(ones, pick, across)
            else:
                sums_ref[...] = dot(pick, vectors)
                count_ref[...] = dot(ones, pick, across)
    mine = features // 2
    here = pl.ds(pl.multiple_of(core * mine, mine), mine)
    there = pl.ds(pl.multiple_of((1 - core) * mine, mine), mine)
    sum_hi[...], sum_lo[...] = split(sums_ref[...])
    halves = [
        copy(sum_hi.at[:, there], pair_hi, beside), copy(sum_lo.at[:, there], pair_lo, beside)
    ]
    cents = cents_ref[...]
    first = ((0,), (0,))
    cov_ref[...] = dot(sum_hi[:, here], cents, first) + dot(sum_lo[:, here], cents, first)
    for made in [shown] + halves:
        made.wait_recv()
    cents = pair_cents[...]
    cov_ref[...] += dot(pair_hi[...], cents, first) + dot(pair_lo[...], cents, first)
    cov_ref[0:8, 0:128] = cov_ref[0:8, 0:128] + bad
    for made in started:
        made.wait_send()


def vmem(n):
    return [pl.BlockSpec(memory_space=pltpu.VMEM)] * n


def exchange(labels, points, cents):
    data_ways = lax.axis_size("dp")
    rows, features = cents.shape
    steps = points.shape[0] // CHUNK
    copies = 2 * (data_ways - 1) + 3
    return pl.pallas_call(
        functools.partial(exchange_kernel, rows),
        in_specs=vmem(1) + [pl.BlockSpec(memory_space=pl.ANY)] + vmem(1),
        out_specs=vmem(3),
        out_shape=[
            jax.ShapeDtypeStruct((rows, features), F32),
            jax.ShapeDtypeStruct((8, rows), F32),
            jax.ShapeDtypeStruct((features // 2, features), F32),
        ],
        scratch_shapes=[
            pltpu.VMEM((steps, CHUNK, features), BF16),
            pltpu.VMEM((CHUNK, CHUNK), BF16),
            pltpu.VMEM((steps * data_ways, CHUNK), F32),
            pltpu.VMEM((steps, 1, CHUNK), jnp.int32),
            pltpu.VMEM((steps, 16, CHUNK), BF16),
            pltpu.VMEM((steps * KEEP, features), BF16),
            pltpu.VMEM((16, steps * KEEP), BF16),
            pltpu.VMEM((data_ways, SLOT, features), BF16),
            pltpu.VMEM((data_ways, SLOT, features), BF16),
            pltpu.VMEM((data_ways, 16, SLOT), BF16),
            pltpu.VMEM((data_ways, 16, SLOT), BF16),
            pltpu.VMEM((rows, features), BF16),
            pltpu.VMEM((rows, features), BF16),
            pltpu.VMEM((rows, features // 2), BF16),
            pltpu.VMEM((rows, features // 2), BF16),
            pltpu.VMEM((rows, features), BF16),
            pltpu.SemaphoreType.DMA((steps,)),
            pltpu.SemaphoreType.DMA((copies,)),
            pltpu.SemaphoreType.DMA((copies,)),
        ],
        compiler_params=pltpu.CompilerParams(
            collective_id=0, has_side_effects=True, vmem_limit_bytes=40 << 20
        ),
        name="exchange",
    )(labels.reshape(steps, 1, CHUNK), points, cents)


def settle_kernel(
    part_ref, sums_ref, count_ref, cents_ref, rot_ref, new_ref, got1, got2, got3, acc, own, hx, lx, top, low, square,
    sum_hi, sum_lo, counts, fresh, send, recv, tile_send, tile_recv,
):
    xyz, core = place()
    panel = lax.axis_index("cent")
    features = part_ref.shape[1]
    mine = features // 2
    tile = 256
    tiles = features // tile
    barrier = pltpu.get_barrier_semaphore()
    other = device(xyz, 1 - core)
    partners = [other] + [
        device(moved(xyz, axis, by), core) for axis in range(3) for by in range(1, WAYS)
    ]
    for partner in partners:
        pl.semaphore_signal(barrier, inc=1, device_id=partner, device_id_type=MESH)
    pl.semaphore_wait(barrier, len(partners))

    used = [0]
    started = []

    def remote(src, dst, s, r, to):
        made = pltpu.make_async_remote_copy(
            src_ref=src, dst_ref=dst, send_sem=s, recv_sem=r, device_id=to, device_id_type=MESH
        )
        started.append(made)
        return made

    def copy(src, dst, to):
        n = used[0]
        used[0] += 1
        made = remote(src, dst, send.at[n], recv.at[n], to)
        made.start()
        return made

    here = pl.multiple_of(core * mine, mine)
    parts = range(len(LANES))
    lanes = [pl.ds(lane, width) for lane, width in LANES]
    sizes = [mine // WAYS ** (stage + 1) for stage in range(2)]
    gots = (got1, got2)
    base = [0, 0, 0]

    def scatter(stage, part):
        size, axis = sizes[stage], (part + stage) % 3
        made = []
        for by in range(1, WAYS):
            to = moved(xyz, axis, by)
            start = pl.multiple_of(base[part] + to[axis] * size, size)
            made.append(
                copy(
                    (acc if stage else part_ref).at[pl.ds(start, size), lanes[part]],
                    gots[stage].at[by - 1, :, lanes[part]],
                    device(to, core),
                )
            )
        return made

    def spread(stage, part):
        size, axis = sizes[stage], (part + stage) % 3
        span = own.at[pl.ds(pl.multiple_of(base[part], size), size), lanes[part]]
        made = [copy(span, span, device(moved(xyz, axis, by), core)) for by in range(1, WAYS)]
        base[part] = base[part] - xyz[axis] * size
        return made

    def share(part):
        span = acc.at[pl.ds(base[part], sizes[1]), lanes[part]]
        return [
            copy(span, got3.at[by - 1, :, lanes[part]], device(moved(xyz, (part + 2) % 3, by), core))
            for by in range(1, WAYS)
        ]

    def arrived(part):
        for made in waits[part]:
            made.wait_recv()

    waits = [scatter(0, part) for part in parts]

    sum_hi[...], sum_lo[...] = split(sums_ref[...])
    unit = jnp.where(iota((8, 128), 0) == 0, 1.0, 0.0)
    counts[...] = lax.dot_general(
        count_ref[...], unit, (((0,), (0,)), ((), ())),
        precision=lax.Precision.HIGHEST, preferred_element_type=F32,
    )

    for stage in range(2):
        size = sizes[stage]
        for part in parts:
            arrived(part)
            base[part] = pl.multiple_of(base[part] + xyz[(part + stage) % 3] * size, size)
            at = (pl.ds(base[part], size), lanes[part])
            total = (acc if stage else part_ref)[at]
            for by in range(1, WAYS):
                total = total + gots[stage][by - 1, :, lanes[part]]
            acc[at] = total
            waits[part] = share(part) if stage else scatter(1, part)
    for part in parts:
        arrived(part)
        at = (pl.ds(base[part], sizes[1]), lanes[part])
        own[at] = (acc[at] + got3[1, :, lanes[part]]) + (
            got3[0, :, lanes[part]] + got3[2, :, lanes[part]]
        )
        waits[part] = spread(1, part)
    for part in parts:
        arrived(part)
        waits[part] = spread(0, part)
    squares = jnp.zeros((1, 1), F32)
    for part in parts:
        arrived(part)
        at = (slice(0, mine), lanes[part])
        value = own[at]
        hx[0, 0:mine, lanes[part]], lx[0, 0:mine, lanes[part]] = split(value)
        waits[part] = [
            copy(ref.at[0, pl.ds(0, mine), lanes[part]], ref.at[0, pl.ds(mine, mine), lanes[part]], other)
            for ref in (hx, lx)
        ]
        squares = squares + jnp.sum(
            jnp.sum(value * value, axis=0, keepdims=True), axis=1, keepdims=True
        )
    square[0] = jnp.broadcast_to(squares, square.shape[1:])
    waits.append([copy(square.at[0], square.at[1], other)])

    def sent(step, b, c, ref):
        cols = pl.ds(pl.multiple_of(c * tile, tile), tile)
        if step == NS_STEPS - 1:
            src, dst = own.at[:, cols], rot_ref.at[pl.ds(here, mine), cols]
        else:
            src = ref.at[(step + 1) % 2, pl.ds(0, mine), cols]
            dst = ref.at[(step + 1) % 2, pl.ds(mine, mine), cols]
        return pltpu.make_async_remote_copy(
            src_ref=src, dst_ref=dst, send_sem=tile_send.at[step, b, c],
            recv_sem=tile_recv.at[step, b, c], device_id=other, device_id_type=MESH,
        )

    both = ((1,), (1,))
    keep, turned = 1.5, 0.5
    for step in range(NS_STEPS):
        now, later = step % 2, (step + 1) % 2

        def inner(j):
            rows = pl.ds(pl.multiple_of(j * tile, tile), tile)
            hi, lo = hx[now, 0:mine, :], lx[now, 0:mine, :]
            there_hi = hx[now, rows, :]
            value = dot(hi, there_hi, both) + (
                dot(hi, lx[now, rows, :], both) + dot(lo, there_hi, both)
            )
            top[:, rows], low[:, rows] = split(value)

        pl.loop(0, tiles // 2)(inner)
        if step == 0:
            for row in waits:
                for made in row:
                    made.wait_recv()
            for made in started:
                made.wait_send()
            total = square[0, 0:1, 0:1] + square[1, 0:1, 0:1]
            inverse = 1.0 / (3.0 * jnp.sqrt(total / features + epsilon))
            keep, turned = 1.5 * inverse, 0.5 * inverse * inverse * inverse
        else:
            keep, turned = 1.5, 0.5
            for c in range(tiles):
                for b, ref in enumerate((hx, lx)):
                    sent(step - 1, b, c, ref).wait()
        pl.loop(tiles // 2, tiles)(inner)

        def update(c):
            cols = pl.ds(pl.multiple_of(c * tile, tile), tile)
            hi = hx[now, :, cols]
            turn = dot(top[...], hi) + (dot(top[...], lx[now, :, cols]) + dot(low[...], hi))
            value = keep * own[:, cols] - turned * turn
            own[:, cols] = value
            if step == NS_STEPS - 1:
                rot_ref[pl.ds(here, mine), cols] = value
                sent(step, 0, c, None).start()
            else:
                hx[later, 0:mine, cols], lx[later, 0:mine, cols] = split(value)
                for b, ref in enumerate((hx, lx)):
                    sent(step, b, c, ref).start()

        if step < NS_STEPS - 1:
            pl.loop(0, tiles)(update)

    begun = len(started)
    rings = []
    span = features // RINGS
    per = tiles // RINGS
    for c in range(tiles + 1):
        if c < tiles:
            update(c)
        if c and c % per == 0:
            for done in range(c - per, c):
                sent(NS_STEPS - 1, 0, done, None).wait()
            cols = slice((c - per) * tile, c * tile)
            rot_hi, rot_lo = split(rot_ref[:, cols])
            moved_rows = dot(sum_hi[...], rot_hi) + (
                dot(sum_hi[...], rot_lo) + dot(sum_lo[...], rot_hi)
            )
            value = (
                (moved_rows + cents_ref[:, cols].astype(F32)) / (counts[:, 0:1] + 1.0)
            ).astype(BF16)
            fresh[:, cols] = value
            ring = Ring(copy, xyz, core, fresh, new_ref, pl.ds((c - per) * tile, span))
            ring.begin()
            rings.append(ring)
    rows = fresh.shape[0]
    new_ref[pl.ds(pl.multiple_of(lax.axis_index("cent") * rows, rows), rows), :] = fresh[...]
    for ring in rings:
        ring.forward()
    for ring in rings:
        ring.last()
    for ring in rings:
        ring.finish()
    for made in started[begun:]:
        made.wait_send()


def settle(part, sums, count, cents):
    features = part.shape[1]
    panel_ways = 2 * WAYS
    mine = features // 2
    sizes = [mine // WAYS**n for n in (1, 2, 2)]
    copies = 5 * 3 * (WAYS - 1) + 2 * 3 + 1 + RING * RINGS
    return pl.pallas_call(
        settle_kernel,
        in_specs=vmem(4),
        out_specs=vmem(2),
        out_shape=[
            jax.ShapeDtypeStruct((features, features), F32),
            jax.ShapeDtypeStruct((panel_ways * sums.shape[0], features), BF16),
        ],
        scratch_shapes=[pltpu.VMEM((WAYS - 1, size, features), F32) for size in sizes]
        + [pltpu.VMEM((mine, features), F32)] * 2
        + [pltpu.VMEM((2, features, features), BF16)] * 2
        + [pltpu.VMEM((mine, features), BF16)] * 2
        + [pltpu.VMEM((2, 8, 128), F32)]
        + [pltpu.VMEM(cents.shape, BF16)] * 2
        + [pltpu.VMEM((cents.shape[0], 128), F32), pltpu.VMEM(cents.shape, BF16)]
        + [pltpu.SemaphoreType.DMA((copies,))] * 2
        + [pltpu.SemaphoreType.DMA((NS_STEPS, 2, features // 256))] * 2,
        compiler_params=pltpu.CompilerParams(
            collective_id=1, has_side_effects=True, vmem_limit_bytes=28 << 20
        ),
        name="settle",
    )(part, sums, count, cents)


def emit_kernel(new_ref, rot_ref, new_out, rot_out, bad_ref, done):
    copies = [
        pltpu.make_async_copy(src, dst, done.at[n])
        for n, (src, dst) in enumerate(((new_ref, new_out), (rot_ref, rot_out)))
    ]
    for made in copies:
        made.start()
    bad_ref[...] = jnp.where(jnp.abs(rot_ref[0:1, 0:1]) < jnp.inf, 0, 1)
    for made in copies:
        made.wait()


def emit(new, rot):
    return pl.pallas_call(
        emit_kernel,
        in_specs=vmem(2),
        out_specs=[pl.BlockSpec(memory_space=pltpu.HBM)] * 2 + vmem(1),
        out_shape=[
            jax.ShapeDtypeStruct(new.shape, new.dtype),
            jax.ShapeDtypeStruct(rot.shape, rot.dtype),
            jax.ShapeDtypeStruct((1, 1), jnp.int32),
        ],
        scratch_shapes=[pltpu.SemaphoreType.DMA((2,))],
        compiler_params=pltpu.CompilerParams(vmem_limit_bytes=16 << 20),
        name="emit",
    )(new, rot)


def summed(x, axes, ways):
    parts = lax.all_to_all(x, axes, 0, 0, tiled=True)
    return jnp.sum(parts.reshape(ways, x.shape[0] // ways, *x.shape[1:]), axis=0)


def joined(x, axes, ways):
    copies = jnp.broadcast_to(x[None], (ways, *x.shape)).reshape(ways * x.shape[0], *x.shape[1:])
    return lax.all_to_all(copies, axes, 0, 0, tiled=True)


def dense(points, labels, centroids):
    data_ways = lax.axis_size("dp")
    panel_ways = lax.axis_size("cent")
    block_rows = centroids.shape[0]
    features = points.shape[1]
    column = lax.axis_index("cent")
    owner_block = labels // block_rows
    inside = owner_block % panel_ways == column
    slot_index = jnp.where(
        inside, owner_block // panel_ways * block_rows + labels % block_rows, data_ways * block_rows
    )
    vectors = points.astype(F32)
    local_sums = jax.ops.segment_sum(vectors, slot_index, num_segments=data_ways * block_rows)
    local_counts = jax.ops.segment_sum(
        jnp.ones((*labels.shape, 128), F32), slot_index, num_segments=data_ways * block_rows
    )[:, 0]
    label_sums = summed(local_sums, "dp", data_ways)
    label_counts = summed(local_counts, "dp", data_ways)
    old_rows = centroids.astype(F32)
    part = lax.dot_general(
        label_sums, old_rows, (((0,), (0,)), ((), ())), precision=lax.Precision.HIGHEST
    )
    every = ("dp", "cent")
    cross_cov = joined(
        summed(part, every, data_ways * panel_ways), every, data_ways * panel_ways
    )
    scale_root = jnp.sqrt(jnp.sum(cross_cov * cross_cov) / features + epsilon)
    rotation = cross_cov / (3.0 * scale_root)
    for iteration in range(NS_STEPS):
        inner_prod = jnp.dot(rotation, rotation.T, precision=lax.Precision.HIGHEST)
        rotation = 1.5 * rotation - 0.5 * jnp.dot(
            inner_prod, rotation, precision=lax.Precision.HIGHEST
        )
    rotated_sums = jnp.dot(label_sums, rotation, precision=lax.Precision.HIGHEST)
    moved_rows = joined(rotated_sums + old_rows, "cent", panel_ways)
    all_counts = joined(label_counts, "cent", panel_ways)
    return ((moved_rows / (all_counts[:, None] + 1.0)).astype(BF16), rotation)


def local(points, labels, centroids):
    sums, count, part = exchange(labels, points, centroids)
    rotation, new_centroids = settle(part, sums, count, centroids)
    new_centroids, rotation, bad = emit(new_centroids, rotation)
    _, new_centroids, rotation = lax.while_loop(
        lambda state: state[0] > 0,
        lambda state: (jnp.int32(0), *dense(points, labels, centroids)),
        (bad.reshape(()), new_centroids, rotation),
    )
    return new_centroids, rotation


def solution(mesh):
    return jax.shard_map(
        local,
        mesh=mesh,
        in_specs=(P("dp", None), P("dp"), P(("dp", "cent"), None)),
        out_specs=(P("dp", None), P()),
        check_vma=False,
    )
```

```python
import functools

import jax
import jax.numpy as jnp
from jax import lax
from jax.experimental import pallas as pl
from jax.experimental.pallas import tpu as pltpu
from jax.sharding import PartitionSpec as P

MESH = pl.DeviceIdType.MESH
F32 = jnp.float32
BF16 = jnp.bfloat16

NS_STEPS = 3
epsilon = 1e-06

CHUNK = 512
KEEP = 128
CAP = 112
SLOT = 128
WAYS = 4
LANES = ((0, 384), (384, 384), (768, 256))


def dot(a, b, dims=((1,), (0,))):
    return lax.dot_general(a, b, (dims, ((), ())), preferred_element_type=F32)


def split(x):
    hi = x.astype(BF16)
    return hi, (x - hi.astype(F32)).astype(BF16)


def iota(shape, axis):
    return lax.broadcasted_iota(jnp.int32, shape, axis)


def place():
    dp, cent = lax.axis_index("dp"), lax.axis_index("cent")
    x, y, z = cent // 2, cent % 2 * 2 + dp // 8, dp // 2 % 4
    return (x, y, z), dp % 2


def device(xyz, core):
    x, y, z = xyz
    return {"dp": (y % 2 * 4 + z) * 2 + core, "cent": x * 2 + y // 2}


def moved(xyz, axis, by):
    return tuple((c + by) % WAYS if a == axis else c for a, c in enumerate(xyz))


class Ring:
    def __init__(self, copy, xyz, core, fresh, all_ref, lanes):
        self.copy, self.xyz, self.core = copy, xyz, core
        self.fresh, self.all_ref, self.lanes = fresh, all_ref, lanes
        self.right, self.left = moved(xyz, 0, 1), moved(xyz, 0, WAYS - 1)
        self.across = moved(xyz, 1, 2)

    def spot(self, owner, part):
        half = self.all_ref.shape[0] // (4 * WAYS)
        start = ((owner[0] * 2 + owner[1] // 2) * 2 + part) * half
        return self.all_ref.at[pl.ds(pl.multiple_of(start, half), half), self.lanes]

    def send(self, owner, part, to, fresh=False):
        spot = self.spot(owner, part)
        half = spot.shape[0]
        own = self.fresh.at[pl.ds(part * half, half), self.lanes]
        return self.copy(own if fresh else spot, spot, device(to, self.core))

    def begin(self):
        me = self.xyz
        self.over = [self.send(me, 0, self.across, True)]
        self.rights = [self.send(me, 0, self.right, True)]
        self.lefts = [None, self.send(me, 1, self.left, True)]
        self.over.append(self.send(me, 1, self.across, True))
        self.rights.append(self.send(me, 1, self.right, True))
        self.lefts[0] = self.send(me, 0, self.left, True)

    def forward(self):
        self.rights[0].wait_recv()
        self.overs = []
        self.ends = [self.send(self.left, 0, self.right)]
        self.lefts[1].wait_recv()
        self.ends.append(self.send(self.right, 1, self.left))

    def onward(self):
        self.over[0].wait_recv()
        self.rights2 = [self.send(self.across, 0, self.right)]
        self.lefts2 = [self.send(self.across, 0, self.left)]
        self.over[1].wait_recv()
        self.lefts2.append(self.send(self.across, 1, self.left))
        self.rights2.append(self.send(self.across, 1, self.right))

    def last(self):
        opposite = moved(self.xyz, 0, 2)
        for part in range(2):
            self.ends[part].wait_recv()
            self.overs.append(self.send(opposite, part, self.across))

    def finish(self):
        late = [self.rights[1], self.lefts[0]] + self.rights2 + self.lefts2 + self.overs
        for made in late:
            made.wait_recv()


RING = 14
RINGS = 2


def exchange_kernel(
    block_rows, lab_ref, pts_ref, cents_ref, sums_ref, count_ref, cov_ref,
    pts, tri, hits, rank, meta, kept, metas, out, got, out_id, got_id, sum_hi, sum_lo, pair_hi, pair_lo, pair_cents, load, send, recv,
):
    dp, panel = lax.axis_index("dp"), lax.axis_index("cent")
    data_ways, panel_ways = lax.axis_size("dp"), lax.axis_size("cent")
    steps = lab_ref.shape[0]
    yl, z, core = dp // 8, dp // 2 % 4, dp % 2

    def at(dy, dz, dc):
        return {"dp": ((yl + dy) % 2 * 4 + (z + dz) % 4) * 2 + (core + dc) % 2}

    loads = []
    for step in range(steps):
        loads.append(
            pltpu.make_async_copy(
                pts_ref.at[pl.ds(step * CHUNK, CHUNK)], pts.at[step], load.at[step]
            )
        )
        loads[-1].start()
    barrier = pltpu.get_barrier_semaphore()
    for dy in range(2):
        for dz in range(4):
            for dc in range(2):
                if dy or dz or dc:
                    pl.semaphore_signal(
                        barrier, inc=1, device_id=at(dy, dz, dc), device_id_type=MESH
                    )

    tri[...] = jnp.where(
        iota((CHUNK, CHUNK), 0) <= iota((CHUNK, CHUNK), 1), 1.0, 0.0
    ).astype(BF16)
    for step in range(steps):
        block = lab_ref[step] // block_rows
        dest = block // panel_ways
        hits[step * data_ways : (step + 1) * data_ways, :] = jnp.where(
            jnp.logical_and(
                iota((data_ways, CHUNK), 0) == dest, block % panel_ways == panel
            ),
            1.0,
            0.0,
        )
    counts = dot(hits[...].astype(BF16), tri[...])
    carry = jnp.zeros((data_ways, 1), F32)
    most = jnp.zeros((1, 1), F32)
    row = iota((16, CHUNK), 0)
    for step in range(steps):
        hit = hits[step * data_ways : (step + 1) * data_ways, :]
        count = counts[step * data_ways : (step + 1) * data_ways, :]
        order = jnp.sum(
            hit * jnp.sum(count, axis=0, keepdims=True), axis=0, keepdims=True
        )
        rank[step] = order.astype(jnp.int32)
        spot = jnp.sum(hit * (count + carry), axis=0, keepdims=True)
        last = count[:, CHUNK - 1 : CHUNK]
        carry = carry + last
        most = jnp.maximum(most, jnp.sum(last, axis=0, keepdims=True))
        lab = lab_ref[step]
        dest = (lab // block_rows // panel_ways).astype(F32)
        slot = (lab % block_rows + 1).astype(F32)
        meta[step] = jnp.where(
            row == 0,
            dest,
            jnp.where(row == 1, jnp.minimum(spot, 255.0), jnp.where(row == 2, slot, 0.0)),
        ).astype(BF16)
    over = jnp.logical_or(most > KEEP, jnp.max(carry, axis=0, keepdims=True) > CAP)
    bad = jnp.where(over, jnp.inf, 0.0)

    used = [0]
    started = []

    def copy(src, dst, to):
        n = used[0]
        used[0] += 1
        made = pltpu.make_async_remote_copy(
            src_ref=src, dst_ref=dst, send_sem=send.at[n], recv_sem=recv.at[n],
            device_id=to, device_id_type=MESH,
        )
        made.start()
        started.append(made)
        return made

    for step in range(steps):
        pick = jnp.where(iota((KEEP, CHUNK), 0) + 1 == rank[step], 1.0, 0.0).astype(BF16)
        metas[:, step * KEEP : (step + 1) * KEEP] = dot(
            meta[step], pick, ((1,), (1,))
        ).astype(BF16)
        loads[step].wait()
        kept[step * KEEP : (step + 1) * KEEP, :] = dot(pick, pts[step]).astype(BF16)

    pl.semaphore_wait(barrier, data_ways - 1)
    beside = at(0, 0, 1)
    shown = copy(cents_ref, pair_cents, beside)
    places = metas[...]
    whole = places.astype(F32).astype(jnp.int32)
    dests, spots = whole[0:1, :], whole[1:2, :]
    total = places.shape[1]
    arrive = {}
    order = [(1, 2), (0, 2), (1, 1), (0, 3), (1, 3), (0, 1), (1, 0), (0, 0)]
    for dy, dz in order:
        wanted = jnp.concatenate(
            [
                jnp.broadcast_to(
                    jnp.where(dests == at(dy, dz, dc)["dp"], spots, 0), (SLOT, total)
                )
                for dc in range(2)
            ],
            axis=0,
        )
        pick = jnp.where(iota((2 * SLOT, total), 0) % SLOT + 1 == wanted, 1.0, 0.0).astype(BF16)
        rows = dot(pick, kept[...]).astype(BF16)
        ids = dot(places, pick, ((1,), (1,))).astype(BF16)
        for dc in range(2):
            k = (dy * 4 + dz) * 2 + dc
            out[k] = rows[dc * SLOT : (dc + 1) * SLOT, :]
            out_id[k] = ids[:, dc * SLOT : (dc + 1) * SLOT]
            if k:
                to = at(dy, dz, dc)
                arrive[k] = [
                    copy(out_id.at[k], got_id.at[k], to),
                    copy(out.at[k, pl.ds(0, CAP)], got.at[k, pl.ds(0, CAP)], to),
                ]

    rows, features = sums_ref.shape
    got[:, CAP:SLOT, :] = jnp.zeros((data_ways, SLOT - CAP, features), BF16)
    ones = jnp.ones((8, SLOT), BF16)
    across = ((1,), (1,))
    for dy, dz in order[-1:] + order[:-1]:
        for dc in range(2):
            k = (dy * 4 + dz) * 2 + dc
            for made in arrive.get(k, ()):
                made.wait_recv()
            ids = (got_id if k else out_id)[k].astype(F32).astype(jnp.int32)
            pick = jnp.where(iota((rows, SLOT), 0) + 1 == ids[2:3, :], 1.0, 0.0).astype(BF16)
            vectors = (got if k else out)[k]
            if k:
                sums_ref[...] += dot(pick, vectors)
                count_ref[...] += dot(ones, pick, across)
            else:
                sums_ref[...] = dot(pick, vectors)
                count_ref[...] = dot(ones, pick, across)
    mine = features // 2
    here = pl.ds(pl.multiple_of(core * mine, mine), mine)
    there = pl.ds(pl.multiple_of((1 - core) * mine, mine), mine)
    sum_hi[...], sum_lo[...] = split(sums_ref[...])
    halves = [
        copy(sum_hi.at[:, there], pair_hi, beside), copy(sum_lo.at[:, there], pair_lo, beside)
    ]
    cents = cents_ref[...]
    first = ((0,), (0,))
    cov_ref[...] = dot(sum_hi[:, here], cents, first) + dot(sum_lo[:, here], cents, first)
    for made in [shown] + halves:
        made.wait_recv()
    cents = pair_cents[...]
    cov_ref[...] += dot(pair_hi[...], cents, first) + dot(pair_lo[...], cents, first)
    cov_ref[0:8, 0:128] = cov_ref[0:8, 0:128] + bad
    for made in started:
        made.wait_send()


def vmem(n):
    return [pl.BlockSpec(memory_space=pltpu.VMEM)] * n


def exchange(labels, points, cents):
    data_ways = lax.axis_size("dp")
    rows, features = cents.shape
    steps = points.shape[0] // CHUNK
    copies = 2 * (data_ways - 1) + 3
    return pl.pallas_call(
        functools.partial(exchange_kernel, rows),
        in_specs=vmem(1) + [pl.BlockSpec(memory_space=pl.ANY)] + vmem(1),
        out_specs=vmem(3),
        out_shape=[
            jax.ShapeDtypeStruct((rows, features), F32),
            jax.ShapeDtypeStruct((8, rows), F32),
            jax.ShapeDtypeStruct((features // 2, features), F32),
        ],
        scratch_shapes=[
            pltpu.VMEM((steps, CHUNK, features), BF16),
            pltpu.VMEM((CHUNK, CHUNK), BF16),
            pltpu.VMEM((steps * data_ways, CHUNK), F32),
            pltpu.VMEM((steps, 1, CHUNK), jnp.int32),
            pltpu.VMEM((steps, 16, CHUNK), BF16),
            pltpu.VMEM((steps * KEEP, features), BF16),
            pltpu.VMEM((16, steps * KEEP), BF16),
            pltpu.VMEM((data_ways, SLOT, features), BF16),
            pltpu.VMEM((data_ways, SLOT, features), BF16),
            pltpu.VMEM((data_ways, 16, SLOT), BF16),
            pltpu.VMEM((data_ways, 16, SLOT), BF16),
            pltpu.VMEM((rows, features), BF16),
            pltpu.VMEM((rows, features), BF16),
            pltpu.VMEM((rows, features // 2), BF16),
            pltpu.VMEM((rows, features // 2), BF16),
            pltpu.VMEM((rows, features), BF16),
            pltpu.SemaphoreType.DMA((steps,)),
            pltpu.SemaphoreType.DMA((copies,)),
            pltpu.SemaphoreType.DMA((copies,)),
        ],
        compiler_params=pltpu.CompilerParams(
            collective_id=0, has_side_effects=True, vmem_limit_bytes=40 << 20
        ),
        name="exchange",
    )(labels.reshape(steps, 1, CHUNK), points, cents)


def settle_kernel(
    part_ref, sums_ref, count_ref, cents_ref, rot_ref, new_ref, got1, got2, got3, acc, own, hx, lx, top, low, square,
    sum_hi, sum_lo, counts, fresh, send, recv, tile_send, tile_recv,
):
    xyz, core = place()
    panel = lax.axis_index("cent")
    features = part_ref.shape[1]
    mine = features // 2
    tile = 256
    tiles = features // tile
    barrier = pltpu.get_barrier_semaphore()
    other = device(xyz, 1 - core)
    partners = [other] + [
        device(moved(xyz, axis, by), core) for axis in range(3) for by in range(1, WAYS)
    ]
    for partner in partners:
        pl.semaphore_signal(barrier, inc=1, device_id=partner, device_id_type=MESH)
    pl.semaphore_wait(barrier, len(partners))

    used = [0]
    started = []

    def remote(src, dst, s, r, to):
        made = pltpu.make_async_remote_copy(
            src_ref=src, dst_ref=dst, send_sem=s, recv_sem=r, device_id=to, device_id_type=MESH
        )
        started.append(made)
        return made

    def copy(src, dst, to):
        n = used[0]
        used[0] += 1
        made = remote(src, dst, send.at[n], recv.at[n], to)
        made.start()
        return made

    here = pl.multiple_of(core * mine, mine)
    parts = range(len(LANES))
    lanes = [pl.ds(lane, width) for lane, width in LANES]
    sizes = [mine // WAYS ** (stage + 1) for stage in range(2)]
    gots = (got1, got2)
    base = [0, 0, 0]

    def scatter(stage, part):
        size, axis = sizes[stage], (part + stage) % 3
        made = []
        for by in range(1, WAYS):
            to = moved(xyz, axis, by)
            start = pl.multiple_of(base[part] + to[axis] * size, size)
            made.append(
                copy(
                    (acc if stage else part_ref).at[pl.ds(start, size), lanes[part]],
                    gots[stage].at[by - 1, :, lanes[part]],
                    device(to, core),
                )
            )
        return made

    def spread(stage, part):
        size, axis = sizes[stage], (part + stage) % 3
        span = own.at[pl.ds(pl.multiple_of(base[part], size), size), lanes[part]]
        made = [copy(span, span, device(moved(xyz, axis, by), core)) for by in range(1, WAYS)]
        base[part] = base[part] - xyz[axis] * size
        return made

    def share(part):
        span = acc.at[pl.ds(base[part], sizes[1]), lanes[part]]
        return [
            copy(span, got3.at[by - 1, :, lanes[part]], device(moved(xyz, (part + 2) % 3, by), core))
            for by in range(1, WAYS)
        ]

    def arrived(part):
        for made in waits[part]:
            made.wait_recv()

    waits = [scatter(0, part) for part in parts]

    sum_hi[...], sum_lo[...] = split(sums_ref[...])
    unit = jnp.where(iota((8, 128), 0) == 0, 1.0, 0.0)
    counts[...] = lax.dot_general(
        count_ref[...], unit, (((0,), (0,)), ((), ())),
        precision=lax.Precision.HIGHEST, preferred_element_type=F32,
    )

    for stage in range(2):
        size = sizes[stage]
        for part in parts:
            arrived(part)
            base[part] = pl.multiple_of(base[part] + xyz[(part + stage) % 3] * size, size)
            at = (pl.ds(base[part], size), lanes[part])
            total = (acc if stage else part_ref)[at]
            for by in range(1, WAYS):
                total = total + gots[stage][by - 1, :, lanes[part]]
            acc[at] = total
            waits[part] = share(part) if stage else scatter(1, part)
    for part in parts:
        arrived(part)
        at = (pl.ds(base[part], sizes[1]), lanes[part])
        own[at] = (acc[at] + got3[1, :, lanes[part]]) + (
            got3[0, :, lanes[part]] + got3[2, :, lanes[part]]
        )
        waits[part] = spread(1, part)
    for part in parts:
        arrived(part)
        waits[part] = spread(0, part)
    squares = jnp.zeros((1, 1), F32)
    for part in parts:
        arrived(part)
        at = (slice(0, mine), lanes[part])
        value = own[at]
        hx[0, 0:mine, lanes[part]], lx[0, 0:mine, lanes[part]] = split(value)
        waits[part] = [
            copy(ref.at[0, pl.ds(0, mine), lanes[part]], ref.at[0, pl.ds(mine, mine), lanes[part]], other)
            for ref in (hx, lx)
        ]
        squares = squares + jnp.sum(
            jnp.sum(value * value, axis=0, keepdims=True), axis=1, keepdims=True
        )
    square[0] = jnp.broadcast_to(squares, square.shape[1:])
    waits.append([copy(square.at[0], square.at[1], other)])

    def sent(step, b, c, ref):
        cols = pl.ds(pl.multiple_of(c * tile, tile), tile)
        if step == NS_STEPS - 1:
            src, dst = own.at[:, cols], rot_ref.at[pl.ds(here, mine), cols]
        else:
            src = ref.at[(step + 1) % 2, pl.ds(0, mine), cols]
            dst = ref.at[(step + 1) % 2, pl.ds(mine, mine), cols]
        return pltpu.make_async_remote_copy(
            src_ref=src, dst_ref=dst, send_sem=tile_send.at[step, b, c],
            recv_sem=tile_recv.at[step, b, c], device_id=other, device_id_type=MESH,
        )

    both = ((1,), (1,))
    keep, turned = 1.5, 0.5
    for step in range(NS_STEPS):
        now, later = step % 2, (step + 1) % 2

        def inner(j):
            rows = pl.ds(pl.multiple_of(j * tile, tile), tile)
            hi, lo = hx[now, 0:mine, :], lx[now, 0:mine, :]
            there_hi = hx[now, rows, :]
            value = dot(hi, there_hi, both) + (
                dot(hi, lx[now, rows, :], both) + dot(lo, there_hi, both)
            )
            top[:, rows], low[:, rows] = split(value)

        pl.loop(0, tiles // 2)(inner)
        if step == 0:
            for row in waits:
                for made in row:
                    made.wait_recv()
            for made in started:
                made.wait_send()
            total = square[0, 0:1, 0:1] + square[1, 0:1, 0:1]
            inverse = 1.0 / (3.0 * jnp.sqrt(total / features + epsilon))
            keep, turned = 1.5 * inverse, 0.5 * inverse * inverse * inverse
        else:
            keep, turned = 1.5, 0.5
            for c in range(tiles):
                for b, ref in enumerate((hx, lx)):
                    sent(step - 1, b, c, ref).wait()
        pl.loop(tiles // 2, tiles)(inner)

        def update(c):
            cols = pl.ds(pl.multiple_of(c * tile, tile), tile)
            hi = hx[now, :, cols]
            turn = dot(top[...], hi) + (dot(top[...], lx[now, :, cols]) + dot(low[...], hi))
            value = keep * own[:, cols] - turned * turn
            own[:, cols] = value
            if step == NS_STEPS - 1:
                rot_ref[pl.ds(here, mine), cols] = value
                sent(step, 0, c, None).start()
            else:
                hx[later, 0:mine, cols], lx[later, 0:mine, cols] = split(value)
                for b, ref in enumerate((hx, lx)):
                    sent(step, b, c, ref).start()

        if step < NS_STEPS - 1:
            pl.loop(0, tiles)(update)

    begun = len(started)
    rings = []
    span = features // RINGS
    per = tiles // RINGS
    for c in range(tiles + 1):
        if c < tiles:
            update(c)
        if c and c % per == 0:
            for done in range(c - per, c):
                sent(NS_STEPS - 1, 0, done, None).wait()
            cols = slice((c - per) * tile, c * tile)
            rot_hi, rot_lo = split(rot_ref[:, cols])
            moved_rows = dot(sum_hi[...], rot_hi) + (
                dot(sum_hi[...], rot_lo) + dot(sum_lo[...], rot_hi)
            )
            value = (
                (moved_rows + cents_ref[:, cols].astype(F32)) / (counts[:, 0:1] + 1.0)
            ).astype(BF16)
            fresh[:, cols] = value
            ring = Ring(copy, xyz, core, fresh, new_ref, pl.ds((c - per) * tile, span))
            ring.begin()
            rings.append(ring)
    rows = fresh.shape[0]
    new_ref[pl.ds(pl.multiple_of(lax.axis_index("cent") * rows, rows), rows), :] = fresh[...]
    for ring in rings:
        ring.forward()
    for ring in rings:
        ring.onward()
    for ring in rings:
        ring.last()
    for ring in rings:
        ring.finish()
    for made in started[begun:]:
        made.wait_send()


def settle(part, sums, count, cents):
    features = part.shape[1]
    panel_ways = 2 * WAYS
    mine = features // 2
    sizes = [mine // WAYS**n for n in (1, 2, 2)]
    copies = 5 * 3 * (WAYS - 1) + 2 * 3 + 1 + RING * RINGS
    return pl.pallas_call(
        settle_kernel,
        in_specs=vmem(4),
        out_specs=vmem(2),
        out_shape=[
            jax.ShapeDtypeStruct((features, features), F32),
            jax.ShapeDtypeStruct((panel_ways * sums.shape[0], features), BF16),
        ],
        scratch_shapes=[pltpu.VMEM((WAYS - 1, size, features), F32) for size in sizes]
        + [pltpu.VMEM((mine, features), F32)] * 2
        + [pltpu.VMEM((2, features, features), BF16)] * 2
        + [pltpu.VMEM((mine, features), BF16)] * 2
        + [pltpu.VMEM((2, 8, 128), F32)]
        + [pltpu.VMEM(cents.shape, BF16)] * 2
        + [pltpu.VMEM((cents.shape[0], 128), F32), pltpu.VMEM(cents.shape, BF16)]
        + [pltpu.SemaphoreType.DMA((copies,))] * 2
        + [pltpu.SemaphoreType.DMA((NS_STEPS, 2, features // 256))] * 2,
        compiler_params=pltpu.CompilerParams(
            collective_id=1, has_side_effects=True, vmem_limit_bytes=28 << 20
        ),
        name="settle",
    )(part, sums, count, cents)


def emit_kernel(new_ref, rot_ref, new_out, rot_out, bad_ref, done):
    copies = [
        pltpu.make_async_copy(src, dst, done.at[n])
        for n, (src, dst) in enumerate(((new_ref, new_out), (rot_ref, rot_out)))
    ]
    for made in copies:
        made.start()
    bad_ref[...] = jnp.where(jnp.abs(rot_ref[0:1, 0:1]) < jnp.inf, 0, 1)
    for made in copies:
        made.wait()


def emit(new, rot):
    return pl.pallas_call(
        emit_kernel,
        in_specs=vmem(2),
        out_specs=[pl.BlockSpec(memory_space=pltpu.HBM)] * 2 + vmem(1),
        out_shape=[
            jax.ShapeDtypeStruct(new.shape, new.dtype),
            jax.ShapeDtypeStruct(rot.shape, rot.dtype),
            jax.ShapeDtypeStruct((1, 1), jnp.int32),
        ],
        scratch_shapes=[pltpu.SemaphoreType.DMA((2,))],
        compiler_params=pltpu.CompilerParams(vmem_limit_bytes=16 << 20),
        name="emit",
    )(new, rot)


def summed(x, axes, ways):
    parts = lax.all_to_all(x, axes, 0, 0, tiled=True)
    return jnp.sum(parts.reshape(ways, x.shape[0] // ways, *x.shape[1:]), axis=0)


def joined(x, axes, ways):
    copies = jnp.broadcast_to(x[None], (ways, *x.shape)).reshape(ways * x.shape[0], *x.shape[1:])
    return lax.all_to_all(copies, axes, 0, 0, tiled=True)


def dense(points, labels, centroids):
    data_ways = lax.axis_size("dp")
    panel_ways = lax.axis_size("cent")
    block_rows = centroids.shape[0]
    features = points.shape[1]
    column = lax.axis_index("cent")
    owner_block = labels // block_rows
    inside = owner_block % panel_ways == column
    slot_index = jnp.where(
        inside, owner_block // panel_ways * block_rows + labels % block_rows, data_ways * block_rows
    )
    vectors = points.astype(F32)
    local_sums = jax.ops.segment_sum(vectors, slot_index, num_segments=data_ways * block_rows)
    local_counts = jax.ops.segment_sum(
        jnp.ones((*labels.shape, 128), F32), slot_index, num_segments=data_ways * block_rows
    )[:, 0]
    label_sums = summed(local_sums, "dp", data_ways)
    label_counts = summed(local_counts, "dp", data_ways)
    old_rows = centroids.astype(F32)
    part = lax.dot_general(
        label_sums, old_rows, (((0,), (0,)), ((), ())), precision=lax.Precision.HIGHEST
    )
    every = ("dp", "cent")
    cross_cov = joined(
        summed(part, every, data_ways * panel_ways), every, data_ways * panel_ways
    )
    scale_root = jnp.sqrt(jnp.sum(cross_cov * cross_cov) / features + epsilon)
    rotation = cross_cov / (3.0 * scale_root)
    for iteration in range(NS_STEPS):
        inner_prod = jnp.dot(rotation, rotation.T, precision=lax.Precision.HIGHEST)
        rotation = 1.5 * rotation - 0.5 * jnp.dot(
            inner_prod, rotation, precision=lax.Precision.HIGHEST
        )
    rotated_sums = jnp.dot(label_sums, rotation, precision=lax.Precision.HIGHEST)
    moved_rows = joined(rotated_sums + old_rows, "cent", panel_ways)
    all_counts = joined(label_counts, "cent", panel_ways)
    return ((moved_rows / (all_counts[:, None] + 1.0)).astype(BF16), rotation)


def local(points, labels, centroids):
    sums, count, part = exchange(labels, points, centroids)
    rotation, new_centroids = settle(part, sums, count, centroids)
    new_centroids, rotation, bad = emit(new_centroids, rotation)
    _, new_centroids, rotation = lax.while_loop(
        lambda state: state[0] > 0,
        lambda state: (jnp.int32(0), *dense(points, labels, centroids)),
        (bad.reshape(()), new_centroids, rotation),
    )
    return new_centroids, rotation


def solution(mesh):
    return jax.shard_map(
        local,
        mesh=mesh,
        in_specs=(P("dp", None), P("dp"), P(("dp", "cent"), None)),
        out_specs=(P("dp", None), P()),
        check_vma=False,
    )
```

```python
import functools

import jax
import jax.numpy as jnp
from jax import lax
from jax.experimental import pallas as pl
from jax.experimental.pallas import tpu as pltpu
from jax.sharding import PartitionSpec as P

MESH = pl.DeviceIdType.MESH
F32 = jnp.float32
BF16 = jnp.bfloat16

NS_STEPS = 3
epsilon = 1e-06

CHUNK = 512
KEEP = 128
HALF = 96
SLOT = 128
WAYS = 4
LANES = ((0, 384), (384, 384), (768, 256))


def dot(a, b, dims=((1,), (0,))):
    return lax.dot_general(a, b, (dims, ((), ())), preferred_element_type=F32)


def split(x):
    hi = x.astype(BF16)
    return hi, (x - hi.astype(F32)).astype(BF16)


def iota(shape, axis):
    return lax.broadcasted_iota(jnp.int32, shape, axis)


def place():
    dp, cent = lax.axis_index("dp"), lax.axis_index("cent")
    x, y, z = cent // 2, cent % 2 * 2 + dp // 8, dp // 2 % 4
    return (x, y, z), dp % 2


def device(xyz, core):
    x, y, z = xyz
    return {"dp": (y % 2 * 4 + z) * 2 + core, "cent": x * 2 + y // 2}


def moved(xyz, axis, by):
    return tuple((c + by) % WAYS if a == axis else c for a, c in enumerate(xyz))


class Ring:
    def __init__(self, copy, xyz, core, fresh, all_ref, lanes):
        self.copy, self.xyz, self.core = copy, xyz, core
        self.fresh, self.all_ref, self.lanes = fresh, all_ref, lanes
        self.right, self.left = moved(xyz, 0, 1), moved(xyz, 0, WAYS - 1)
        self.across = moved(xyz, 1, 2)

    def spot(self, owner, part):
        half = self.all_ref.shape[0] // (4 * WAYS)
        start = ((owner[0] * 2 + owner[1] // 2) * 2 + part) * half
        return self.all_ref.at[pl.ds(pl.multiple_of(start, half), half), self.lanes]

    def send(self, owner, part, to, fresh=False):
        spot = self.spot(owner, part)
        half = spot.shape[0]
        own = self.fresh.at[pl.ds(part * half, half), self.lanes]
        return self.copy(own if fresh else spot, spot, device(to, self.core))

    def begin(self):
        me = self.xyz
        self.over = [self.send(me, 0, self.across, True)]
        self.rights = [self.send(me, 0, self.right, True)]
        self.lefts = [None, self.send(me, 1, self.left, True)]
        self.over.append(self.send(me, 1, self.across, True))
        self.rights.append(self.send(me, 1, self.right, True))
        self.lefts[0] = self.send(me, 0, self.left, True)

    def forward(self):
        self.rights[0].wait_recv()
        self.overs = []
        self.ends = [self.send(self.left, 0, self.right)]
        self.lefts[1].wait_recv()
        self.ends.append(self.send(self.right, 1, self.left))

    def onward(self):
        self.over[0].wait_recv()
        self.rights2 = [self.send(self.across, 0, self.right)]
        self.lefts2 = [self.send(self.across, 0, self.left)]
        self.over[1].wait_recv()
        self.lefts2.append(self.send(self.across, 1, self.left))
        self.rights2.append(self.send(self.across, 1, self.right))

    def last(self):
        opposite = moved(self.xyz, 0, 2)
        for part in range(2):
            self.ends[part].wait_recv()
            self.overs.append(self.send(opposite, part, self.across))

    def finish(self):
        late = [self.rights[1], self.lefts[0]] + self.rights2 + self.lefts2 + self.overs
        for made in late:
            made.wait_recv()


RING = 14
RINGS = 2


def exchange_kernel(
    block_rows, lab_ref, pts_ref, cents_ref, sums_ref, count_ref, cov_ref,
    pts, tri, hits, rank, meta, kept, metas, out, got, via, out_id, got_id, via_id, sum_hi, sum_lo, pair_hi, pair_lo, pair_cents, load, send, recv,
):
    dp, panel = lax.axis_index("dp"), lax.axis_index("cent")
    data_ways, panel_ways = lax.axis_size("dp"), lax.axis_size("cent")
    steps = lab_ref.shape[0]
    yl, z, core = dp // 8, dp // 2 % 4, dp % 2

    def at(dy, dz, dc):
        return {"dp": ((yl + dy) % 2 * 4 + (z + dz) % 4) * 2 + (core + dc) % 2}

    def chip_at(dy, dz):
        return (yl + dy) % 2 * 4 + (z + dz) % 4

    chips = data_ways // 2
    loads = []
    for step in range(steps):
        loads.append(
            pltpu.make_async_copy(
                pts_ref.at[pl.ds(step * CHUNK, CHUNK)], pts.at[step], load.at[step]
            )
        )
        loads[-1].start()
    barrier = pltpu.get_barrier_semaphore()
    for dy in range(2):
        for dz in range(4):
            for dc in range(2):
                if dy or dz or dc:
                    pl.semaphore_signal(
                        barrier, inc=1, device_id=at(dy, dz, dc), device_id_type=MESH
                    )

    tri[...] = jnp.where(
        iota((CHUNK, CHUNK), 0) <= iota((CHUNK, CHUNK), 1), 1.0, 0.0
    ).astype(BF16)
    for step in range(steps):
        block = lab_ref[step] // block_rows
        dest = block // panel_ways // 2
        hits[step * chips : (step + 1) * chips, :] = jnp.where(
            jnp.logical_and(
                iota((chips, CHUNK), 0) == dest, block % panel_ways == panel
            ),
            1.0,
            0.0,
        )
    counts = dot(hits[...].astype(BF16), tri[...])
    carry = jnp.zeros((chips, 1), F32)
    most = jnp.zeros((1, 1), F32)
    row = iota((16, CHUNK), 0)
    for step in range(steps):
        hit = hits[step * chips : (step + 1) * chips, :]
        count = counts[step * chips : (step + 1) * chips, :]
        order = jnp.sum(
            hit * jnp.sum(count, axis=0, keepdims=True), axis=0, keepdims=True
        )
        rank[step] = order.astype(jnp.int32)
        spot = jnp.sum(hit * (count + carry), axis=0, keepdims=True)
        last = count[:, CHUNK - 1 : CHUNK]
        carry = carry + last
        most = jnp.maximum(most, jnp.sum(last, axis=0, keepdims=True))
        lab = lab_ref[step]
        dest = lab // block_rows // panel_ways
        slot = (lab % block_rows + 1).astype(F32)
        meta[step] = jnp.where(
            row == 0,
            (dest // 2).astype(F32),
            jnp.where(
                row == 1,
                jnp.minimum(spot, 255.0),
                jnp.where(row == 2, slot, jnp.where(row == 3, (dest % 2).astype(F32), 0.0)),
            ),
        ).astype(BF16)
    over = jnp.logical_or(most > KEEP, jnp.max(carry, axis=0, keepdims=True) > 2 * HALF)
    bad = jnp.where(over, jnp.inf, 0.0)

    used = [0]
    started = []

    def copy(src, dst, to):
        n = used[0]
        used[0] += 1
        made = pltpu.make_async_remote_copy(
            src_ref=src, dst_ref=dst, send_sem=send.at[n], recv_sem=recv.at[n],
            device_id=to, device_id_type=MESH,
        )
        made.start()
        started.append(made)
        return made

    for step in range(steps):
        pick = jnp.where(iota((KEEP, CHUNK), 0) + 1 == rank[step], 1.0, 0.0).astype(BF16)
        metas[:, step * KEEP : (step + 1) * KEEP] = dot(
            meta[step], pick, ((1,), (1,))
        ).astype(BF16)
        loads[step].wait()
        kept[step * KEEP : (step + 1) * KEEP, :] = dot(pick, pts[step]).astype(BF16)

    pl.semaphore_wait(barrier, data_ways - 1)
    beside = at(0, 0, 1)
    shown = copy(cents_ref, pair_cents, beside)
    places = metas[...]
    whole = places.astype(F32).astype(jnp.int32)
    dests, spots = whole[0:1, :], whole[1:2, :]
    arrive, passed = {}, {}
    order = [(1, 2), (0, 2), (1, 1), (0, 3), (1, 3), (0, 1), (1, 0), (0, 0)]
    row = iota((2 * SLOT, 1), 0)
    target = jnp.where(row % SLOT < HALF, row // SLOT * HALF + row % SLOT + 1, -1)
    used_rows = pl.ds(0, HALF)
    for dy, dz in order:
        k = dy * 4 + dz
        wanted = jnp.where(dests == chip_at(dy, dz), spots, 0)
        pick = jnp.where(target == wanted, 1.0, 0.0).astype(BF16)
        rows = dot(pick, kept[...]).astype(BF16)
        ids = dot(places, pick, ((1,), (1,))).astype(BF16)
        for n in range(2):
            out[k, n] = rows[n * SLOT : (n + 1) * SLOT, :]
            out_id[k, n] = ids[:, n * SLOT : (n + 1) * SLOT]
        if k == 0:
            passed[k] = [
                copy(out_id.at[k], via_id.at[k], beside),
                copy(out.at[k, :, used_rows], via.at[k, :, used_rows], beside),
            ]
            continue
        arrive[k] = []
        for dc in range(2):
            n, to = (core + dc) % 2, at(dy, dz, dc)
            arrive[k].append(copy(out_id.at[k, n], got_id.at[k, dc], to))
            arrive[k].append(
                copy(out.at[k, n, used_rows], got.at[k, dc, used_rows], to)
            )

    rows, features = sums_ref.shape
    got[:, :, HALF:SLOT, :] = jnp.zeros((chips, 2, SLOT - HALF, features), BF16)
    via[:, :, HALF:SLOT, :] = jnp.zeros((chips, 2, SLOT - HALF, features), BF16)
    ones = jnp.ones((8, 2 * SLOT), BF16)
    across = ((1,), (1,))

    def add(vectors, ids, fresh=False):
        whole = ids.astype(F32).astype(jnp.int32)
        slots = [jnp.where(whole[n, 3:4, :] == core, whole[n, 2:3, :], 0) for n in range(2)]
        pick = jnp.where(
            iota((rows, 2 * SLOT), 0) + 1 == jnp.concatenate(slots, axis=1), 1.0, 0.0
        ).astype(BF16)
        value = dot(pick, vectors.reshape(2 * SLOT, features))
        number = dot(ones, pick, across)
        if fresh:
            sums_ref[...], count_ref[...] = value, number
        else:
            sums_ref[...] += value
            count_ref[...] += number

    add(out[0], out_id[0], True)
    before = 0
    for dy, dz in order[:-1]:
        k = dy * 4 + dz
        for made in arrive[k]:
            made.wait_recv()
        passed[k] = [
            copy(got_id.at[k], via_id.at[k], beside),
            copy(got.at[k, :, used_rows], via.at[k, :, used_rows], beside),
        ]
        add(got[k], got_id[k])
        for made in passed[before]:
            made.wait_recv()
        add(via[before], via_id[before])
        before = k
    for made in passed[before]:
        made.wait_recv()
    add(via[before], via_id[before])
    mine = features // 2
    here = pl.ds(pl.multiple_of(core * mine, mine), mine)
    there = pl.ds(pl.multiple_of((1 - core) * mine, mine), mine)
    sum_hi[...], sum_lo[...] = split(sums_ref[...])
    halves = [
        copy(sum_hi.at[:, there], pair_hi, beside), copy(sum_lo.at[:, there], pair_lo, beside)
    ]
    cents = cents_ref[...]
    first = ((0,), (0,))
    cov_ref[...] = dot(sum_hi[:, here], cents, first) + dot(sum_lo[:, here], cents, first)
    for made in [shown] + halves:
        made.wait_recv()
    cents = pair_cents[...]
    cov_ref[...] += dot(pair_hi[...], cents, first) + dot(pair_lo[...], cents, first)
    cov_ref[0:8, 0:128] = cov_ref[0:8, 0:128] + bad
    for made in started:
        made.wait_send()


def vmem(n):
    return [pl.BlockSpec(memory_space=pltpu.VMEM)] * n


def exchange(labels, points, cents):
    data_ways = lax.axis_size("dp")
    rows, features = cents.shape
    steps = points.shape[0] // CHUNK
    copies = 4 * (data_ways // 2 - 1) + data_ways + 3
    return pl.pallas_call(
        functools.partial(exchange_kernel, rows),
        in_specs=vmem(1) + [pl.BlockSpec(memory_space=pl.ANY)] + vmem(1),
        out_specs=vmem(3),
        out_shape=[
            jax.ShapeDtypeStruct((rows, features), F32),
            jax.ShapeDtypeStruct((8, rows), F32),
            jax.ShapeDtypeStruct((features // 2, features), F32),
        ],
        scratch_shapes=[
            pltpu.VMEM((steps, CHUNK, features), BF16),
            pltpu.VMEM((CHUNK, CHUNK), BF16),
            pltpu.VMEM((steps * data_ways // 2, CHUNK), F32),
            pltpu.VMEM((steps, 1, CHUNK), jnp.int32),
            pltpu.VMEM((steps, 16, CHUNK), BF16),
            pltpu.VMEM((steps * KEEP, features), BF16),
            pltpu.VMEM((16, steps * KEEP), BF16),
            pltpu.VMEM((data_ways // 2, 2, SLOT, features), BF16),
            pltpu.VMEM((data_ways // 2, 2, SLOT, features), BF16),
            pltpu.VMEM((data_ways // 2, 2, SLOT, features), BF16),
            pltpu.VMEM((data_ways // 2, 2, 16, SLOT), BF16),
            pltpu.VMEM((data_ways // 2, 2, 16, SLOT), BF16),
            pltpu.VMEM((data_ways // 2, 2, 16, SLOT), BF16),
            pltpu.VMEM((rows, features), BF16),
            pltpu.VMEM((rows, features), BF16),
            pltpu.VMEM((rows, features // 2), BF16),
            pltpu.VMEM((rows, features // 2), BF16),
            pltpu.VMEM((rows, features), BF16),
            pltpu.SemaphoreType.DMA((steps,)),
            pltpu.SemaphoreType.DMA((copies,)),
            pltpu.SemaphoreType.DMA((copies,)),
        ],
        compiler_params=pltpu.CompilerParams(
            collective_id=0, has_side_effects=True, vmem_limit_bytes=46 << 20
        ),
        name="exchange",
    )(labels.reshape(steps, 1, CHUNK), points, cents)


def settle_kernel(
    part_ref, sums_ref, count_ref, cents_ref, rot_ref, new_ref, got1, got2, got3, acc, own, hx, lx, top, low, square,
    sum_hi, sum_lo, counts, fresh, send, recv, tile_send, tile_recv,
):
    xyz, core = place()
    panel = lax.axis_index("cent")
    features = part_ref.shape[1]
    mine = features // 2
    tile = 256
    tiles = features // tile
    barrier = pltpu.get_barrier_semaphore()
    other = device(xyz, 1 - core)
    partners = [other] + [
        device(moved(xyz, axis, by), core) for axis in range(3) for by in range(1, WAYS)
    ]
    for partner in partners:
        pl.semaphore_signal(barrier, inc=1, device_id=partner, device_id_type=MESH)
    pl.semaphore_wait(barrier, len(partners))

    used = [0]
    started = []

    def remote(src, dst, s, r, to):
        made = pltpu.make_async_remote_copy(
            src_ref=src, dst_ref=dst, send_sem=s, recv_sem=r, device_id=to, device_id_type=MESH
        )
        started.append(made)
        return made

    def copy(src, dst, to):
        n = used[0]
        used[0] += 1
        made = remote(src, dst, send.at[n], recv.at[n], to)
        made.start()
        return made

    here = pl.multiple_of(core * mine, mine)
    parts = range(len(LANES))
    lanes = [pl.ds(lane, width) for lane, width in LANES]
    sizes = [mine // WAYS ** (stage + 1) for stage in range(2)]
    gots = (got1, got2)
    base = [0, 0, 0]

    def scatter(stage, part):
        size, axis = sizes[stage], (part + stage) % 3
        made = []
        for by in range(1, WAYS):
            to = moved(xyz, axis, by)
            start = pl.multiple_of(base[part] + to[axis] * size, size)
            made.append(
                copy(
                    (acc if stage else part_ref).at[pl.ds(start, size), lanes[part]],
                    gots[stage].at[by - 1, :, lanes[part]],
                    device(to, core),
                )
            )
        return made

    def spread(stage, part):
        size, axis = sizes[stage], (part + stage) % 3
        span = own.at[pl.ds(pl.multiple_of(base[part], size), size), lanes[part]]
        made = [copy(span, span, device(moved(xyz, axis, by), core)) for by in range(1, WAYS)]
        base[part] = base[part] - xyz[axis] * size
        return made

    def share(part):
        span = acc.at[pl.ds(base[part], sizes[1]), lanes[part]]
        return [
            copy(span, got3.at[by - 1, :, lanes[part]], device(moved(xyz, (part + 2) % 3, by), core))
            for by in range(1, WAYS)
        ]

    def arrived(part):
        for made in waits[part]:
            made.wait_recv()

    waits = [scatter(0, part) for part in parts]

    sum_hi[...], sum_lo[...] = split(sums_ref[...])
    unit = jnp.where(iota((8, 128), 0) == 0, 1.0, 0.0)
    counts[...] = lax.dot_general(
        count_ref[...], unit, (((0,), (0,)), ((), ())),
        precision=lax.Precision.HIGHEST, preferred_element_type=F32,
    )

    for stage in range(2):
        size = sizes[stage]
        for part in parts:
            arrived(part)
            base[part] = pl.multiple_of(base[part] + xyz[(part + stage) % 3] * size, size)
            at = (pl.ds(base[part], size), lanes[part])
            total = (acc if stage else part_ref)[at]
            for by in range(1, WAYS):
                total = total + gots[stage][by - 1, :, lanes[part]]
            acc[at] = total
            waits[part] = share(part) if stage else scatter(1, part)
    for part in parts:
        arrived(part)
        at = (pl.ds(base[part], sizes[1]), lanes[part])
        own[at] = (acc[at] + got3[1, :, lanes[part]]) + (
            got3[0, :, lanes[part]] + got3[2, :, lanes[part]]
        )
        waits[part] = spread(1, part)
    for part in parts:
        arrived(part)
        waits[part] = spread(0, part)
    squares = jnp.zeros((1, 1), F32)
    for part in parts:
        arrived(part)
        at = (slice(0, mine), lanes[part])
        value = own[at]
        hx[0, 0:mine, lanes[part]], lx[0, 0:mine, lanes[part]] = split(value)
        waits[part] = [
            copy(ref.at[0, pl.ds(0, mine), lanes[part]], ref.at[0, pl.ds(mine, mine), lanes[part]], other)
            for ref in (hx, lx)
        ]
        squares = squares + jnp.sum(
            jnp.sum(value * value, axis=0, keepdims=True), axis=1, keepdims=True
        )
    square[0] = jnp.broadcast_to(squares, square.shape[1:])
    waits.append([copy(square.at[0], square.at[1], other)])

    def sent(step, b, c, ref):
        cols = pl.ds(pl.multiple_of(c * tile, tile), tile)
        if step == NS_STEPS - 1:
            src, dst = own.at[:, cols], rot_ref.at[pl.ds(here, mine), cols]
        else:
            src = ref.at[(step + 1) % 2, pl.ds(0, mine), cols]
            dst = ref.at[(step + 1) % 2, pl.ds(mine, mine), cols]
        return pltpu.make_async_remote_copy(
            src_ref=src, dst_ref=dst, send_sem=tile_send.at[step, b, c],
            recv_sem=tile_recv.at[step, b, c], device_id=other, device_id_type=MESH,
        )

    both = ((1,), (1,))
    keep, turned = 1.5, 0.5
    for step in range(NS_STEPS):
        now, later = step % 2, (step + 1) % 2

        def inner(j):
            rows = pl.ds(pl.multiple_of(j * tile, tile), tile)
            hi, lo = hx[now, 0:mine, :], lx[now, 0:mine, :]
            there_hi = hx[now, rows, :]
            value = dot(hi, there_hi, both) + (
                dot(hi, lx[now, rows, :], both) + dot(lo, there_hi, both)
            )
            top[:, rows], low[:, rows] = split(value)

        pl.loop(0, tiles // 2)(inner)
        if step == 0:
            for row in waits:
                for made in row:
                    made.wait_recv()
            for made in started:
                made.wait_send()
            total = square[0, 0:1, 0:1] + square[1, 0:1, 0:1]
            inverse = 1.0 / (3.0 * jnp.sqrt(total / features + epsilon))
            keep, turned = 1.5 * inverse, 0.5 * inverse * inverse * inverse
        else:
            keep, turned = 1.5, 0.5
            for c in range(tiles):
                for b, ref in enumerate((hx, lx)):
                    sent(step - 1, b, c, ref).wait()
        pl.loop(tiles // 2, tiles)(inner)

        def update(c):
            cols = pl.ds(pl.multiple_of(c * tile, tile), tile)
            hi = hx[now, :, cols]
            turn = dot(top[...], hi) + (dot(top[...], lx[now, :, cols]) + dot(low[...], hi))
            value = keep * own[:, cols] - turned * turn
            own[:, cols] = value
            if step == NS_STEPS - 1:
                rot_ref[pl.ds(here, mine), cols] = value
                sent(step, 0, c, None).start()
            else:
                hx[later, 0:mine, cols], lx[later, 0:mine, cols] = split(value)
                for b, ref in enumerate((hx, lx)):
                    sent(step, b, c, ref).start()

        if step < NS_STEPS - 1:
            pl.loop(0, tiles)(update)

    begun = len(started)
    rings = []
    span = features // RINGS
    per = tiles // RINGS
    for c in range(tiles + 1):
        if c < tiles:
            update(c)
        if c and c % per == 0:
            for done in range(c - per, c):
                sent(NS_STEPS - 1, 0, done, None).wait()
            cols = slice((c - per) * tile, c * tile)
            rot_hi, rot_lo = split(rot_ref[:, cols])
            moved_rows = dot(sum_hi[...], rot_hi) + (
                dot(sum_hi[...], rot_lo) + dot(sum_lo[...], rot_hi)
            )
            value = (
                (moved_rows + cents_ref[:, cols].astype(F32)) / (counts[:, 0:1] + 1.0)
            ).astype(BF16)
            fresh[:, cols] = value
            ring = Ring(copy, xyz, core, fresh, new_ref, pl.ds((c - per) * tile, span))
            ring.begin()
            rings.append(ring)
    rows = fresh.shape[0]
    new_ref[pl.ds(pl.multiple_of(lax.axis_index("cent") * rows, rows), rows), :] = fresh[...]
    for ring in rings:
        ring.forward()
    for ring in rings:
        ring.onward()
    for ring in rings:
        ring.last()
    for ring in rings:
        ring.finish()
    for made in started[begun:]:
        made.wait_send()


def settle(part, sums, count, cents):
    features = part.shape[1]
    panel_ways = 2 * WAYS
    mine = features // 2
    sizes = [mine // WAYS**n for n in (1, 2, 2)]
    copies = 5 * 3 * (WAYS - 1) + 2 * 3 + 1 + RING * RINGS
    return pl.pallas_call(
        settle_kernel,
        in_specs=vmem(4),
        out_specs=vmem(2),
        out_shape=[
            jax.ShapeDtypeStruct((features, features), F32),
            jax.ShapeDtypeStruct((panel_ways * sums.shape[0], features), BF16),
        ],
        scratch_shapes=[pltpu.VMEM((WAYS - 1, size, features), F32) for size in sizes]
        + [pltpu.VMEM((mine, features), F32)] * 2
        + [pltpu.VMEM((2, features, features), BF16)] * 2
        + [pltpu.VMEM((mine, features), BF16)] * 2
        + [pltpu.VMEM((2, 8, 128), F32)]
        + [pltpu.VMEM(cents.shape, BF16)] * 2
        + [pltpu.VMEM((cents.shape[0], 128), F32), pltpu.VMEM(cents.shape, BF16)]
        + [pltpu.SemaphoreType.DMA((copies,))] * 2
        + [pltpu.SemaphoreType.DMA((NS_STEPS, 2, features // 256))] * 2,
        compiler_params=pltpu.CompilerParams(
            collective_id=1, has_side_effects=True, vmem_limit_bytes=28 << 20
        ),
        name="settle",
    )(part, sums, count, cents)


def emit_kernel(new_ref, rot_ref, new_out, rot_out, bad_ref, done):
    copies = [
        pltpu.make_async_copy(src, dst, done.at[n])
        for n, (src, dst) in enumerate(((new_ref, new_out), (rot_ref, rot_out)))
    ]
    for made in copies:
        made.start()
    bad_ref[...] = jnp.where(jnp.abs(rot_ref[0:1, 0:1]) < jnp.inf, 0, 1)
    for made in copies:
        made.wait()


def emit(new, rot):
    return pl.pallas_call(
        emit_kernel,
        in_specs=vmem(2),
        out_specs=[pl.BlockSpec(memory_space=pltpu.HBM)] * 2 + vmem(1),
        out_shape=[
            jax.ShapeDtypeStruct(new.shape, new.dtype),
            jax.ShapeDtypeStruct(rot.shape, rot.dtype),
            jax.ShapeDtypeStruct((1, 1), jnp.int32),
        ],
        scratch_shapes=[pltpu.SemaphoreType.DMA((2,))],
        compiler_params=pltpu.CompilerParams(vmem_limit_bytes=16 << 20),
        name="emit",
    )(new, rot)


def summed(x, axes, ways):
    parts = lax.all_to_all(x, axes, 0, 0, tiled=True)
    return jnp.sum(parts.reshape(ways, x.shape[0] // ways, *x.shape[1:]), axis=0)


def joined(x, axes, ways):
    copies = jnp.broadcast_to(x[None], (ways, *x.shape)).reshape(ways * x.shape[0], *x.shape[1:])
    return lax.all_to_all(copies, axes, 0, 0, tiled=True)


def dense(points, labels, centroids):
    data_ways = lax.axis_size("dp")
    panel_ways = lax.axis_size("cent")
    block_rows = centroids.shape[0]
    features = points.shape[1]
    column = lax.axis_index("cent")
    owner_block = labels // block_rows
    inside = owner_block % panel_ways == column
    slot_index = jnp.where(
        inside, owner_block // panel_ways * block_rows + labels % block_rows, data_ways * block_rows
    )
    vectors = points.astype(F32)
    local_sums = jax.ops.segment_sum(vectors, slot_index, num_segments=data_ways * block_rows)
    local_counts = jax.ops.segment_sum(
        jnp.ones((*labels.shape, 128), F32), slot_index, num_segments=data_ways * block_rows
    )[:, 0]
    label_sums = summed(local_sums, "dp", data_ways)
    label_counts = summed(local_counts, "dp", data_ways)
    old_rows = centroids.astype(F32)
    part = lax.dot_general(
        label_sums, old_rows, (((0,), (0,)), ((), ())), precision=lax.Precision.HIGHEST
    )
    every = ("dp", "cent")
    cross_cov = joined(
        summed(part, every, data_ways * panel_ways), every, data_ways * panel_ways
    )
    scale_root = jnp.sqrt(jnp.sum(cross_cov * cross_cov) / features + epsilon)
    rotation = cross_cov / (3.0 * scale_root)
    for iteration in range(NS_STEPS):
        inner_prod = jnp.dot(rotation, rotation.T, precision=lax.Precision.HIGHEST)
        rotation = 1.5 * rotation - 0.5 * jnp.dot(
            inner_prod, rotation, precision=lax.Precision.HIGHEST
        )
    rotated_sums = jnp.dot(label_sums, rotation, precision=lax.Precision.HIGHEST)
    moved_rows = joined(rotated_sums + old_rows, "cent", panel_ways)
    all_counts = joined(label_counts, "cent", panel_ways)
    return ((moved_rows / (all_counts[:, None] + 1.0)).astype(BF16), rotation)


def local(points, labels, centroids):
    sums, count, part = exchange(labels, points, centroids)
    rotation, new_centroids = settle(part, sums, count, centroids)
    new_centroids, rotation, bad = emit(new_centroids, rotation)
    _, new_centroids, rotation = lax.while_loop(
        lambda state: state[0] > 0,
        lambda state: (jnp.int32(0), *dense(points, labels, centroids)),
        (bad.reshape(()), new_centroids, rotation),
    )
    return new_centroids, rotation


def solution(mesh):
    return jax.shard_map(
        local,
        mesh=mesh,
        in_specs=(P("dp", None), P("dp"), P(("dp", "cent"), None)),
        out_specs=(P("dp", None), P()),
        check_vma=False,
    )
```

```python
import functools

import jax
import jax.numpy as jnp
from jax import lax
from jax.experimental import pallas as pl
from jax.experimental.pallas import tpu as pltpu
from jax.sharding import PartitionSpec as P

MESH = pl.DeviceIdType.MESH
F32 = jnp.float32
BF16 = jnp.bfloat16

NS_STEPS = 3
epsilon = 1e-06

CHUNK = 512
KEEP = 128
HALF = 96
SLOT = 128
WAYS = 4
LANES = ((0, 384), (384, 384), (768, 256))


def dot(a, b, dims=((1,), (0,))):
    return lax.dot_general(a, b, (dims, ((), ())), preferred_element_type=F32)


def split(x):
    hi = x.astype(BF16)
    return hi, (x - hi.astype(F32)).astype(BF16)


def iota(shape, axis):
    return lax.broadcasted_iota(jnp.int32, shape, axis)


def place():
    dp, cent = lax.axis_index("dp"), lax.axis_index("cent")
    x, y, z = cent // 2, cent % 2 * 2 + dp // 8, dp // 2 % 4
    return (x, y, z), dp % 2


def device(xyz, core):
    x, y, z = xyz
    return {"dp": (y % 2 * 4 + z) * 2 + core, "cent": x * 2 + y // 2}


def moved(xyz, axis, by):
    return tuple((c + by) % WAYS if a == axis else c for a, c in enumerate(xyz))


class Ring:
    def __init__(self, copy, xyz, core, fresh, all_ref, lanes):
        self.copy, self.xyz, self.core = copy, xyz, core
        self.fresh, self.all_ref, self.lanes = fresh, all_ref, lanes
        self.right, self.left = moved(xyz, 0, 1), moved(xyz, 0, WAYS - 1)
        self.across = moved(xyz, 1, 2)

    def spot(self, owner, part):
        half = self.all_ref.shape[0] // (4 * WAYS)
        start = ((owner[0] * 2 + owner[1] // 2) * 2 + part) * half
        return self.all_ref.at[pl.ds(pl.multiple_of(start, half), half), self.lanes]

    def send(self, owner, part, to, fresh=False):
        spot = self.spot(owner, part)
        half = spot.shape[0]
        own = self.fresh.at[pl.ds(part * half, half), self.lanes]
        return self.copy(own if fresh else spot, spot, device(to, self.core))

    def send_whole(self, owner, to, fresh=False):
        rows = self.all_ref.shape[0] // (2 * WAYS)
        start = (owner[0] * 2 + owner[1] // 2) * rows
        spot = self.all_ref.at[pl.ds(pl.multiple_of(start, rows), rows), self.lanes]
        own = self.fresh.at[:, self.lanes]
        return self.copy(own if fresh else spot, spot, device(to, self.core))

    def begin(self):
        me = self.xyz
        self.over = self.send_whole(me, self.across, True)
        self.rights = [self.send(me, 0, self.right, True)]
        self.lefts = [None, self.send(me, 1, self.left, True)]
        self.rights.append(self.send(me, 1, self.right, True))
        self.lefts[0] = self.send(me, 0, self.left, True)

    def forward(self):
        self.rights[0].wait_recv()
        self.overs = []
        self.ends = [self.send(self.left, 0, self.right)]
        self.lefts[1].wait_recv()
        self.ends.append(self.send(self.right, 1, self.left))

    def onward(self):
        self.over.wait_recv()
        self.beyond = [self.send_whole(self.across, to) for to in (self.right, self.left)]

    def last(self):
        opposite = moved(self.xyz, 0, 2)
        for part in range(2):
            self.ends[part].wait_recv()
            self.overs.append(self.send(opposite, part, self.across))

    def finish(self):
        late = [self.rights[1], self.lefts[0]] + self.beyond + self.overs
        for made in late:
            made.wait_recv()


RING = 11
RINGS = 2


def exchange_kernel(
    block_rows, lab_ref, pts_ref, cents_ref, sums_ref, count_ref, cov_ref,
    pts, tri, hits, rank, meta, kept, metas, out, got, via, out_id, got_id, via_id, sum_hi, sum_lo, pair_hi, pair_lo, pair_cents, load, send, recv,
):
    dp, panel = lax.axis_index("dp"), lax.axis_index("cent")
    data_ways, panel_ways = lax.axis_size("dp"), lax.axis_size("cent")
    steps = lab_ref.shape[0]
    yl, z, core = dp // 8, dp // 2 % 4, dp % 2

    def at(dy, dz, dc):
        return {"dp": ((yl + dy) % 2 * 4 + (z + dz) % 4) * 2 + (core + dc) % 2}

    def chip_at(dy, dz):
        return (yl + dy) % 2 * 4 + (z + dz) % 4

    chips = data_ways // 2
    loads = []
    for step in range(steps):
        loads.append(
            pltpu.make_async_copy(
                pts_ref.at[pl.ds(step * CHUNK, CHUNK)], pts.at[step], load.at[step]
            )
        )
        loads[-1].start()
    barrier = pltpu.get_barrier_semaphore()
    for dy in range(2):
        for dz in range(4):
            for dc in range(2):
                if dy or dz or dc:
                    pl.semaphore_signal(
                        barrier, inc=1, device_id=at(dy, dz, dc), device_id_type=MESH
                    )

    tri[...] = jnp.where(
        iota((CHUNK, CHUNK), 0) <= iota((CHUNK, CHUNK), 1), 1.0, 0.0
    ).astype(BF16)
    for step in range(steps):
        block = lab_ref[step] // block_rows
        dest = block // panel_ways // 2
        hits[step * chips : (step + 1) * chips, :] = jnp.where(
            jnp.logical_and(
                iota((chips, CHUNK), 0) == dest, block % panel_ways == panel
            ),
            1.0,
            0.0,
        )
    counts = dot(hits[...].astype(BF16), tri[...])
    carry = jnp.zeros((chips, 1), F32)
    most = jnp.zeros((1, 1), F32)
    row = iota((16, CHUNK), 0)
    for step in range(steps):
        hit = hits[step * chips : (step + 1) * chips, :]
        count = counts[step * chips : (step + 1) * chips, :]
        order = jnp.sum(
            hit * jnp.sum(count, axis=0, keepdims=True), axis=0, keepdims=True
        )
        rank[step] = order.astype(jnp.int32)
        spot = jnp.sum(hit * (count + carry), axis=0, keepdims=True)
        last = count[:, CHUNK - 1 : CHUNK]
        carry = carry + last
        most = jnp.maximum(most, jnp.sum(last, axis=0, keepdims=True))
        lab = lab_ref[step]
        dest = lab // block_rows // panel_ways
        slot = (lab % block_rows + 1).astype(F32)
        meta[step] = jnp.where(
            row == 0,
            (dest // 2).astype(F32),
            jnp.where(
                row == 1,
                jnp.minimum(spot, 255.0),
                jnp.where(row == 2, slot, jnp.where(row == 3, (dest % 2).astype(F32), 0.0)),
            ),
        ).astype(BF16)
    over = jnp.logical_or(most > KEEP, jnp.max(carry, axis=0, keepdims=True) > 2 * HALF)
    bad = jnp.where(over, jnp.inf, 0.0)

    used = [0]
    started = []

    def copy(src, dst, to):
        n = used[0]
        used[0] += 1
        made = pltpu.make_async_remote_copy(
            src_ref=src, dst_ref=dst, send_sem=send.at[n], recv_sem=recv.at[n],
            device_id=to, device_id_type=MESH,
        )
        made.start()
        started.append(made)
        return made

    for step in range(steps):
        pick = jnp.where(iota((KEEP, CHUNK), 0) + 1 == rank[step], 1.0, 0.0).astype(BF16)
        metas[:, step * KEEP : (step + 1) * KEEP] = dot(
            meta[step], pick, ((1,), (1,))
        ).astype(BF16)
        loads[step].wait()
        kept[step * KEEP : (step + 1) * KEEP, :] = dot(pick, pts[step]).astype(BF16)

    pl.semaphore_wait(barrier, data_ways - 1)
    beside = at(0, 0, 1)
    shown = copy(cents_ref, pair_cents, beside)
    places = metas[...]
    whole = places.astype(F32).astype(jnp.int32)
    dests, spots = whole[0:1, :], whole[1:2, :]
    arrive, passed = {}, {}
    order = [(1, 2), (0, 2), (1, 1), (0, 3), (1, 3), (0, 1), (1, 0), (0, 0)]
    row = iota((2 * SLOT, 1), 0)
    target = jnp.where(row % SLOT < HALF, row // SLOT * HALF + row % SLOT + 1, -1)
    used_rows = pl.ds(0, HALF)
    for dy, dz in order:
        k = dy * 4 + dz
        wanted = jnp.where(dests == chip_at(dy, dz), spots, 0)
        pick = jnp.where(target == wanted, 1.0, 0.0).astype(BF16)
        rows = dot(pick, kept[...]).astype(BF16)
        ids = dot(places, pick, ((1,), (1,))).astype(BF16)
        for n in range(2):
            out[k, n] = rows[n * SLOT : (n + 1) * SLOT, :]
            out_id[k, n] = ids[:, n * SLOT : (n + 1) * SLOT]
        if k == 0:
            passed[k] = [
                copy(out_id.at[k], via_id.at[k], beside),
                copy(out.at[k, :, used_rows], via.at[k, :, used_rows], beside),
            ]
            continue
        arrive[k] = []
        for dc in range(2):
            n, to = (core + dc) % 2, at(dy, dz, dc)
            arrive[k].append(copy(out_id.at[k, n], got_id.at[k, dc], to))
            arrive[k].append(
                copy(out.at[k, n, used_rows], got.at[k, dc, used_rows], to)
            )

    rows, features = sums_ref.shape
    got[:, :, HALF:SLOT, :] = jnp.zeros((chips, 2, SLOT - HALF, features), BF16)
    via[:, :, HALF:SLOT, :] = jnp.zeros((chips, 2, SLOT - HALF, features), BF16)
    ones = jnp.ones((8, 2 * SLOT), BF16)
    across = ((1,), (1,))

    def add(vectors, ids, fresh=False):
        whole = ids.astype(F32).astype(jnp.int32)
        slots = [jnp.where(whole[n, 3:4, :] == core, whole[n, 2:3, :], 0) for n in range(2)]
        pick = jnp.where(
            iota((rows, 2 * SLOT), 0) + 1 == jnp.concatenate(slots, axis=1), 1.0, 0.0
        ).astype(BF16)
        value = dot(pick, vectors.reshape(2 * SLOT, features))
        number = dot(ones, pick, across)
        if fresh:
            sums_ref[...], count_ref[...] = value, number
        else:
            sums_ref[...] += value
            count_ref[...] += number

    add(out[0], out_id[0], True)
    before = 0
    for dy, dz in order[:-1]:
        k = dy * 4 + dz
        for made in arrive[k]:
            made.wait_recv()
        passed[k] = [
            copy(got_id.at[k], via_id.at[k], beside),
            copy(got.at[k, :, used_rows], via.at[k, :, used_rows], beside),
        ]
        add(got[k], got_id[k])
        for made in passed[before]:
            made.wait_recv()
        add(via[before], via_id[before])
        before = k
    for made in passed[before]:
        made.wait_recv()
    add(via[before], via_id[before])
    mine = features // 2
    here = pl.ds(pl.multiple_of(core * mine, mine), mine)
    there = pl.ds(pl.multiple_of((1 - core) * mine, mine), mine)
    sum_hi[...], sum_lo[...] = split(sums_ref[...])
    halves = [
        copy(sum_hi.at[:, there], pair_hi, beside), copy(sum_lo.at[:, there], pair_lo, beside)
    ]
    cents = cents_ref[...]
    first = ((0,), (0,))
    cov_ref[...] = dot(sum_hi[:, here], cents, first) + dot(sum_lo[:, here], cents, first)
    for made in [shown] + halves:
        made.wait_recv()
    cents = pair_cents[...]
    cov_ref[...] += dot(pair_hi[...], cents, first) + dot(pair_lo[...], cents, first)
    cov_ref[0:8, 0:128] = cov_ref[0:8, 0:128] + bad
    for made in started:
        made.wait_send()


def vmem(n):
    return [pl.BlockSpec(memory_space=pltpu.VMEM)] * n


def exchange(labels, points, cents):
    data_ways = lax.axis_size("dp")
    rows, features = cents.shape
    steps = points.shape[0] // CHUNK
    copies = 4 * (data_ways // 2 - 1) + data_ways + 3
    return pl.pallas_call(
        functools.partial(exchange_kernel, rows),
        in_specs=vmem(1) + [pl.BlockSpec(memory_space=pl.ANY)] + vmem(1),
        out_specs=vmem(3),
        out_shape=[
            jax.ShapeDtypeStruct((rows, features), F32),
            jax.ShapeDtypeStruct((8, rows), F32),
            jax.ShapeDtypeStruct((features // 2, features), F32),
        ],
        scratch_shapes=[
            pltpu.VMEM((steps, CHUNK, features), BF16),
            pltpu.VMEM((CHUNK, CHUNK), BF16),
            pltpu.VMEM((steps * data_ways // 2, CHUNK), F32),
            pltpu.VMEM((steps, 1, CHUNK), jnp.int32),
            pltpu.VMEM((steps, 16, CHUNK), BF16),
            pltpu.VMEM((steps * KEEP, features), BF16),
            pltpu.VMEM((16, steps * KEEP), BF16),
            pltpu.VMEM((data_ways // 2, 2, SLOT, features), BF16),
            pltpu.VMEM((data_ways // 2, 2, SLOT, features), BF16),
            pltpu.VMEM((data_ways // 2, 2, SLOT, features), BF16),
            pltpu.VMEM((data_ways // 2, 2, 16, SLOT), BF16),
            pltpu.VMEM((data_ways // 2, 2, 16, SLOT), BF16),
            pltpu.VMEM((data_ways // 2, 2, 16, SLOT), BF16),
            pltpu.VMEM((rows, features), BF16),
            pltpu.VMEM((rows, features), BF16),
            pltpu.VMEM((rows, features // 2), BF16),
            pltpu.VMEM((rows, features // 2), BF16),
            pltpu.VMEM((rows, features), BF16),
            pltpu.SemaphoreType.DMA((steps,)),
            pltpu.SemaphoreType.DMA((copies,)),
            pltpu.SemaphoreType.DMA((copies,)),
        ],
        compiler_params=pltpu.CompilerParams(
            collective_id=0, has_side_effects=True, vmem_limit_bytes=46 << 20
        ),
        name="exchange",
    )(labels.reshape(steps, 1, CHUNK), points, cents)


def settle_kernel(
    part_ref, sums_ref, count_ref, cents_ref, rot_ref, new_ref, bad_ref, got1, got2, got3, acc, own, hx, lx, top, low, square,
    sum_hi, sum_lo, counts, fresh, send, recv, tile_send, tile_recv,
):
    xyz, core = place()
    panel = lax.axis_index("cent")
    features = part_ref.shape[1]
    mine = features // 2
    tile = 256
    tiles = features // tile
    barrier = pltpu.get_barrier_semaphore()
    other = device(xyz, 1 - core)
    partners = [other] + [
        device(moved(xyz, axis, by), core) for axis in range(3) for by in range(1, WAYS)
    ]
    for partner in partners:
        pl.semaphore_signal(barrier, inc=1, device_id=partner, device_id_type=MESH)
    pl.semaphore_wait(barrier, len(partners))

    used = [0]
    started = []

    def remote(src, dst, s, r, to):
        made = pltpu.make_async_remote_copy(
            src_ref=src, dst_ref=dst, send_sem=s, recv_sem=r, device_id=to, device_id_type=MESH
        )
        started.append(made)
        return made

    def copy(src, dst, to):
        n = used[0]
        used[0] += 1
        made = remote(src, dst, send.at[n], recv.at[n], to)
        made.start()
        return made

    here = pl.multiple_of(core * mine, mine)
    parts = range(len(LANES))
    lanes = [pl.ds(lane, width) for lane, width in LANES]
    sizes = [mine // WAYS ** (stage + 1) for stage in range(2)]
    gots = (got1, got2)
    base = [0, 0, 0]

    def scatter(stage, part):
        size, axis = sizes[stage], (part + stage) % 3
        made = []
        for by in range(1, WAYS):
            to = moved(xyz, axis, by)
            start = pl.multiple_of(base[part] + to[axis] * size, size)
            made.append(
                copy(
                    (acc if stage else part_ref).at[pl.ds(start, size), lanes[part]],
                    gots[stage].at[by - 1, :, lanes[part]],
                    device(to, core),
                )
            )
        return made

    def spread(stage, part):
        size, axis = sizes[stage], (part + stage) % 3
        span = own.at[pl.ds(pl.multiple_of(base[part], size), size), lanes[part]]
        made = [copy(span, span, device(moved(xyz, axis, by), core)) for by in range(1, WAYS)]
        base[part] = base[part] - xyz[axis] * size
        return made

    def share(part):
        span = acc.at[pl.ds(base[part], sizes[1]), lanes[part]]
        return [
            copy(span, got3.at[by - 1, :, lanes[part]], device(moved(xyz, (part + 2) % 3, by), core))
            for by in range(1, WAYS)
        ]

    def arrived(part):
        for made in waits[part]:
            made.wait_recv()

    waits = [scatter(0, part) for part in parts]

    sum_hi[...], sum_lo[...] = split(sums_ref[...])
    unit = jnp.where(iota((8, 128), 0) == 0, 1.0, 0.0)
    counts[...] = lax.dot_general(
        count_ref[...], unit, (((0,), (0,)), ((), ())),
        precision=lax.Precision.HIGHEST, preferred_element_type=F32,
    )

    for stage in range(2):
        size = sizes[stage]
        for part in parts:
            arrived(part)
            base[part] = pl.multiple_of(base[part] + xyz[(part + stage) % 3] * size, size)
            at = (pl.ds(base[part], size), lanes[part])
            total = (acc if stage else part_ref)[at]
            for by in range(1, WAYS):
                total = total + gots[stage][by - 1, :, lanes[part]]
            acc[at] = total
            waits[part] = share(part) if stage else scatter(1, part)
    for part in parts:
        arrived(part)
        at = (pl.ds(base[part], sizes[1]), lanes[part])
        own[at] = (acc[at] + got3[1, :, lanes[part]]) + (
            got3[0, :, lanes[part]] + got3[2, :, lanes[part]]
        )
        waits[part] = spread(1, part)
    for part in parts:
        arrived(part)
        waits[part] = spread(0, part)
    squares = jnp.zeros((1, 1), F32)
    for part in parts:
        arrived(part)
        at = (slice(0, mine), lanes[part])
        value = own[at]
        hx[0, 0:mine, lanes[part]], lx[0, 0:mine, lanes[part]] = split(value)
        waits[part] = [
            copy(ref.at[0, pl.ds(0, mine), lanes[part]], ref.at[0, pl.ds(mine, mine), lanes[part]], other)
            for ref in (hx, lx)
        ]
        squares = squares + jnp.sum(
            jnp.sum(value * value, axis=0, keepdims=True), axis=1, keepdims=True
        )
    square[0] = jnp.broadcast_to(squares, square.shape[1:])
    waits.append([copy(square.at[0], square.at[1], other)])

    def sent(step, b, c, ref):
        cols = pl.ds(pl.multiple_of(c * tile, tile), tile)
        if step == NS_STEPS - 1:
            src, dst = own.at[:, cols], rot_ref.at[pl.ds(here, mine), cols]
        else:
            src = ref.at[(step + 1) % 2, pl.ds(0, mine), cols]
            dst = ref.at[(step + 1) % 2, pl.ds(mine, mine), cols]
        return pltpu.make_async_remote_copy(
            src_ref=src, dst_ref=dst, send_sem=tile_send.at[step, b, c],
            recv_sem=tile_recv.at[step, b, c], device_id=other, device_id_type=MESH,
        )

    both = ((1,), (1,))
    keep, turned = 1.5, 0.5
    for step in range(NS_STEPS):
        now, later = step % 2, (step + 1) % 2

        def inner(j):
            rows = pl.ds(pl.multiple_of(j * tile, tile), tile)
            hi, lo = hx[now, 0:mine, :], lx[now, 0:mine, :]
            there_hi = hx[now, rows, :]
            value = dot(hi, there_hi, both) + (
                dot(hi, lx[now, rows, :], both) + dot(lo, there_hi, both)
            )
            top[:, rows], low[:, rows] = split(value)

        pl.loop(0, tiles // 2)(inner)
        if step == 0:
            for row in waits:
                for made in row:
                    made.wait_recv()
            for made in started:
                made.wait_send()
            total = square[0, 0:1, 0:1] + square[1, 0:1, 0:1]
            inverse = 1.0 / (3.0 * jnp.sqrt(total / features + epsilon))
            keep, turned = 1.5 * inverse, 0.5 * inverse * inverse * inverse
        else:
            keep, turned = 1.5, 0.5
            for c in range(tiles):
                for b, ref in enumerate((hx, lx)):
                    sent(step - 1, b, c, ref).wait()
        pl.loop(tiles // 2, tiles)(inner)

        def update(c):
            cols = pl.ds(pl.multiple_of(c * tile, tile), tile)
            hi = hx[now, :, cols]
            turn = dot(top[...], hi) + (dot(top[...], lx[now, :, cols]) + dot(low[...], hi))
            value = keep * own[:, cols] - turned * turn
            own[:, cols] = value
            if step == NS_STEPS - 1:
                rot_ref[pl.ds(here, mine), cols] = value
                sent(step, 0, c, None).start()
            else:
                hx[later, 0:mine, cols], lx[later, 0:mine, cols] = split(value)
                for b, ref in enumerate((hx, lx)):
                    sent(step, b, c, ref).start()

        if step < NS_STEPS - 1:
            pl.loop(0, tiles)(update)

    begun = len(started)
    rings = []
    span = features // RINGS
    per = tiles // RINGS
    for c in range(tiles + 1):
        if c < tiles:
            update(c)
        if c and c % per == 0:
            for done in range(c - per, c):
                sent(NS_STEPS - 1, 0, done, None).wait()
            cols = slice((c - per) * tile, c * tile)
            rot_hi, rot_lo = split(rot_ref[:, cols])
            moved_rows = dot(sum_hi[...], rot_hi) + (
                dot(sum_hi[...], rot_lo) + dot(sum_lo[...], rot_hi)
            )
            value = (
                (moved_rows + cents_ref[:, cols].astype(F32)) / (counts[:, 0:1] + 1.0)
            ).astype(BF16)
            fresh[:, cols] = value
            ring = Ring(copy, xyz, core, fresh, new_ref, pl.ds((c - per) * tile, span))
            ring.begin()
            rings.append(ring)
    bad_ref[...] = jnp.where(jnp.abs(rot_ref[0:1, 0:1]) < jnp.inf, 0, 1)
    rows = fresh.shape[0]
    new_ref[pl.ds(pl.multiple_of(lax.axis_index("cent") * rows, rows), rows), :] = fresh[...]
    for ring in rings:
        ring.forward()
    for ring in rings:
        ring.onward()
    for ring in rings:
        ring.last()
    for ring in rings:
        ring.finish()
    for made in started[begun:]:
        made.wait_send()


def settle(part, sums, count, cents):
    features = part.shape[1]
    panel_ways = 2 * WAYS
    mine = features // 2
    sizes = [mine // WAYS**n for n in (1, 2, 2)]
    copies = 5 * 3 * (WAYS - 1) + 2 * 3 + 1 + RING * RINGS
    return pl.pallas_call(
        settle_kernel,
        in_specs=vmem(4),
        out_specs=vmem(3),
        out_shape=[
            jax.ShapeDtypeStruct((features, features), F32),
            jax.ShapeDtypeStruct((panel_ways * sums.shape[0], features), BF16),
            jax.ShapeDtypeStruct((1, 1), jnp.int32),
        ],
        scratch_shapes=[pltpu.VMEM((WAYS - 1, size, features), F32) for size in sizes]
        + [pltpu.VMEM((mine, features), F32)] * 2
        + [pltpu.VMEM((2, features, features), BF16)] * 2
        + [pltpu.VMEM((mine, features), BF16)] * 2
        + [pltpu.VMEM((2, 8, 128), F32)]
        + [pltpu.VMEM(cents.shape, BF16)] * 2
        + [pltpu.VMEM((cents.shape[0], 128), F32), pltpu.VMEM(cents.shape, BF16)]
        + [pltpu.SemaphoreType.DMA((copies,))] * 2
        + [pltpu.SemaphoreType.DMA((NS_STEPS, 2, features // 256))] * 2,
        compiler_params=pltpu.CompilerParams(
            collective_id=1, has_side_effects=True, vmem_limit_bytes=28 << 20
        ),
        name="settle",
    )(part, sums, count, cents)


def emit_kernel(new_ref, rot_ref, new_out, rot_out, done):
    copies = [
        pltpu.make_async_copy(src, dst, done.at[n])
        for n, (src, dst) in enumerate(((new_ref, new_out), (rot_ref, rot_out)))
    ]
    for made in copies:
        made.start()
    for made in copies:
        made.wait()


def emit(new, rot):
    return pl.pallas_call(
        emit_kernel,
        in_specs=vmem(2),
        out_specs=[pl.BlockSpec(memory_space=pltpu.HBM)] * 2,
        out_shape=[
            jax.ShapeDtypeStruct(new.shape, new.dtype),
            jax.ShapeDtypeStruct(rot.shape, rot.dtype),
        ],
        scratch_shapes=[pltpu.SemaphoreType.DMA((2,))],
        compiler_params=pltpu.CompilerParams(vmem_limit_bytes=16 << 20),
        name="emit",
    )(new, rot)


def summed(x, axes, ways):
    parts = lax.all_to_all(x, axes, 0, 0, tiled=True)
    return jnp.sum(parts.reshape(ways, x.shape[0] // ways, *x.shape[1:]), axis=0)


def joined(x, axes, ways):
    copies = jnp.broadcast_to(x[None], (ways, *x.shape)).reshape(ways * x.shape[0], *x.shape[1:])
    return lax.all_to_all(copies, axes, 0, 0, tiled=True)


def dense(points, labels, centroids):
    data_ways = lax.axis_size("dp")
    panel_ways = lax.axis_size("cent")
    block_rows = centroids.shape[0]
    features = points.shape[1]
    column = lax.axis_index("cent")
    owner_block = labels // block_rows
    inside = owner_block % panel_ways == column
    slot_index = jnp.where(
        inside, owner_block // panel_ways * block_rows + labels % block_rows, data_ways * block_rows
    )
    vectors = points.astype(F32)
    local_sums = jax.ops.segment_sum(vectors, slot_index, num_segments=data_ways * block_rows)
    local_counts = jax.ops.segment_sum(
        jnp.ones((*labels.shape, 128), F32), slot_index, num_segments=data_ways * block_rows
    )[:, 0]
    label_sums = summed(local_sums, "dp", data_ways)
    label_counts = summed(local_counts, "dp", data_ways)
    old_rows = centroids.astype(F32)
    part = lax.dot_general(
        label_sums, old_rows, (((0,), (0,)), ((), ())), precision=lax.Precision.HIGHEST
    )
    every = ("dp", "cent")
    cross_cov = joined(
        summed(part, every, data_ways * panel_ways), every, data_ways * panel_ways
    )
    scale_root = jnp.sqrt(jnp.sum(cross_cov * cross_cov) / features + epsilon)
    rotation = cross_cov / (3.0 * scale_root)
    for iteration in range(NS_STEPS):
        inner_prod = jnp.dot(rotation, rotation.T, precision=lax.Precision.HIGHEST)
        rotation = 1.5 * rotation - 0.5 * jnp.dot(
            inner_prod, rotation, precision=lax.Precision.HIGHEST
        )
    rotated_sums = jnp.dot(label_sums, rotation, precision=lax.Precision.HIGHEST)
    moved_rows = joined(rotated_sums + old_rows, "cent", panel_ways)
    all_counts = joined(label_counts, "cent", panel_ways)
    return ((moved_rows / (all_counts[:, None] + 1.0)).astype(BF16), rotation)


def local(points, labels, centroids):
    sums, count, part = exchange(labels, points, centroids)
    rotation, new_centroids, bad = settle(part, sums, count, centroids)
    new_centroids, rotation = emit(new_centroids, rotation)
    _, new_centroids, rotation = lax.while_loop(
        lambda state: state[0] > 0,
        lambda state: (jnp.int32(0), *dense(points, labels, centroids)),
        (bad.reshape(()), new_centroids, rotation),
    )
    return new_centroids, rotation


def solution(mesh):
    return jax.shard_map(
        local,
        mesh=mesh,
        in_specs=(P("dp", None), P("dp"), P(("dp", "cent"), None)),
        out_specs=(P("dp", None), P()),
        check_vma=False,
    )
```
